32 devices in a mesh: section: 2 (over core), seq: 4 (over z), rows: 4 (over y, x).
Axes of the slice: x: 2, y: 2, z: 4, core: 2. Of those that a mesh axis runs over, the one named last changes fastest.
Arguments:
- inputs: bfloat16 [2, 4, 4096, 512], P(None, 'rows', 'seq'), may hold values from -25 to 25
- cotangent: bfloat16 [2, 4, 4096, 512], P(None, 'rows', 'seq'), may hold values from -6 to 6
- starts: int32 [2, 4, 4096], P(None, 'rows', 'seq'), may hold values from 0 to 1, as said below
- valid: int32 [2, 4, 4096], P(None, 'rows', 'seq'), may hold values from 0 to 1, as said below
- norm_gain: float32 [2, 512], P('section'), may hold values from 0.1 to 1.9
- norm_bias: float32 [2, 512], P('section'), may hold values from -3 to 3
- running_mean: float32 [2, 512], P('section'), may hold values from -3 to 3
- running_var: float32 [2, 512], P('section'), may hold values from 0.5 to 2
- b_proj: bfloat16 [2, 512, 512], P('section'), may hold values from -0.25 to 0.25
- nu_log: float32 [2, 256], P('section'), may hold values from -12 to -3
- theta_log: float32 [2, 256], P('section'), may hold values from -4 to -1
- gamma_log: float32 [2, 256], P('section'), may hold values from -6 to -1
- c_proj: bfloat16 [2, 512, 512], P('section'), may hold values from -0.25 to 0.25
- d_skip: float32 [2, 512], P('section'), may hold values from -4 to 4
- glu_weight: bfloat16 [2, 512, 1024], P('section'), may hold values from -0.25 to 0.25
- glu_bias: float32 [2, 1024], P('section'), may hold values from -3 to 3
Outputs:
- activations: bfloat16 [2, 2, 4, 4096, 512], P('section', None, 'rows', 'seq')
- input_grad: bfloat16 [2, 2, 4, 4096, 512], P('section', None, 'rows', 'seq')
- grad_norm_gain: float32 [2, 512], P('section')
- grad_norm_bias: float32 [2, 512], P('section')
- grad_b_proj: float32 [2, 512, 512], P('section')
- grad_nu_log: float32 [2, 256], P('section')
- grad_theta_log: float32 [2, 256], P('section')
- grad_gamma_log: float32 [2, 256], P('section')
- grad_c_proj: float32 [2, 512, 512], P('section')
- grad_d_skip: float32 [2, 512], P('section')
- grad_glu_weight: float32 [2, 512, 1024], P('section')
- grad_glu_bias: float32 [2, 1024], P('section')
- new_running_mean: float32 [2, 512], P('section')
- new_running_var: float32 [2, 512], P('section')
The draws below stay inside these ranges and needn't reach their ends.
Inputs may be any that keep to these rules, and one draw needn't show every extreme that they name: `starts`: position 0 of every row holds 1. In each micro-batch one row, drawn from the seed, has no other 1 and no padding; every other row has at most 3 further 1s. `valid`: in each row the 1s form a prefix of more than 3072 positions.
All inputs are finite; a program needn't handle non-finite values.
Results may differ from the reference program's by a relative error of at most 0.018.
Values may be sent and summed in bfloat16 or wider, within the bound.
A program may use at most 192 MiB of HBM per device.

```python
import math
import jax
import jax.numpy as jnp
from jax import lax

D = 512
STATES = 256
MICRO = 2
ROWS = 4
LENGTH = 4096


def packing_plan(key):
    full_rows = jax.random.randint(jax.random.fold_in(key, 11), (MICRO,), 0, ROWS)
    paddings = jax.random.randint(jax.random.fold_in(key, 12), (MICRO, ROWS), 0, LENGTH // 4)
    whole_row = jnp.arange(ROWS)[None, :] == full_rows[:, None]
    paddings = jnp.where(whole_row, 0, paddings)
    return (whole_row, paddings)


def decay_rates(key, slow_share):
    picked = jax.random.uniform(jax.random.fold_in(key, 21), (2, STATES)) < slow_share
    slow_rate = jax.random.uniform(jax.random.fold_in(key, 22), (2, STATES), minval=0.3, maxval=2.0) / LENGTH
    fast_rate = jax.random.uniform(jax.random.fold_in(key, 23), (2, STATES), minval=1.0 / 50.0, maxval=1.0 / 30.0)
    return jnp.where(picked, slow_rate, fast_rate)


def draw_starts(key, part):
    whole_row, paddings = packing_plan(key)
    key = jax.random.fold_in(key, 1)
    cut_places = jax.random.randint(key, (MICRO, ROWS, 3), 1, LENGTH)
    places = jnp.arange(LENGTH)
    hits = jnp.any(places[None, None, None, :] == cut_places[..., None], axis=2)
    hits = hits & jnp.logical_not(whole_row)[..., None]
    hits = hits | (places == 0)[None, None, :]
    return hits.astype(jnp.int32)


def draw_valid(key, part):
    whole_row, paddings = packing_plan(key)
    places = jnp.arange(LENGTH)
    return (places[None, None, :] < (LENGTH - paddings)[..., None]).astype(jnp.int32)


def draw_inputs(key, part):
    key = jax.random.fold_in(key, 3)
    first_key, second_key = jax.random.split(key, 2)
    ramp = 0.6 + 1.2 * jnp.arange(LENGTH, dtype=jnp.float32) / max(LENGTH - 1, 1)
    channel = jnp.exp(jax.random.uniform(second_key, (D,), minval=-0.7, maxval=0.7))
    base = jnp.clip(jax.random.normal(first_key, (MICRO, ROWS, LENGTH, D)), -6.0, 6.0)
    values = base * ramp[:, None] * channel
    return values.astype(jnp.bfloat16)


def draw_nu_log(key, part):
    rates = decay_rates(key, 0.5)
    return jnp.log(rates)


def draw_gamma_log(key, part):
    rates = decay_rates(key, 0.5)
    key = jax.random.fold_in(key, 5)
    noise = jax.random.uniform(key, (2, STATES), minval=-0.25, maxval=0.25)
    return 0.5 * jnp.log(-jnp.expm1(-2.0 * rates)) + noise


def shard_levels(key, extent, cuts, smallest, largest):
    level = 1.0
    for axis_at, shards_of in cuts:
        heights = jax.random.uniform(jax.random.fold_in(jax.random.fold_in(key, 6), axis_at), (shards_of,), jnp.float32, smallest / len(cuts), largest / len(cuts))
        level = level * jnp.repeat(jnp.exp(heights), extent[axis_at] // shards_of).reshape((-1,) + (1,) * (len(extent) - 1 - axis_at))
    return level


def bell_draw(key, shape, spread, limit, cuts=(), held_as=jnp.bfloat16):
    array = spread * jax.random.normal(key, shape, jnp.float32)
    if cuts:
        array = array * shard_levels(key, shape, cuts, -0.22, 0.18)
    return jnp.clip(array, -limit, limit).astype(held_as)


def setup_inputs(seed: int = 0) -> dict:
    seeds = jax.random.split(jax.random.key(seed), 17)
    return {
        "inputs": draw_inputs(jax.random.fold_in(seeds[16], 71), 0),
        "cotangent": bell_draw(seeds[1], (MICRO, ROWS, LENGTH, D), 1.0, 6.0, ((1, 4), (2, 4))),
        "starts": draw_starts(jax.random.fold_in(seeds[16], 71), 0),
        "valid": draw_valid(jax.random.fold_in(seeds[16], 71), 0),
        "norm_gain": jnp.clip(1.0 + 0.18 * jax.random.normal(seeds[4], (2, D), jnp.float32), 0.1, 1.9),
        "norm_bias": bell_draw(seeds[5], (2, D), 0.5, 3.0, ((0, 2),), jnp.float32),
        "running_mean": bell_draw(seeds[6], (2, D), 0.5, 3.0, ((0, 2),), jnp.float32),
        "running_var": jnp.clip(0.5 + 1.5 * jax.random.uniform(seeds[7], (2, D), jnp.float32) ** shard_levels(seeds[7], (2, D), ((0, 2),), -0.2, 0.2), 0.5, 2.0),
        "b_proj": bell_draw(seeds[8], (2, D, 2 * STATES), D ** -0.5, 0.25, ((0, 2),)),
        "nu_log": draw_nu_log(jax.random.fold_in(seeds[16], 71), 0),
        "theta_log": jnp.clip(-4.0 + 3.0 * jax.random.uniform(seeds[10], (2, STATES), jnp.float32) ** shard_levels(seeds[10], (2, STATES), ((0, 2),), -0.2, 0.2), -4.0, -1.0),
        "gamma_log": draw_gamma_log(jax.random.fold_in(seeds[16], 71), 0),
        "c_proj": bell_draw(seeds[12], (2, 2 * STATES, D), (2 * STATES) ** -0.5, 0.25, ((0, 2),)),
        "d_skip": bell_draw(seeds[13], (2, D), 1.0, 4.0, ((0, 2),), jnp.float32),
        "glu_weight": bell_draw(seeds[14], (2, D, 2 * D), D ** -0.5, 0.25, ((0, 2),)),
        "glu_bias": bell_draw(seeds[15], (2, 2 * D), 0.5, 3.0, ((0, 2),), jnp.float32),
    }


NORM_EPS = 1e-05
MOMENTUM = 0.1
HIGHEST_PRECISION = lax.Precision.HIGHEST

@jax.custom_vjp
def low(v):
    return lax.optimization_barrier(v.astype(jnp.bfloat16)).astype(jnp.float32)

@jax.custom_vjp
def low_back(v):
    return v

def low_keep(v):
    return (low(v), None)

def low_pass(kept, grad):
    return (grad,)

def back_keep(v):
    return (v, None)

def back_low(kept, grad):
    return (low(grad),)
low.defvjp(low_keep, low_pass)
low_back.defvjp(back_keep, back_low)

def decay_terms(nu_row, theta_row, gamma_row):
    modulus = jnp.exp(-jnp.exp(nu_row))
    phase = jnp.exp(theta_row)
    return (modulus * jnp.cos(phase), modulus * jnp.sin(phase), jnp.exp(gamma_row))

def recurrence(keep_mask, drive_re, drive_im, lam_re, lam_im):
    row_count, length, state_count = drive_re.shape
    block_size = math.gcd(length, 64)
    block_count = length // block_size

    def advance(carry, element):
        prev_re, prev_im = carry
        keep_now, input_re, input_im = element
        decay_re = lam_re * keep_now[:, None]
        decay_im = lam_im * keep_now[:, None]
        next_re = decay_re * prev_re - decay_im * prev_im + input_re
        next_im = decay_re * prev_im + decay_im * prev_re + input_im
        return ((next_re, next_im), (next_re, next_im))

    @jax.checkpoint
    def run_block(carry, block_items):
        return lax.scan(advance, carry, block_items)
    block_items = (keep_mask.T.reshape(block_count, block_size, row_count), jnp.transpose(drive_re, (1, 0, 2)).reshape(block_count, block_size, row_count, state_count), jnp.transpose(drive_im, (1, 0, 2)).reshape(block_count, block_size, row_count, state_count))
    initial = (jnp.zeros((row_count, state_count), jnp.float32), jnp.zeros((row_count, state_count), jnp.float32))
    _, (state_re, state_im) = lax.scan(run_block, initial, block_items)
    state_re = jnp.transpose(state_re.reshape(length, row_count, state_count), (1, 0, 2))
    state_im = jnp.transpose(state_im.reshape(length, row_count, state_count), (1, 0, 2))
    return (state_re, state_im)

def block_layer(layer_raw, valid_rows, start_rows, weights, is_upper):
    gain_row, bias_row, b_mat, nu_row, theta_row, gamma_row, c_mat, skip_gain, w_glu, b_glu = weights
    layer_in = low_back(layer_raw)
    start_flags = start_rows.astype(jnp.float32)
    live_mask = valid_rows.astype(jnp.float32)
    if is_upper:
        layer_in = jnp.flip(layer_in, 1)
        start_flags = jnp.flip(start_flags, 1)
        live_mask = jnp.flip(live_mask, 1)
        keep_mask = jnp.concatenate([jnp.ones_like(start_flags[:, :1]), 1.0 - start_flags[:, :-1]], axis=1)
    else:
        keep_mask = 1.0 - start_flags
    token_total = jnp.sum(live_mask)
    norm_mean = lax.optimization_barrier(jnp.sum(layer_in * live_mask[..., None], axis=(0, 1))) / token_total
    centred = layer_in - norm_mean
    norm_var = lax.optimization_barrier(jnp.sum(centred * centred * live_mask[..., None], axis=(0, 1))) / token_total
    normed = centred * lax.rsqrt(norm_var + NORM_EPS)
    normed_in = normed * gain_row + bias_row
    b_out = low_back(jnp.einsum('rtd,ds->rts', low(normed_in), b_mat, precision=HIGHEST_PRECISION))
    lam_re, lam_im, gamma_gain = decay_terms(nu_row, theta_row, gamma_row)
    state_count = nu_row.shape[0]
    state_re, state_im = recurrence(keep_mask, gamma_gain * b_out[..., :state_count], gamma_gain * b_out[..., state_count:], lam_re, lam_im)
    state_low = low(jnp.concatenate([state_re, state_im], axis=-1))
    readout = low_back(jnp.einsum('rts,sd->rtd', state_low, c_mat, precision=HIGHEST_PRECISION))
    mixed_sum = readout + skip_gain * normed_in
    act_low = low(jax.nn.gelu(mixed_sum, approximate=True))
    glu_pre = low_back(jnp.einsum('rtd,de->rte', act_low, w_glu, precision=HIGHEST_PRECISION) + b_glu)
    model_width = layer_in.shape[-1]
    branch_out = glu_pre[..., :model_width] * jax.nn.sigmoid(glu_pre[..., model_width:])
    layer_out = low(layer_in + branch_out)
    if is_upper:
        layer_out = jnp.flip(layer_out, 1)
    return (layer_out, (norm_mean, norm_var))

def reference(inputs, cotangent, starts, valid, norm_gain, norm_bias, running_mean, running_var, b_proj, nu_log, theta_log, gamma_log, c_proj, d_skip, glu_weight, glu_bias):
    trained = tuple((parameter.astype(jnp.float32) for parameter in (norm_gain, norm_bias, b_proj, nu_log, theta_log, gamma_log, c_proj, d_skip, glu_weight, glu_bias)))
    inputs_float = inputs.astype(jnp.float32)
    input_probe = jnp.zeros_like(inputs_float)
    micro_count = inputs.shape[0]

    def forward(first_in, probe_in, *weight_list):
        lower_weights = tuple((parameter[0] for parameter in weight_list))
        upper_weights = tuple((parameter[1] for parameter in weight_list))
        lower_list = []
        upper_list = []
        stat_list = []
        for micro_index in range(micro_count):
            lower_out, lower_stats = block_layer(first_in[micro_index], valid[micro_index], starts[micro_index], lower_weights, False)
            upper_out, upper_stats = block_layer(lower_out + probe_in[micro_index], valid[micro_index], starts[micro_index], upper_weights, True)
            lower_list.append(lower_out)
            upper_list.append(upper_out)
            stat_list.append((lower_stats, upper_stats))
        return ((jnp.stack(lower_list), jnp.stack(upper_list)), tuple(stat_list))
    outputs_pair, backward_fn, stat_list = jax.vjp(forward, inputs_float, input_probe, *trained, has_aux=True)
    gradients = backward_fn((jnp.zeros_like(outputs_pair[0]), cotangent.astype(jnp.float32)))
    run_mean = running_mean
    run_var = running_var
    for micro_index in range(micro_count):
        lower_stats, upper_stats = stat_list[micro_index]
        run_mean = (1.0 - MOMENTUM) * run_mean + MOMENTUM * jnp.stack([lower_stats[0], upper_stats[0]])
        run_var = (1.0 - MOMENTUM) * run_var + MOMENTUM * jnp.stack([lower_stats[1], upper_stats[1]])
    activations = jnp.stack([outputs_pair[0], outputs_pair[1]]).astype(jnp.bfloat16)
    input_grad = jnp.stack([gradients[0], gradients[1]]).astype(jnp.bfloat16)
    return (activations, input_grad, gradients[2], gradients[3], gradients[4], gradients[5], gradients[6], gradients[7], gradients[8], gradients[9], gradients[10], gradients[11], run_mean, run_var)
```

```python
import functools
import math

import jax
import jax.numpy as jnp
from jax import lax
from jax.experimental import pallas as pl
from jax.experimental.pallas import tpu as pltpu
from jax.sharding import PartitionSpec as P

NORM_EPS = 1e-05
MOMENTUM = 0.1
GELU_C = math.sqrt(2.0 / math.pi)
GELU_K = 0.044715
MESH = pl.DeviceIdType.MESH
F32 = jnp.float32
BF16 = jnp.bfloat16
SUB = 8
LANES = 128


def dot_nn(a, b):
    return lax.dot_general(a, b, (((1,), (0,)), ((), ())), preferred_element_type=F32)


def dot_nt(a, b):
    return lax.dot_general(a, b, (((1,), (1,)), ((), ())), preferred_element_type=F32)


def dot_tn(a, b):
    return lax.dot_general(a, b, (((0,), (0,)), ((), ())), preferred_element_type=F32)


def wide(mask, times):
    return jnp.concatenate([mask] * times, axis=1)


def to_tile(row):
    return jnp.concatenate(
        [row[:, i * LANES : (i + 1) * LANES] for i in range(row.shape[1] // LANES)], axis=0
    )


def to_row(tile):
    return jnp.concatenate([tile[i : i + 1, :] for i in range(tile.shape[0])], axis=1)


def cmul(ar, ai, br, bi):
    return ar * br - ai * bi, ar * bi + ai * br


def cpow(re, im, count):
    out = None
    while count:
        if count % 2:
            out = (re, im) if out is None else cmul(out[0], out[1], re, im)
        count //= 2
        if count:
            re, im = cmul(re, im, re, im)
    return out


def fold_rows(value):
    return jnp.sum(value.reshape(value.shape[0] // SUB, SUB, value.shape[1]), axis=0)


def step_kernel(
    n_seq,
    n_rows,
    x_hbm,
    cot_hbm,
    starts_ref,
    valid_ref,
    gain_ref,
    bias_ref,
    rmean_ref,
    rvar_ref,
    b_hbm,
    nu_ref,
    theta_ref,
    gamma_ref,
    c_hbm,
    skip_ref,
    glu_hbm,
    glub_ref,
    act_out,
    ig_out,
    ggain_out,
    gbias_out,
    gb_out,
    gnu_out,
    gtheta_out,
    ggamma_out,
    gc_out,
    gskip_out,
    gglu_out,
    gglub_out,
    nmean_out,
    nvar_out,
    xnat,
    cnat,
    wb,
    wc,
    wg,
    pv,
    dv,
    perm,
    perm_t,
    keep_a,
    keep_d,
    live,
    hid,
    ulow,
    drive,
    state,
    slow,
    alow,
    dgate,
    dread,
    gst,
    dproj,
    dmix,
    dunit,
    dout,
    sig_s,
    gat_s,
    dgelu_s,
    low_s,
    nat,
    sv,
    sm,
    meta,
    gst_all,
    gline,
    gsmall,
    gbuf,
    xbuf,
    rbuf,
    r2buf,
    gfin,
    in_sem,
    wsend_sem,
    wrecv_sem,
    gs_sem,
    gr_sem,
    out_sem,
    osend_sem,
    orecv_sem,
    rs_sem,
    rr_sem,
):
    micro = x_hbm.shape[0]
    tokens = x_hbm.shape[2]
    half = tokens // 2
    seg = half // SUB
    width = x_hbm.shape[3]
    ns = nu_ref.shape[1]
    n_line = 2 * n_seq
    n_all = n_line * n_rows
    chunk = min(128, half)
    n_chunk = half // chunk

    s = lax.axis_index("section")
    q = lax.axis_index("seq")
    r = lax.axis_index("rows")
    rank = q * 2 + s
    me = rank * n_rows + r
    partner = (1 - s, q, r)

    def peer_all(d):
        g = lax.rem(me + d, n_all)
        k = g // n_rows
        return (k % 2, k // 2, g % n_rows)

    def peer_line(d):
        k = lax.rem(rank + d, n_line)
        return (k % 2, k // 2, r)

    def gather_start(buf, mine, count, peer, sem):
        def one(d, carry):
            pltpu.make_async_remote_copy(
                src_ref=buf.at[mine],
                dst_ref=buf.at[mine],
                send_sem=gs_sem.at[sem],
                recv_sem=gr_sem.at[sem],
                device_id=peer(d),
                device_id_type=MESH,
            ).start()
            return carry

        lax.fori_loop(1, count, one, 0)

    def gather_wait(buf, count, sem):
        part = buf.at[pl.ds(0, count - 1)]
        pltpu.make_async_copy(part, part, gr_sem.at[sem]).wait()

    def gather_sent(buf, count, sem):
        part = buf.at[pl.ds(0, count - 1)]
        pltpu.make_async_copy(part, part, gs_sem.at[sem]).wait()

    barrier = pltpu.get_barrier_semaphore()

    def greet(d, carry):
        pl.semaphore_signal(barrier, inc=1, device_id=peer_all(d), device_id_type=MESH)
        return carry

    lax.fori_loop(1, n_all, greet, 0)

    start_at = pl.multiple_of(s * half, half)
    my_tokens = pl.ds(start_at, half)
    loads = []
    for m in range(micro):
        loads.append(
            pltpu.make_async_copy(x_hbm.at[m, 0, my_tokens], xnat.at[m], in_sem.at[m])
        )
    own_w = [
        pltpu.make_async_copy(b_hbm.at[0], wb.at[s], in_sem.at[4]),
        pltpu.make_async_copy(c_hbm.at[0], wc.at[s], in_sem.at[5]),
        pltpu.make_async_copy(glu_hbm.at[0], wg.at[s], in_sem.at[6]),
    ]
    cot_loads = [
        pltpu.make_async_copy(cot_hbm.at[m, 0, my_tokens], cnat.at[m], in_sem.at[2 + m])
        for m in range(micro)
    ]
    for item in loads + own_w + cot_loads:
        item.start()

    pv[s, 0:1, :] = gain_ref[...]
    pv[s, 1:2, :] = bias_ref[...]
    pv[s, 2:3, :] = skip_ref[...]
    pv[s, 3:4, :] = glub_ref[:, :width]
    pv[s, 4:5, :] = glub_ref[:, width:]
    pv[s, 5:6, :] = jnp.concatenate([nu_ref[...], theta_ref[...]], axis=1)
    pv[s, 6:7, :] = jnp.concatenate([gamma_ref[...], gamma_ref[...]], axis=1)
    pv[s, 7:8, :] = jnp.zeros((1, width), F32)

    here = lax.broadcasted_iota(jnp.int32, (half, half), 0)
    there = lax.broadcasted_iota(jnp.int32, (half, half), 1)
    perm[...] = jnp.where((here % SUB) * seg + here // SUB == there, 1.0, 0.0).astype(BF16)
    perm_t[...] = jnp.where((there % SUB) * seg + there // SUB == here, 1.0, 0.0).astype(BF16)

    st_all = starts_ref[:, 0, :].astype(F32)
    va_all = valid_ref[:, 0, :].astype(F32)
    nx_all = pltpu.roll(st_all, tokens - 1, 1)
    on_upper = s == 1
    st_half = jnp.where(on_upper, st_all[:, half:], st_all[:, :half])
    va_half = jnp.where(on_upper, va_all[:, half:], va_all[:, :half])
    nx_half = jnp.where(on_upper, nx_all[:, half:], nx_all[:, :half])
    place = lax.broadcasted_iota(jnp.int32, (micro, half), 1)
    nx_half = jnp.where(place == half - 1, 0.0, nx_half)
    counts = []
    for m in range(micro):
        stacked = jnp.concatenate(
            [
                jnp.broadcast_to(1.0 - st_half[m : m + 1], (LANES, half)),
                jnp.broadcast_to(1.0 - nx_half[m : m + 1], (LANES, half)),
                jnp.broadcast_to(va_half[m : m + 1], (LANES, half)),
            ],
            axis=0,
        ).astype(BF16)
        spread = dot_nt(perm[...], stacked)
        keep_a[m] = spread[:, :LANES]
        keep_d[m] = spread[:, LANES : 2 * LANES]
        live[m] = spread[:, 2 * LANES :]
        counts.append(jnp.sum(va_half[m : m + 1], axis=1, keepdims=True))
    rows_low = lax.broadcasted_iota(jnp.int32, (SUB, LANES), 0) < 4
    meta[me] = jnp.where(
        rows_low,
        jnp.broadcast_to(counts[0], (SUB, LANES)),
        jnp.broadcast_to(counts[micro - 1], (SUB, LANES)),
    )

    pl.semaphore_wait(barrier, n_all - 1)

    def share(source, target, index):
        return pltpu.make_async_remote_copy(
            src_ref=source,
            dst_ref=target,
            send_sem=wsend_sem.at[index],
            recv_sem=wrecv_sem.at[index],
            device_id=partner,
            device_id_type=MESH,
        )

    shares = [
        share(pv.at[s], pv.at[s], 0),
        share(b_hbm.at[0], wb.at[s], 1),
        share(c_hbm.at[0], wc.at[s], 2),
        share(glu_hbm.at[0], wg.at[s], 3),
    ]
    SEM_META, SEM_STAT, SEM_NORM, SEM_LINE, SEM_SMALL = 0, 1, 5, 9, 17
    gather_start(meta, me, n_all, peer_all, SEM_META)
    for item in shares:
        item.start()

    def chunks(body, init):
        return lax.fori_loop(0, n_chunk, lambda c, acc: body(pl.multiple_of(c * chunk, chunk), acc), init)

    zero_sum = jnp.zeros((SUB, width), F32)

    def enter(m):
        def body(at, acc):
            rows = pl.ds(at, chunk)
            value = dot_nn(perm[rows, :], xnat[m])
            hid[m, rows, :] = value
            return acc + fold_rows(value * wide(live[m, rows, :], width // LANES))

        return chunks(body, zero_sum)

    def send_stats(l, m, total):
        mean = jnp.sum(total, axis=0, keepdims=True) / jnp.maximum(counts[m], 1.0)

        def body(at, acc):
            rows = pl.ds(at, chunk)
            off = hid[2 * l + m, rows, :] - mean
            return acc + fold_rows(off * off * wide(live[m, rows, :], width // LANES))

        spread = jnp.sum(chunks(body, zero_sum), axis=0, keepdims=True)
        buf = gst_all.at[2 * l + m]
        buf[me] = jnp.concatenate([to_tile(mean), to_tile(spread)], axis=0)
        gather_start(buf, me, n_all, peer_all, SEM_STAT + 2 * l + m)

    def take_stats(l, m):
        buf = gst_all.at[2 * l + m]
        gather_wait(buf, n_all, SEM_STAT + 2 * l + m)
        data = buf[...]
        count = meta[:, 4 * m : 4 * m + 1, :] if micro == 2 else meta[:, 0:1, :]
        total = jnp.sum(count, axis=0)
        low4 = lax.broadcasted_iota(jnp.int32, (1, SUB, LANES), 1) < 4
        weighted = jnp.sum(data * jnp.where(low4, count, 1.0), axis=0)
        mean = weighted[0:4] / total
        apart = data[:, 0:4, :] - mean[None]
        var = (weighted[4:8] + jnp.sum(count * apart * apart, axis=0)) / total
        mean_row, var_row = to_row(mean), to_row(var)
        scale = lax.rsqrt(var_row + NORM_EPS)
        box = sv.at[2 * l + m]
        box[0:1, :] = mean_row
        box[1:2, :] = scale
        box[2:3, :] = scale * pv[l, 0:1, :]
        box[3:4, :] = var_row
        box[4:5, :] = jnp.broadcast_to(total[:, 0:1], (1, width))

    def unit_of(l, m, rows):
        box = sv.at[2 * l + m]
        return (hid[2 * l + m, rows, :] - box[0:1, :]) * box[2:3, :] + pv[l, 1:2, :]

    def lam_rows(l, which, conj):
        re = dv[l, which : which + 1, :ns]
        im = dv[l, which : which + 1, ns:]
        return re, (-im if conj else im)

    unroll = min(8, seg)

    def scan_local(u_ref, keep_ref, l, desc, conj):
        lr, li = lam_rows(l, 0, conj)
        lr = jnp.broadcast_to(lr, (SUB, ns))
        li = jnp.broadcast_to(li, (SUB, ns))

        def body(jj, carry):
            re, im = carry
            for t in range(unroll):
                j = jj * unroll + t
                if desc:
                    j = seg - 1 - j
                rows = pl.ds(pl.multiple_of(j * SUB, SUB), SUB)
                keep = wide(keep_ref[rows, :], ns // LANES)
                u = u_ref[rows, :]
                kr, ki = keep * re, keep * im
                re = lr * kr - li * ki + u[:, :ns]
                im = lr * ki + li * kr + u[:, ns:]
            return re, im

        zero = jnp.zeros((SUB, ns), F32)
        return lax.fori_loop(0, seg // unroll, body, (zero, zero))

    spot = lambda: lax.broadcasted_iota(jnp.int32, (SUB, ns), 0)

    def before(value, step, desc, blank):
        if desc:
            return jnp.where(spot() < SUB - step, pltpu.roll(value, SUB - step, 0), blank)
        return jnp.where(spot() >= step, pltpu.roll(value, step, 0), blank)

    def join_segments(er, ei, keep_ref, l, desc, conj):
        shut = jnp.min(keep_ref[...].reshape(seg, SUB, LANES), axis=0)
        lr, li = lam_rows(l, 1, conj)
        ar, ai = lr * wide(shut, ns // LANES), li * wide(shut, ns // LANES)
        for step in (1, 2, 4):
            pr, pi = cmul(ar, ai, before(er, step, desc, 0.0), before(ei, step, desc, 0.0))
            er, ei = er + pr, ei + pi
            ar, ai = cmul(ar, ai, before(ar, step, desc, 1.0), before(ai, step, desc, 0.0))
        last = 0 if desc else SUB - 1
        out = (er[last : last + 1], ei[last : last + 1], jnp.min(shut, axis=0, keepdims=True))
        shifted = (
            before(er, 1, desc, 0.0),
            before(ei, 1, desc, 0.0),
            before(ar, 1, desc, 1.0),
            before(ai, 1, desc, 0.0),
        )
        return out, shifted

    def send_carry(phase, l, m, u_ref, desc, conj):
        keep_ref = keep_d.at[m] if desc else keep_a.at[m]
        er, ei = scan_local(u_ref, keep_ref, l, desc, conj)
        (tr, ti, shut), shifted = join_segments(er, ei, keep_ref, l, desc, conj)
        if desc:
            first = keep_a[m, 0:1, :]
            tr, ti, shut = tr * wide(first, ns // LANES), ti * wide(first, ns // LANES), shut * first
        index = phase * 4 + 2 * l + m
        buf = gline.at[index]
        buf[rank] = jnp.concatenate(
            [
                to_tile(tr),
                to_tile(ti),
                shut,
                jnp.zeros((SUB - 2 * ns // LANES - 1, LANES), F32),
            ],
            axis=0,
        )
        gather_start(buf, rank, n_line, peer_line, SEM_LINE + index)
        return shifted

    def take_carry(phase, l, m, shifted, desc, conj):
        index = phase * 4 + 2 * l + m
        buf = gline.at[index]
        gather_wait(buf, n_line, SEM_LINE + index)
        lr, li = lam_rows(l, 2, conj)
        tiles = ns // LANES

        def body(step, carry):
            cr, ci = carry
            k = n_line - 1 - step if desc else step
            box = buf[k]
            shut = wide(box[2 * tiles : 2 * tiles + 1], tiles)
            pr, pi = cmul(lr * shut, li * shut, cr, ci)
            pr = pr + to_row(box[:tiles])
            pi = pi + to_row(box[tiles : 2 * tiles])
            use = k > rank if desc else k < rank
            return jnp.where(use, pr, cr), jnp.where(use, pi, ci)

        zero = jnp.zeros((1, ns), F32)
        cr, ci = lax.fori_loop(0, n_line, body, (zero, zero))
        er, ei, ar, ai = shifted
        pr, pi = cmul(ar, ai, cr, ci)
        return er + pr, ei + pi

    def fill_states(l, m, shifted):
        desc = l == 1
        re, im = take_carry(0, l, m, shifted, desc, False)
        keep_ref = keep_d.at[m] if desc else keep_a.at[m]
        u_ref, s_ref = drive.at[2 * l + m], state.at[2 * l + m]
        lr, li = lam_rows(l, 0, False)
        lr = jnp.broadcast_to(lr, (SUB, ns))
        li = jnp.broadcast_to(li, (SUB, ns))
        s_ref[pl.ds(half if desc else 0, SUB), :] = jnp.concatenate([re, im], axis=1)

        def body(jj, carry):
            re, im = carry
            for t in range(unroll):
                j = jj * unroll + t
                if desc:
                    j = seg - 1 - j
                at = pl.multiple_of(j * SUB, SUB)
                rows = pl.ds(at, SUB)
                keep = wide(keep_ref[rows, :], ns // LANES)
                u = u_ref[rows, :]
                kr, ki = keep * re, keep * im
                re = lr * kr - li * ki + u[:, :ns]
                im = lr * ki + li * kr + u[:, ns:]
                to = rows if desc else pl.ds(at + SUB, SUB)
                s_ref[to, :] = jnp.concatenate([re, im], axis=1)
            return re, im

        lax.fori_loop(0, seg // unroll, body, (re, im))

    def fill_grads(l, m, shifted):
        desc = l == 0
        re, im = take_carry(1, l, m, shifted, desc, True)
        keep_ref = keep_d.at[m] if desc else keep_a.at[m]
        pkeep_ref = keep_a.at[m] if desc else keep_d.at[m]
        u_ref, s_ref, g_ref = drive.at[2 * l + m], state.at[2 * l + m], gst.at[m]
        lr, li = lam_rows(l, 0, True)
        lr = jnp.broadcast_to(lr, (SUB, ns))
        li = jnp.broadcast_to(li, (SUB, ns))
        zero = jnp.zeros((SUB, ns), F32)

        def body(jj, carry):
            re, im, dr, di, dg = carry
            for t in range(unroll):
                j = jj * unroll + t
                if desc:
                    j = seg - 1 - j
                at = pl.multiple_of(j * SUB, SUB)
                rows = pl.ds(at, SUB)
                keep = wide(keep_ref[rows, :], ns // LANES)
                g = g_ref[rows, :]
                kr, ki = keep * re, keep * im
                re = lr * kr - li * ki + g[:, :ns]
                im = lr * ki + li * kr + g[:, ns:]
                g_ref[rows, :] = jnp.concatenate([re, im], axis=1)
                u = u_ref[rows, :]
                dg = dg + (re * u[:, :ns] + im * u[:, ns:])
                old = s_ref[rows if desc else pl.ds(at + SUB, SUB), :]
                pkeep = wide(pkeep_ref[rows, :], ns // LANES)
                pr, pi = pkeep * old[:, :ns], pkeep * old[:, ns:]
                dr = dr + (pr * re + pi * im)
                di = di + (pr * im - pi * re)
            return re, im, dr, di, dg

        _, _, dr, di, dg = lax.fori_loop(0, seg // unroll, body, (re, im, zero, zero, zero))
        box = sm.at[2 * l + m]
        box[3:4, :] = jnp.sum(jnp.concatenate([dr, di], axis=1), axis=0, keepdims=True)
        box[4:5, :] = jnp.sum(jnp.concatenate([dg, dg], axis=1), axis=0, keepdims=True)

    def project(l, m):
        gamma2 = dv[l, 3:4, :]

        def body(at, acc):
            rows = pl.ds(at, chunk)
            low = unit_of(l, m, rows).astype(BF16)
            ulow[l, pl.ds(m * half + at, chunk), :] = low
            drive[2 * l + m, rows, :] = dot_nn(low, wb[l]) * gamma2
            return acc

        chunks(body, 0)
        return send_carry(0, l, m, drive.at[2 * l + m], l == 1, False)

    def mix(l, m, at):
        rows = pl.ds(at, chunk)
        big = pl.ds(m * half + at, chunk)
        low = state[2 * l + m, pl.ds(at + (0 if l == 1 else SUB), chunk), :].astype(BF16)
        slow[l, big, :] = low
        unit = unit_of(l, m, rows)
        mixed = dot_nn(low, wc[l]) + pv[l, 2:3, :] * unit
        square = mixed * mixed
        t = jnp.tanh((GELU_C * mixed) * (1.0 + GELU_K * square))
        half_up = 0.5 * (1.0 + t)
        act = (mixed * half_up).astype(BF16)
        alow[l, big, :] = act
        slope = half_up + (0.5 * GELU_C) * mixed * (1.0 - t * t) * (1.0 + (3.0 * GELU_K) * square)
        gates = dot_nn(act, wg[l])
        value = gates[:, :width] + pv[l, 3:4, :]
        gate = 0.5 * jnp.tanh(0.5 * (gates[:, width:] + pv[l, 4:5, :])) + 0.5
        branch = value * gate
        return unit, slope, gate, branch, (hid[2 * l + m, rows, :] + branch).astype(BF16)

    def finish_lower(m):
        def body(at, acc):
            rows = pl.ds(at, chunk)
            unit, slope, gate, branch, low = mix(0, m, at)
            sig_s[m, rows, :] = gate.astype(BF16)
            gat_s[m, rows, :] = (branch * (1.0 - gate)).astype(BF16)
            dgelu_s[m, rows, :] = slope.astype(BF16)
            low_s[m, rows, :] = low
            value = low.astype(F32)
            hid[2 + m, rows, :] = value
            return acc + fold_rows(value * wide(live[m, rows, :], width // LANES))

        return chunks(body, zero_sum)

    def to_natural(low_ref, nat_ref):
        def body(at, acc):
            rows = pl.ds(at, chunk)
            nat_ref[rows, :] = dot_nn(perm_t[rows, :], low_ref[...]).astype(BF16)
            return acc

        chunks(body, 0)

    def ship(out, m, tag):
        base = tag * 2 + m
        local = pltpu.make_async_copy(
            nat.at[s, m], out.at[0, m, 0, my_tokens], out_sem.at[base]
        )
        remote = pltpu.make_async_remote_copy(
            src_ref=nat.at[1 - s, m],
            dst_ref=out.at[0, m, 0, my_tokens],
            send_sem=osend_sem.at[base],
            recv_sem=orecv_sem.at[base],
            device_id=partner,
            device_id_type=MESH,
        )
        local.start()
        remote.start()
        return local, remote

    def gate_grads(l, m, at, unit, slope, gate, other, grad, acc):
        rows = pl.ds(at, chunk)
        big = pl.ds(m * half + at, chunk)
        d_gates = jnp.concatenate([grad * gate, grad * other], axis=1).astype(BF16)
        dgate[big, :] = d_gates
        d_mixed = dot_nt(d_gates, wg[l]) * slope
        dmix[m, rows, :] = d_mixed
        d_read = d_mixed.astype(BF16)
        dread[big, :] = d_read
        gst[m, rows, :] = dot_nt(d_read, wc[l])
        return acc[0] + fold_rows(d_gates.astype(F32)), acc[1] + fold_rows(d_mixed * unit)

    gate_zero = (jnp.zeros((SUB, 2 * width), F32), zero_sum)

    def keep_gate_sums(l, m, acc):
        box = sm.at[2 * l + m]
        box[0:1, :] = jnp.sum(acc[1], axis=0, keepdims=True)
        both = jnp.sum(acc[0], axis=0, keepdims=True)
        box[1:2, :] = both[:, :width]
        box[2:3, :] = both[:, width:]

    def turn_upper(m):
        def body(at, acc):
            rows = pl.ds(at, chunk)
            unit, slope, gate, branch, low = mix(1, m, at)
            low_s[m, rows, :] = low
            grad = dot_nn(perm[rows, :], cnat[m])
            dout[m, rows, :] = grad
            return gate_grads(1, m, at, unit, slope, gate, branch * (1.0 - gate), grad, acc)

        keep_gate_sums(1, m, chunks(body, gate_zero))
        return send_carry(1, 1, m, gst.at[m], False, True)

    def unproject(l, m):
        gamma2 = dv[l, 3:4, :]

        def body(at, acc):
            rows = pl.ds(at, chunk)
            low = (gst[m, rows, :] * gamma2).astype(BF16)
            dproj[pl.ds(m * half + at, chunk), :] = low
            value = dmix[m, rows, :] * pv[l, 2:3, :] + dot_nt(low, wb[l])
            dunit[m, rows, :] = value
            normed = (hid[2 * l + m, rows, :] - sv[2 * l + m, 0:1, :]) * sv[2 * l + m, 1:2, :]
            return acc[0] + fold_rows(value), acc[1] + fold_rows(value * normed)

        by_bias, by_gain = chunks(body, (zero_sum, zero_sum))
        buf = gst_all.at[4 + 2 * l + m]
        buf[me] = jnp.concatenate(
            [
                to_tile(jnp.sum(by_bias, axis=0, keepdims=True)),
                to_tile(jnp.sum(by_gain, axis=0, keepdims=True)),
            ],
            axis=0,
        )
        gather_start(buf, me, n_all, peer_all, SEM_NORM + 2 * l + m)

    def take_norm(l, m):
        buf = gst_all.at[4 + 2 * l + m]
        gather_wait(buf, n_all, SEM_NORM + 2 * l + m)
        both = jnp.sum(buf[...], axis=0)
        box = sv.at[2 * l + m]
        box[5:6, :] = to_row(both[0:4])
        box[6:7, :] = to_row(both[4:8])

    def input_grads(l, m, rows):
        box = sv.at[2 * l + m]
        share_of = 1.0 / box[4:5, :]
        by_bias = box[2:3, :] * box[5:6, :] * share_of
        by_gain = box[2:3, :] * box[6:7, :] * share_of
        normed = (hid[2 * l + m, rows, :] - box[0:1, :]) * box[1:2, :]
        mask = wide(live[m, rows, :], width // LANES)
        return (
            dout[m, rows, :]
            + dunit[m, rows, :] * box[2:3, :]
            - mask * (by_bias + normed * by_gain)
        ).astype(BF16)

    def turn_lower(m):
        def body(at, acc):
            rows = pl.ds(at, chunk)
            low = input_grads(1, m, rows)
            low_s[m, rows, :] = low
            grad = low.astype(F32)
            dout[m, rows, :] = grad
            return gate_grads(
                0,
                m,
                at,
                unit_of(0, m, rows),
                dgelu_s[m, rows, :].astype(F32),
                sig_s[m, rows, :].astype(F32),
                gat_s[m, rows, :].astype(F32),
                grad,
                acc,
            )

        keep_gate_sums(0, m, chunks(body, gate_zero))
        return send_carry(1, 0, m, gst.at[m], True, True)

    def finish_grads(m):
        def body(at, acc):
            rows = pl.ds(at, chunk)
            low_s[m, rows, :] = input_grads(0, m, rows)
            return acc

        chunks(body, 0)

    part = 128

    def weight_grads(l, left, right, column, row_at):
        def body(c, acc):
            at = pl.multiple_of(c * part, part)
            value = dot_tn(left[l, :, pl.ds(at, part)], right[:, column : column + width])
            gbuf[l, pl.ds(pl.multiple_of(row_at + at, part), part), :] = value.astype(BF16)
            return acc

        lax.fori_loop(0, width // part, body, 0)

    def send_small(l):
        buf = gsmall.at[l]
        both = sm[2 * l]
        for m in range(1, micro):
            both = both + sm[2 * l + m]
        buf[me] = jnp.concatenate(
            [to_tile(both[i : i + 1]) for i in range(5)] + [jnp.zeros((4, LANES), F32)], axis=0
        )
        gather_start(buf, me, n_all, peer_all, SEM_SMALL + l)

    for item in loads:
        item.wait()
    for m in range(micro):
        send_stats(0, m, enter(m))
    for item in own_w:
        item.wait()
    for item in shares:
        item.wait()
    for l in range(2):
        decay = jnp.exp(-jnp.exp(pv[l, 5:6, :ns]))
        phase = jnp.exp(pv[l, 5:6, ns:])
        re, im = decay * jnp.cos(phase), decay * jnp.sin(phase)
        dv[l, 0:1, :] = jnp.concatenate([re, im], axis=1)
        dv[l, 1:2, :] = jnp.concatenate(cpow(re, im, seg), axis=1)
        dv[l, 2:3, :] = jnp.concatenate(cpow(re, im, half), axis=1)
        dv[l, 3:4, :] = jnp.exp(pv[l, 6:7, :])
    gather_wait(meta, n_all, SEM_META)

    shifted = {}
    for m in range(micro):
        take_stats(0, m)
        shifted[m] = project(0, m)
    for m in range(micro):
        fill_states(0, m, shifted[m])
        send_stats(1, m, finish_lower(m))
        to_natural(low_s.at[m], nat.at[0, m])
    for m in range(micro):
        take_stats(1, m)
        shifted[m] = project(1, m)
    for item in cot_loads:
        item.wait()
    outgoing = []
    for m in range(micro):
        fill_states(1, m, shifted[m])
        shifted[m] = turn_upper(m)
        to_natural(low_s.at[m], nat.at[1, m])
        outgoing += ship(act_out, m, 0)
    weight_grads(1, slow, dread, 0, width)
    weight_grads(1, alow, dgate, 0, 2 * width)
    weight_grads(1, alow, dgate, width, 3 * width)
    for m in range(micro):
        fill_grads(1, m, shifted[m])
        unproject(1, m)
    weight_grads(1, ulow, dproj, 0, 0)
    send_small(1)
    for item in outgoing:
        item.wait()
    outgoing = []
    for m in range(micro):
        take_norm(1, m)
        shifted[m] = turn_lower(m)
        to_natural(low_s.at[m], nat.at[1, m])
    weight_grads(0, slow, dread, 0, width)
    weight_grads(0, alow, dgate, 0, 2 * width)
    weight_grads(0, alow, dgate, width, 3 * width)
    for m in range(micro):
        fill_grads(0, m, shifted[m])
        unproject(0, m)
    weight_grads(0, ulow, dproj, 0, 0)
    send_small(0)
    for m in range(micro):
        take_norm(0, m)
        finish_grads(m)
        to_natural(low_s.at[m], nat.at[0, m])
        outgoing += ship(ig_out, m, 1)

    rows_all = gbuf.shape[1]
    n1 = rows_all // n_rows
    n2 = n1 // n_seq
    pair = pltpu.make_async_remote_copy(
        src_ref=gbuf.at[1 - s],
        dst_ref=xbuf,
        send_sem=rs_sem.at[0],
        recv_sem=rr_sem.at[0],
        device_id=partner,
        device_id_type=MESH,
    )
    pair.start()
    pair.wait()
    mine = gbuf.at[s]

    def add_pair(c, acc):
        rows = pl.ds(pl.multiple_of(c * part, part), part)
        total = mine[rows, :].astype(F32) + xbuf[rows, :].astype(F32)
        xbuf[rows, :] = total.astype(BF16)
        return acc

    lax.fori_loop(0, rows_all // part, add_pair, 0)

    def row_peer(d):
        return lax.rem(r + d, n_rows)

    def seq_peer(d):
        return lax.rem(q + d, n_seq)

    def spread_out(count, sem, make):
        def one(d, acc):
            source, target, where = make(d)
            pltpu.make_async_remote_copy(
                src_ref=source,
                dst_ref=target,
                send_sem=rs_sem.at[sem],
                recv_sem=rr_sem.at[sem],
                device_id=where,
                device_id_type=MESH,
            ).start()
            return acc

        lax.fori_loop(1, count, one, 0)

    def await_all(ref, sem):
        pltpu.make_async_copy(ref, ref, rr_sem.at[sem]).wait()

    def piece(ref, index, size):
        return ref.at[pl.ds(pl.multiple_of(index * size, size), size)]

    spread_out(
        n_rows,
        1,
        lambda d: (piece(xbuf, row_peer(d), n1), rbuf.at[d - 1], (s, q, row_peer(d))),
    )
    await_all(rbuf, 1)
    tile = min(128, n2)

    def add_rows(c, acc):
        rows = pl.ds(pl.multiple_of(r * n1 + c * tile, tile), tile)
        total = xbuf[rows, :].astype(F32)
        for d in range(n_rows - 1):
            total = total + rbuf[d, pl.ds(pl.multiple_of(c * tile, tile), tile), :].astype(F32)
        xbuf[rows, :] = total.astype(BF16)
        return acc

    lax.fori_loop(0, n1 // tile, add_rows, 0)
    spread_out(
        n_seq,
        2,
        lambda d: (
            piece(xbuf, r * n_seq + seq_peer(d), n2),
            r2buf.at[d - 1],
            (s, seq_peer(d), r),
        ),
    )
    await_all(r2buf, 2)
    final_rows = pl.ds(pl.multiple_of((r * n_seq + q) * n2, n2), n2)
    total = xbuf[final_rows, :].astype(F32)
    total = lax.fori_loop(
        0, n_seq - 1, lambda d, acc: acc + r2buf[d].astype(F32), total
    )
    gfin[final_rows, :] = total.astype(BF16)
    spread_out(
        n_seq,
        3,
        lambda d: (
            piece(gfin, r * n_seq + q, n2),
            piece(gfin, r * n_seq + q, n2),
            (s, seq_peer(d), r),
        ),
    )
    await_all(r2buf, 3)
    spread_out(
        n_rows,
        4,
        lambda d: (piece(gfin, r, n1), piece(gfin, r, n1), (s, q, row_peer(d))),
    )
    await_all(rbuf, 4)

    def widen(c, acc):
        at = pl.multiple_of(c * part, part)
        rows = pl.ds(at, part)
        gb_out[0, rows, :] = gfin[rows, :].astype(F32)
        gc_out[0, rows, :] = gfin[pl.ds(width + at, part), :].astype(F32)
        gglu_out[0, rows, :width] = gfin[pl.ds(2 * width + at, part), :].astype(F32)
        gglu_out[0, rows, width:] = gfin[pl.ds(3 * width + at, part), :].astype(F32)
        return acc

    lax.fori_loop(0, width // part, widen, 0)

    def pick(values):
        return jnp.where(on_upper, values[1], values[0])

    totals = []
    for l in range(2):
        gather_wait(gsmall.at[l], n_all, SEM_SMALL + l)
        zero_tile = jnp.zeros(gsmall.shape[2:], F32)
        totals.append(
            lax.fori_loop(0, n_all, lambda g, acc, l=l: acc + gsmall[l, g], zero_tile)
        )
    tile_sum = pick(totals)
    wt = width // LANES
    rows_of = [to_row(tile_sum[i * wt : (i + 1) * wt]) for i in range(5)]
    gskip_out[...] = rows_of[0]
    gglub_out[:, :width] = rows_of[1]
    gglub_out[:, width:] = rows_of[2]
    dr, di, dg = rows_of[3][:, :ns], rows_of[3][:, ns:], rows_of[4][:, :ns]
    lam = pick([dv[l, 0:1, :] for l in range(2)])
    lr, li = lam[:, :ns], lam[:, ns:]
    gnu_out[...] = -jnp.exp(nu_ref[...]) * (lr * dr + li * di)
    gtheta_out[...] = jnp.exp(theta_ref[...]) * (lr * di - li * dr)
    ggamma_out[...] = dg
    mean, var = rmean_ref[...], rvar_ref[...]
    for m in range(micro):
        mean = (1.0 - MOMENTUM) * mean + MOMENTUM * pick([sv[2 * l + m, 0:1, :] for l in range(2)])
        var = (1.0 - MOMENTUM) * var + MOMENTUM * pick([sv[2 * l + m, 3:4, :] for l in range(2)])
    nmean_out[...] = mean
    nvar_out[...] = var
    gbias_out[...] = pick([sum(sv[2 * l + m, 5:6, :] for m in range(micro)) for l in range(2)])
    ggain_out[...] = pick([sum(sv[2 * l + m, 6:7, :] for m in range(micro)) for l in range(2)])

    gather_sent(meta, n_all, SEM_META)
    for i in range(4):
        gather_sent(gst_all.at[i], n_all, SEM_STAT + i)
        gather_sent(gst_all.at[4 + i], n_all, SEM_NORM + i)
    for i in range(8):
        gather_sent(gline.at[i], n_line, SEM_LINE + i)
    for l in range(2):
        gather_sent(gsmall.at[l], n_all, SEM_SMALL + l)
    for ref, sem in ((rbuf, 1), (r2buf, 2), (r2buf, 3), (rbuf, 4)):
        pltpu.make_async_copy(ref, ref, rs_sem.at[sem]).wait()
    for item in outgoing:
        item.wait()


def on_device(n_seq, n_rows, *args):
    inputs, starts = args[0], args[2]
    micro, _, tokens, width = inputs.shape
    ns = args[9].shape[1]
    half = tokens // 2
    n_line = 2 * n_seq
    n_all = n_line * n_rows
    any_space = pl.BlockSpec(memory_space=pl.ANY)
    vmem = pl.BlockSpec(memory_space=pltpu.VMEM)
    in_specs = [vmem] * 16
    for i in (0, 1, 8, 12, 14):
        in_specs[i] = any_space
    flow = jax.ShapeDtypeStruct((1, micro, 1, tokens, width), BF16)
    row = lambda size: jax.ShapeDtypeStruct((1, size), F32)
    mat = lambda size: jax.ShapeDtypeStruct((1, width, size), F32)
    out_shape = (
        flow,
        flow,
        row(width),
        row(width),
        mat(2 * ns),
        row(ns),
        row(ns),
        row(ns),
        mat(width),
        row(width),
        mat(2 * width),
        row(2 * width),
        row(width),
        row(width),
    )
    out_specs = [any_space, any_space] + [vmem] * 12
    vf = lambda *shape: pltpu.VMEM(shape, F32)
    vb = lambda *shape: pltpu.VMEM(shape, BF16)
    dma = lambda count: pltpu.SemaphoreType.DMA((count,))
    rows_all = 4 * width
    scratch = [
        vb(micro, half, width),
        vb(micro, half, width),
        vb(2, width, 2 * ns),
        vb(2, 2 * ns, width),
        vb(2, width, 2 * width),
        vf(2, SUB, width),
        vf(2, SUB, width),
        vb(half, half),
        vb(half, half),
        vf(micro, half, LANES),
        vf(micro, half, LANES),
        vf(micro, half, LANES),
        vf(2 * micro, half, width),
        vb(2, micro * half, width),
        vf(2 * micro, half, width),
        vf(2 * micro, half + SUB, width),
        vb(2, micro * half, width),
        vb(2, micro * half, width),
        vb(micro * half, 2 * width),
        vb(micro * half, width),
        vf(micro, half, width),
        vb(micro * half, width),
        vf(micro, half, width),
        vf(micro, half, width),
        vf(micro, half, width),
        vb(micro, half, width),
        vb(micro, half, width),
        vb(micro, half, width),
        vb(micro, half, width),
        vb(2, micro, half, width),
        vf(2 * micro, SUB, width),
        vf(2 * micro, SUB, width),
        vf(n_all, SUB, LANES),
        vf(8, n_all, SUB, LANES),
        vf(8, n_line, SUB, LANES),
        vf(2, n_all, 24, LANES),
        vb(2, rows_all, width),
        vb(rows_all, width),
        vb(n_rows - 1, rows_all // n_rows, width),
        vb(n_seq - 1, rows_all // n_rows // n_seq, width),
        vb(rows_all, width),
        dma(7),
        dma(4),
        dma(4),
        dma(19),
        dma(19),
        dma(4),
        dma(4),
        dma(4),
        dma(5),
        dma(5),
    ]
    return pl.pallas_call(
        functools.partial(step_kernel, n_seq, n_rows),
        out_shape=out_shape,
        in_specs=in_specs,
        out_specs=out_specs,
        scratch_shapes=scratch,
        compiler_params=pltpu.CompilerParams(
            collective_id=0, has_side_effects=True, vmem_limit_bytes=63 * 2**20
        ),
        name="lru_blocks",
    )(*args)


def solution(mesh):
    placed = (
        P(None, "rows", "seq", None),
        P(None, "rows", "seq", None),
        P(None, "rows", "seq"),
        P(None, "rows", "seq"),
        P("section", None),
        P("section", None),
        P("section", None),
        P("section", None),
        P("section", None, None),
        P("section", None),
        P("section", None),
        P("section", None),
        P("section", None, None),
        P("section", None),
        P("section", None, None),
        P("section", None),
    )
    return jax.shard_map(
        functools.partial(on_device, mesh.shape["seq"], mesh.shape["rows"]),
        mesh=mesh,
        in_specs=placed,
        out_specs=(
            P("section", None, "rows", "seq", None),
            P("section", None, "rows", "seq", None),
            P("section", None),
            P("section", None),
            P("section", None, None),
            P("section", None),
            P("section", None),
            P("section", None),
            P("section", None, None),
            P("section", None),
            P("section", None, None),
            P("section", None),
            P("section", None),
            P("section", None),
        ),
        check_vma=False,
    )
```

```python
import functools
import math

import jax
import jax.numpy as jnp
from jax import lax
from jax.experimental import pallas as pl
from jax.experimental.pallas import tpu as pltpu
from jax.sharding import PartitionSpec as P

NORM_EPS = 1e-05
MOMENTUM = 0.1
GELU_C = math.sqrt(2.0 / math.pi)
GELU_K = 0.044715
MESH = pl.DeviceIdType.MESH
F32 = jnp.float32
BF16 = jnp.bfloat16
SUB = 8
LANES = 128
GRAD_COLS = 256


def dot_nn(a, b):
    return lax.dot_general(a, b, (((1,), (0,)), ((), ())), preferred_element_type=F32)


def dot_nt(a, b):
    return lax.dot_general(a, b, (((1,), (1,)), ((), ())), preferred_element_type=F32)


def dot_tn(a, b):
    return lax.dot_general(a, b, (((0,), (0,)), ((), ())), preferred_element_type=F32)


def wide(mask, times):
    return jnp.concatenate([mask] * times, axis=1)


def to_tile(row):
    return jnp.concatenate(
        [row[:, i * LANES : (i + 1) * LANES] for i in range(row.shape[1] // LANES)], axis=0
    )


def to_row(tile):
    return jnp.concatenate([tile[i : i + 1, :] for i in range(tile.shape[0])], axis=1)


def cmul(ar, ai, br, bi):
    return ar * br - ai * bi, ar * bi + ai * br


def cpow(re, im, count):
    out = None
    while count:
        if count % 2:
            out = (re, im) if out is None else cmul(out[0], out[1], re, im)
        count //= 2
        if count:
            re, im = cmul(re, im, re, im)
    return out


def fold_rows(value):
    return jnp.sum(value.reshape(value.shape[0] // SUB, SUB, value.shape[1]), axis=0)


def step_kernel(
    n_seq,
    n_rows,
    x_hbm,
    cot_hbm,
    starts_ref,
    valid_ref,
    gain_ref,
    bias_ref,
    rmean_ref,
    rvar_ref,
    b_hbm,
    nu_ref,
    theta_ref,
    gamma_ref,
    c_hbm,
    skip_ref,
    glu_hbm,
    glub_ref,
    act_out,
    ig_out,
    grad_out,
    small_out,
    xnat,
    cnat,
    wb,
    wc,
    wg,
    pv,
    dv,
    perm,
    perm_t,
    keep_a,
    keep_d,
    live,
    hid,
    ulow,
    drive,
    state,
    slow,
    alow,
    dgate,
    dread,
    gst,
    dproj,
    dmix,
    dunit,
    dout,
    sig_s,
    gat_s,
    dgelu_s,
    low_s,
    nat,
    sv,
    sm,
    meta,
    gst_all,
    gline,
    gsmall,
    gbuf,
    pair_buf,
    rows_buf,
    seq_buf,
    gfin,
    in_sem,
    wsend_sem,
    wrecv_sem,
    gs_sem,
    gr_sem,
    out_sem,
    osend_sem,
    orecv_sem,
    rs_sem,
    rr_sem,
    gout_sem,
):
    micro = x_hbm.shape[0]
    tokens = x_hbm.shape[2]
    half = tokens // 2
    seg = half // SUB
    width = x_hbm.shape[3]
    ns = nu_ref.shape[1]
    n_line = 2 * n_seq
    n_all = n_line * n_rows
    chunk = min(128, half)
    n_chunk = half // chunk

    s = lax.axis_index("section")
    q = lax.axis_index("seq")
    r = lax.axis_index("rows")
    rank = q * 2 + s
    me = rank * n_rows + r
    partner = (1 - s, q, r)

    def peer_all(d):
        g = lax.rem(me + d, n_all)
        k = g // n_rows
        return (k % 2, k // 2, g % n_rows)

    def peer_line(d):
        k = lax.rem(rank + d, n_line)
        return (k % 2, k // 2, r)

    def gather_start(buf, mine, count, peer, sem):
        def one(d, carry):
            pltpu.make_async_remote_copy(
                src_ref=buf.at[mine],
                dst_ref=buf.at[mine],
                send_sem=gs_sem.at[sem],
                recv_sem=gr_sem.at[sem],
                device_id=peer(d),
                device_id_type=MESH,
            ).start()
            return carry

        lax.fori_loop(1, count, one, 0)

    def gather_wait(buf, count, sem):
        part = buf.at[pl.ds(0, count - 1)]
        pltpu.make_async_copy(part, part, gr_sem.at[sem]).wait()

    def gather_sent(buf, count, sem):
        part = buf.at[pl.ds(0, count - 1)]
        pltpu.make_async_copy(part, part, gs_sem.at[sem]).wait()

    barrier = pltpu.get_barrier_semaphore()

    def greet(d, carry):
        pl.semaphore_signal(barrier, inc=1, device_id=peer_all(d), device_id_type=MESH)
        return carry

    lax.fori_loop(1, n_all, greet, 0)

    start_at = pl.multiple_of(s * half, half)
    my_tokens = pl.ds(start_at, half)
    loads = []
    for m in range(micro):
        loads.append(
            pltpu.make_async_copy(x_hbm.at[m, 0, my_tokens], xnat.at[m], in_sem.at[m])
        )
    own_w = [
        pltpu.make_async_copy(b_hbm.at[0], wb.at[s], in_sem.at[4]),
        pltpu.make_async_copy(c_hbm.at[0], wc.at[s], in_sem.at[5]),
        pltpu.make_async_copy(glu_hbm.at[0], wg.at[s], in_sem.at[6]),
    ]
    cot_loads = [
        pltpu.make_async_copy(cot_hbm.at[m, 0, my_tokens], cnat.at[m], in_sem.at[2 + m])
        for m in range(micro)
    ]
    for item in loads + own_w + cot_loads:
        item.start()

    pv[s, 0:1, :] = gain_ref[...]
    pv[s, 1:2, :] = bias_ref[...]
    pv[s, 2:3, :] = skip_ref[...]
    pv[s, 3:4, :] = glub_ref[:, :width]
    pv[s, 4:5, :] = glub_ref[:, width:]
    pv[s, 5:6, :] = jnp.concatenate([nu_ref[...], theta_ref[...]], axis=1)
    pv[s, 6:7, :] = jnp.concatenate([gamma_ref[...], gamma_ref[...]], axis=1)
    pv[s, 7:8, :] = jnp.zeros((1, width), F32)

    here = lax.broadcasted_iota(jnp.int32, (half, half), 0)
    there = lax.broadcasted_iota(jnp.int32, (half, half), 1)
    perm[...] = jnp.where((here % SUB) * seg + here // SUB == there, 1.0, 0.0).astype(BF16)
    perm_t[...] = jnp.where((there % SUB) * seg + there // SUB == here, 1.0, 0.0).astype(BF16)

    st_all = starts_ref[:, 0, :].astype(F32)
    va_all = valid_ref[:, 0, :].astype(F32)
    nx_all = pltpu.roll(st_all, tokens - 1, 1)
    on_upper = s == 1
    st_half = jnp.where(on_upper, st_all[:, half:], st_all[:, :half])
    va_half = jnp.where(on_upper, va_all[:, half:], va_all[:, :half])
    nx_half = jnp.where(on_upper, nx_all[:, half:], nx_all[:, :half])
    place = lax.broadcasted_iota(jnp.int32, (micro, half), 1)
    nx_half = jnp.where(place == half - 1, 0.0, nx_half)
    counts = []
    for m in range(micro):
        stacked = jnp.concatenate(
            [
                jnp.broadcast_to(1.0 - st_half[m : m + 1], (LANES, half)),
                jnp.broadcast_to(1.0 - nx_half[m : m + 1], (LANES, half)),
                jnp.broadcast_to(va_half[m : m + 1], (LANES, half)),
            ],
            axis=0,
        ).astype(BF16)
        spread = dot_nt(perm[...], stacked)
        keep_a[m] = spread[:, :LANES]
        keep_d[m] = spread[:, LANES : 2 * LANES]
        live[m] = spread[:, 2 * LANES :]
        counts.append(jnp.sum(va_half[m : m + 1], axis=1, keepdims=True))
    rows_low = lax.broadcasted_iota(jnp.int32, (SUB, LANES), 0) < 4
    meta[me] = jnp.where(
        rows_low,
        jnp.broadcast_to(counts[0], (SUB, LANES)),
        jnp.broadcast_to(counts[micro - 1], (SUB, LANES)),
    )

    pl.semaphore_wait(barrier, n_all - 1)

    def share(source, target, index):
        return pltpu.make_async_remote_copy(
            src_ref=source,
            dst_ref=target,
            send_sem=wsend_sem.at[index],
            recv_sem=wrecv_sem.at[index],
            device_id=partner,
            device_id_type=MESH,
        )

    shares = [
        share(pv.at[s], pv.at[s], 0),
        share(b_hbm.at[0], wb.at[s], 1),
        share(c_hbm.at[0], wc.at[s], 2),
        share(glu_hbm.at[0], wg.at[s], 3),
    ]
    SEM_META, SEM_STAT, SEM_NORM, SEM_LINE, SEM_SMALL = 0, 1, 5, 9, 17
    gather_start(meta, me, n_all, peer_all, SEM_META)
    for item in shares:
        item.start()

    def chunks(body, init):
        return lax.fori_loop(0, n_chunk, lambda c, acc: body(pl.multiple_of(c * chunk, chunk), acc), init)

    zero_sum = jnp.zeros((SUB, width), F32)

    def enter(m):
        def body(at, acc):
            rows = pl.ds(at, chunk)
            value = dot_nn(perm[rows, :], xnat[m])
            hid[m, rows, :] = value
            return acc + fold_rows(value * wide(live[m, rows, :], width // LANES))

        return chunks(body, zero_sum)

    def send_stats(l, m, total):
        mean = jnp.sum(total, axis=0, keepdims=True) / jnp.maximum(counts[m], 1.0)

        def body(at, acc):
            rows = pl.ds(at, chunk)
            off = hid[2 * l + m, rows, :] - mean
            return acc + fold_rows(off * off * wide(live[m, rows, :], width // LANES))

        spread = jnp.sum(chunks(body, zero_sum), axis=0, keepdims=True)
        buf = gst_all.at[2 * l + m]
        buf[me] = jnp.concatenate([to_tile(mean), to_tile(spread)], axis=0)
        gather_start(buf, me, n_all, peer_all, SEM_STAT + 2 * l + m)

    def take_stats(l, m):
        buf = gst_all.at[2 * l + m]
        gather_wait(buf, n_all, SEM_STAT + 2 * l + m)
        data = buf[...]
        count = meta[:, 4 * m : 4 * m + 1, :] if micro == 2 else meta[:, 0:1, :]
        total = jnp.sum(count, axis=0)
        low4 = lax.broadcasted_iota(jnp.int32, (1, SUB, LANES), 1) < 4
        weighted = jnp.sum(data * jnp.where(low4, count, 1.0), axis=0)
        mean = weighted[0:4] / total
        apart = data[:, 0:4, :] - mean[None]
        var = (weighted[4:8] + jnp.sum(count * apart * apart, axis=0)) / total
        mean_row, var_row = to_row(mean), to_row(var)
        scale = lax.rsqrt(var_row + NORM_EPS)
        box = sv.at[2 * l + m]
        box[0:1, :] = mean_row
        box[1:2, :] = scale
        box[2:3, :] = scale * pv[l, 0:1, :]
        box[3:4, :] = var_row
        box[4:5, :] = jnp.broadcast_to(total[:, 0:1], (1, width))

    def unit_of(l, m, rows):
        box = sv.at[2 * l + m]
        return (hid[2 * l + m, rows, :] - box[0:1, :]) * box[2:3, :] + pv[l, 1:2, :]

    def lam_rows(l, which, conj):
        re = dv[l, which : which + 1, :ns]
        im = dv[l, which : which + 1, ns:]
        return re, (-im if conj else im)

    unroll = min(8, seg)

    def scan_local(u_ref, keep_ref, l, desc, conj):
        lr, li = lam_rows(l, 0, conj)
        lr = jnp.broadcast_to(lr, (SUB, ns))
        li = jnp.broadcast_to(li, (SUB, ns))

        def body(jj, carry):
            re, im = carry
            for t in range(unroll):
                j = jj * unroll + t
                if desc:
                    j = seg - 1 - j
                rows = pl.ds(pl.multiple_of(j * SUB, SUB), SUB)
                keep = wide(keep_ref[rows, :], ns // LANES)
                u = u_ref[rows, :]
                kr, ki = keep * re, keep * im
                re = lr * kr - li * ki + u[:, :ns]
                im = lr * ki + li * kr + u[:, ns:]
            return re, im

        zero = jnp.zeros((SUB, ns), F32)
        return lax.fori_loop(0, seg // unroll, body, (zero, zero))

    spot = lambda: lax.broadcasted_iota(jnp.int32, (SUB, ns), 0)

    def before(value, step, desc, blank):
        if desc:
            return jnp.where(spot() < SUB - step, pltpu.roll(value, SUB - step, 0), blank)
        return jnp.where(spot() >= step, pltpu.roll(value, step, 0), blank)

    def join_segments(er, ei, keep_ref, l, desc, conj):
        shut = jnp.min(keep_ref[...].reshape(seg, SUB, LANES), axis=0)
        lr, li = lam_rows(l, 1, conj)
        ar, ai = lr * wide(shut, ns // LANES), li * wide(shut, ns // LANES)
        for step in (1, 2, 4):
            pr, pi = cmul(ar, ai, before(er, step, desc, 0.0), before(ei, step, desc, 0.0))
            er, ei = er + pr, ei + pi
            ar, ai = cmul(ar, ai, before(ar, step, desc, 1.0), before(ai, step, desc, 0.0))
        last = 0 if desc else SUB - 1
        out = (er[last : last + 1], ei[last : last + 1], jnp.min(shut, axis=0, keepdims=True))
        shifted = (
            before(er, 1, desc, 0.0),
            before(ei, 1, desc, 0.0),
            before(ar, 1, desc, 1.0),
            before(ai, 1, desc, 0.0),
        )
        return out, shifted

    def send_carry(phase, l, m, u_ref, desc, conj):
        keep_ref = keep_d.at[m] if desc else keep_a.at[m]
        er, ei = scan_local(u_ref, keep_ref, l, desc, conj)
        (tr, ti, shut), shifted = join_segments(er, ei, keep_ref, l, desc, conj)
        if desc:
            first = keep_a[m, 0:1, :]
            tr, ti, shut = tr * wide(first, ns // LANES), ti * wide(first, ns // LANES), shut * first
        index = phase * 4 + 2 * l + m
        buf = gline.at[index]
        buf[rank] = jnp.concatenate(
            [
                to_tile(tr),
                to_tile(ti),
                shut,
                jnp.zeros((SUB - 2 * ns // LANES - 1, LANES), F32),
            ],
            axis=0,
        )
        gather_start(buf, rank, n_line, peer_line, SEM_LINE + index)
        return shifted

    def take_carry(phase, l, m, shifted, desc, conj):
        index = phase * 4 + 2 * l + m
        buf = gline.at[index]
        gather_wait(buf, n_line, SEM_LINE + index)
        lr, li = lam_rows(l, 2, conj)
        tiles = ns // LANES

        def body(step, carry):
            cr, ci = carry
            k = n_line - 1 - step if desc else step
            box = buf[k]
            shut = wide(box[2 * tiles : 2 * tiles + 1], tiles)
            pr, pi = cmul(lr * shut, li * shut, cr, ci)
            pr = pr + to_row(box[:tiles])
            pi = pi + to_row(box[tiles : 2 * tiles])
            use = k > rank if desc else k < rank
            return jnp.where(use, pr, cr), jnp.where(use, pi, ci)

        zero = jnp.zeros((1, ns), F32)
        cr, ci = lax.fori_loop(0, n_line, body, (zero, zero))
        er, ei, ar, ai = shifted
        pr, pi = cmul(ar, ai, cr, ci)
        return er + pr, ei + pi

    def fill_states(l, m, shifted):
        desc = l == 1
        re, im = take_carry(0, l, m, shifted, desc, False)
        keep_ref = keep_d.at[m] if desc else keep_a.at[m]
        u_ref, s_ref = drive.at[2 * l + m], state.at[2 * l + m]
        lr, li = lam_rows(l, 0, False)
        lr = jnp.broadcast_to(lr, (SUB, ns))
        li = jnp.broadcast_to(li, (SUB, ns))
        s_ref[pl.ds(half if desc else 0, SUB), :] = jnp.concatenate([re, im], axis=1)

        def body(jj, carry):
            re, im = carry
            for t in range(unroll):
                j = jj * unroll + t
                if desc:
                    j = seg - 1 - j
                at = pl.multiple_of(j * SUB, SUB)
                rows = pl.ds(at, SUB)
                keep = wide(keep_ref[rows, :], ns // LANES)
                u = u_ref[rows, :]
                kr, ki = keep * re, keep * im
                re = lr * kr - li * ki + u[:, :ns]
                im = lr * ki + li * kr + u[:, ns:]
                to = rows if desc else pl.ds(at + SUB, SUB)
                s_ref[to, :] = jnp.concatenate([re, im], axis=1)
            return re, im

        lax.fori_loop(0, seg // unroll, body, (re, im))

    def fill_grads(l, m, shifted):
        desc = l == 0
        re, im = take_carry(1, l, m, shifted, desc, True)
        keep_ref = keep_d.at[m] if desc else keep_a.at[m]
        pkeep_ref = keep_a.at[m] if desc else keep_d.at[m]
        u_ref, s_ref, g_ref = drive.at[2 * l + m], state.at[2 * l + m], gst.at[m]
        lr, li = lam_rows(l, 0, True)
        lr = jnp.broadcast_to(lr, (SUB, ns))
        li = jnp.broadcast_to(li, (SUB, ns))
        zero = jnp.zeros((SUB, ns), F32)

        def body(jj, carry):
            re, im, dr, di, dg = carry
            for t in range(unroll):
                j = jj * unroll + t
                if desc:
                    j = seg - 1 - j
                at = pl.multiple_of(j * SUB, SUB)
                rows = pl.ds(at, SUB)
                keep = wide(keep_ref[rows, :], ns // LANES)
                g = g_ref[rows, :]
                kr, ki = keep * re, keep * im
                re = lr * kr - li * ki + g[:, :ns]
                im = lr * ki + li * kr + g[:, ns:]
                g_ref[rows, :] = jnp.concatenate([re, im], axis=1)
                u = u_ref[rows, :]
                dg = dg + (re * u[:, :ns] + im * u[:, ns:])
                old = s_ref[rows if desc else pl.ds(at + SUB, SUB), :]
                pkeep = wide(pkeep_ref[rows, :], ns // LANES)
                pr, pi = pkeep * old[:, :ns], pkeep * old[:, ns:]
                dr = dr + (pr * re + pi * im)
                di = di + (pr * im - pi * re)
            return re, im, dr, di, dg

        _, _, dr, di, dg = lax.fori_loop(0, seg // unroll, body, (re, im, zero, zero, zero))
        box = sm.at[2 * l + m]
        box[3:4, :] = jnp.sum(jnp.concatenate([dr, di], axis=1), axis=0, keepdims=True)
        box[4:5, :] = jnp.sum(jnp.concatenate([dg, dg], axis=1), axis=0, keepdims=True)

    def project(l, m):
        gamma2 = dv[l, 3:4, :]

        def body(at, acc):
            rows = pl.ds(at, chunk)
            low = unit_of(l, m, rows).astype(BF16)
            ulow[l, pl.ds(m * half + at, chunk), :] = low
            drive[2 * l + m, rows, :] = dot_nn(low, wb[l]) * gamma2
            return acc

        chunks(body, 0)
        return send_carry(0, l, m, drive.at[2 * l + m], l == 1, False)

    def mix(l, m, at):
        rows = pl.ds(at, chunk)
        big = pl.ds(m * half + at, chunk)
        low = state[2 * l + m, pl.ds(at + (0 if l == 1 else SUB), chunk), :].astype(BF16)
        slow[l, big, :] = low
        unit = unit_of(l, m, rows)
        mixed = dot_nn(low, wc[l]) + pv[l, 2:3, :] * unit
        square = mixed * mixed
        t = jnp.tanh((GELU_C * mixed) * (1.0 + GELU_K * square))
        half_up = 0.5 * (1.0 + t)
        act = (mixed * half_up).astype(BF16)
        alow[l, big, :] = act
        slope = half_up + (0.5 * GELU_C) * mixed * (1.0 - t * t) * (1.0 + (3.0 * GELU_K) * square)
        gates = dot_nn(act, wg[l])
        value = gates[:, :width] + pv[l, 3:4, :]
        gate = 0.5 * jnp.tanh(0.5 * (gates[:, width:] + pv[l, 4:5, :])) + 0.5
        branch = value * gate
        return unit, slope, gate, branch, (hid[2 * l + m, rows, :] + branch).astype(BF16)

    def finish_lower(m):
        def body(at, acc):
            rows = pl.ds(at, chunk)
            unit, slope, gate, branch, low = mix(0, m, at)
            sig_s[m, rows, :] = gate.astype(BF16)
            gat_s[m, rows, :] = (branch * (1.0 - gate)).astype(BF16)
            dgelu_s[m, rows, :] = slope.astype(BF16)
            low_s[m, rows, :] = low
            value = low.astype(F32)
            hid[2 + m, rows, :] = value
            return acc + fold_rows(value * wide(live[m, rows, :], width // LANES))

        return chunks(body, zero_sum)

    def to_natural(low_ref, nat_ref):
        def body(at, acc):
            rows = pl.ds(at, chunk)
            nat_ref[rows, :] = dot_nn(perm_t[rows, :], low_ref[...]).astype(BF16)
            return acc

        chunks(body, 0)

    def ship(out, m, tag):
        base = tag * 2 + m
        local = pltpu.make_async_copy(
            nat.at[s, m], out.at[0, m, 0, my_tokens], out_sem.at[base]
        )
        remote = pltpu.make_async_remote_copy(
            src_ref=nat.at[1 - s, m],
            dst_ref=out.at[0, m, 0, my_tokens],
            send_sem=osend_sem.at[base],
            recv_sem=orecv_sem.at[base],
            device_id=partner,
            device_id_type=MESH,
        )
        local.start()
        remote.start()
        return local, remote

    def gate_grads(l, m, at, unit, slope, gate, other, grad, acc):
        rows = pl.ds(at, chunk)
        big = pl.ds(m * half + at, chunk)
        d_gates = jnp.concatenate([grad * gate, grad * other], axis=1).astype(BF16)
        dgate[big, :] = d_gates
        d_mixed = dot_nt(d_gates, wg[l]) * slope
        dmix[m, rows, :] = d_mixed
        d_read = d_mixed.astype(BF16)
        dread[big, :] = d_read
        gst[m, rows, :] = dot_nt(d_read, wc[l])
        return acc[0] + fold_rows(d_gates.astype(F32)), acc[1] + fold_rows(d_mixed * unit)

    gate_zero = (jnp.zeros((SUB, 2 * width), F32), zero_sum)

    def keep_gate_sums(l, m, acc):
        box = sm.at[2 * l + m]
        box[0:1, :] = jnp.sum(acc[1], axis=0, keepdims=True)
        both = jnp.sum(acc[0], axis=0, keepdims=True)
        box[1:2, :] = both[:, :width]
        box[2:3, :] = both[:, width:]

    def turn_upper(m):
        def body(at, acc):
            rows = pl.ds(at, chunk)
            unit, slope, gate, branch, low = mix(1, m, at)
            low_s[m, rows, :] = low
            grad = dot_nn(perm[rows, :], cnat[m])
            dout[m, rows, :] = grad
            return gate_grads(1, m, at, unit, slope, gate, branch * (1.0 - gate), grad, acc)

        keep_gate_sums(1, m, chunks(body, gate_zero))
        return send_carry(1, 1, m, gst.at[m], False, True)

    def unproject(l, m):
        gamma2 = dv[l, 3:4, :]

        def body(at, acc):
            rows = pl.ds(at, chunk)
            low = (gst[m, rows, :] * gamma2).astype(BF16)
            dproj[pl.ds(m * half + at, chunk), :] = low
            value = dmix[m, rows, :] * pv[l, 2:3, :] + dot_nt(low, wb[l])
            dunit[m, rows, :] = value
            normed = (hid[2 * l + m, rows, :] - sv[2 * l + m, 0:1, :]) * sv[2 * l + m, 1:2, :]
            return acc[0] + fold_rows(value), acc[1] + fold_rows(value * normed)

        by_bias, by_gain = chunks(body, (zero_sum, zero_sum))
        buf = gst_all.at[4 + 2 * l + m]
        buf[me] = jnp.concatenate(
            [
                to_tile(jnp.sum(by_bias, axis=0, keepdims=True)),
                to_tile(jnp.sum(by_gain, axis=0, keepdims=True)),
            ],
            axis=0,
        )
        gather_start(buf, me, n_all, peer_all, SEM_NORM + 2 * l + m)

    def take_norm(l, m):
        buf = gst_all.at[4 + 2 * l + m]
        gather_wait(buf, n_all, SEM_NORM + 2 * l + m)
        both = jnp.sum(buf[...], axis=0)
        box = sv.at[2 * l + m]
        box[5:6, :] = to_row(both[0:4])
        box[6:7, :] = to_row(both[4:8])

    def input_grads(l, m, rows):
        box = sv.at[2 * l + m]
        share_of = 1.0 / box[4:5, :]
        by_bias = box[2:3, :] * box[5:6, :] * share_of
        by_gain = box[2:3, :] * box[6:7, :] * share_of
        normed = (hid[2 * l + m, rows, :] - box[0:1, :]) * box[1:2, :]
        mask = wide(live[m, rows, :], width // LANES)
        return (
            dout[m, rows, :]
            + dunit[m, rows, :] * box[2:3, :]
            - mask * (by_bias + normed * by_gain)
        ).astype(BF16)

    def turn_lower(m):
        def body(at, acc):
            rows = pl.ds(at, chunk)
            low = input_grads(1, m, rows)
            low_s[m, rows, :] = low
            grad = low.astype(F32)
            dout[m, rows, :] = grad
            return gate_grads(
                0,
                m,
                at,
                unit_of(0, m, rows),
                dgelu_s[m, rows, :].astype(F32),
                sig_s[m, rows, :].astype(F32),
                gat_s[m, rows, :].astype(F32),
                grad,
                acc,
            )

        keep_gate_sums(0, m, chunks(body, gate_zero))
        return send_carry(1, 0, m, gst.at[m], True, True)

    def finish_grads(m):
        def body(at, acc):
            rows = pl.ds(at, chunk)
            low_s[m, rows, :] = input_grads(0, m, rows)
            return acc

        chunks(body, 0)

    part = 256

    def weight_grads(l, left, right, row_at):
        blocks = right.shape[1] // GRAD_COLS

        def body(c, acc):
            at = pl.multiple_of(c * part, part)
            for k in range(blocks):
                columns = pl.ds(k * GRAD_COLS, GRAD_COLS)
                value = dot_tn(left[l, :, pl.ds(at, part)], right[:, columns])
                to = pl.multiple_of(row_at + k * width + at, part)
                gbuf[l, pl.ds(to, part), :] = value.astype(BF16)
            return acc

        lax.fori_loop(0, width // part, body, 0)

    per = width // GRAD_COLS
    groups = ((per * width, 3 * per * width), (0, per * width))

    class Reduce:
        def __init__(self, l, g):
            self.l, self.base, count = l, groups[g][0], groups[g][1]
            self.mine = count // 2
            self.at = 0 if g == 0 else groups[0][1] // 2
            self.n1 = self.mine // n_rows
            self.n2 = max(16, self.n1 // n_seq)
            self.owners = self.n1 // self.n2
            self.at1 = 0 if g == 0 else groups[0][1] // 2 // n_rows
            self.sem = (2 * l + g) * 5
            n2_first = max(16, self.at1 // n_seq)
            self.at2 = 0 if g == 0 else n2_first

        def send(self, source, target, sem, where):
            return pltpu.make_async_remote_copy(
                src_ref=source,
                dst_ref=target,
                send_sem=rs_sem.at[self.sem + sem],
                recv_sem=rr_sem.at[self.sem + sem],
                device_id=where,
                device_id_type=MESH,
            )

        def await_rows(self, count, sem, sems=None):
            ref = gfin.at[0, pl.ds(0, count)]
            pltpu.make_async_copy(ref, ref, (rr_sem if sems is None else sems).at[self.sem + sem]).wait()

        def half_of(self, core):
            return gbuf.at[self.l, pl.ds(pl.multiple_of(self.base + core * self.mine, 16), self.mine)]

        def total(self):
            return pair_buf.at[self.l, pl.ds(self.at, self.mine)]

        def piece(self, ref, index, size):
            return ref.at[pl.ds(pl.multiple_of(index * size, 16), size)]

        def pair(self):
            self.send(self.half_of(1 - s), self.total(), 0, partner).start()

        def rows(self):
            self.await_rows(self.mine, 0)
            own, total = self.half_of(s), self.total()

            def body(c, acc):
                rows = pl.ds(pl.multiple_of(c * 128, 128), 128)
                value = own[rows, :].astype(F32) + total[rows, :].astype(F32)
                total[rows, :] = value.astype(BF16)
                return acc

            lax.fori_loop(0, self.mine // 128, body, 0)
            into = rows_buf.at[self.l, :, pl.ds(self.at1, self.n1)]

            def one(d, acc):
                to = lax.rem(r + d, n_rows)
                self.send(self.piece(total, to, self.n1), into.at[d - 1], 1, (s, q, to)).start()
                return acc

            lax.fori_loop(1, n_rows, one, 0)

        def seq(self):
            self.await_rows((n_rows - 1) * self.n1, 1)
            total = self.piece(self.total(), r, self.n1)
            step = min(64, self.n1)

            def body(c, acc):
                at = pl.multiple_of(c * step, step)
                value = total[pl.ds(at, step), :].astype(F32)
                for d in range(n_rows - 1):
                    value = value + rows_buf[
                        self.l, d, pl.ds(pl.multiple_of(self.at1 + at, step), step), :
                    ].astype(F32)
                total[pl.ds(at, step), :] = value.astype(BF16)
                return acc

            lax.fori_loop(0, self.n1 // step, body, 0)
            into = seq_buf.at[self.l, :, pl.ds(self.at2, self.n2)]

            def one(d, acc):
                to = lax.rem(q + d, n_seq)

                def go():
                    self.send(self.piece(total, to, self.n2), into.at[d - 1], 2, (s, to, r)).start()

                self.when(to < self.owners, go)
                return acc

            lax.fori_loop(1, n_seq, one, 0)

        def when(self, condition, go):
            if self.owners == n_seq:
                go()
            else:
                pl.when(condition)(go)

        def block(self):
            return gfin.at[self.l, pl.ds(pl.multiple_of(self.at + r * self.n1, 16), self.n1)]

        def back_seq(self):
            total = self.piece(self.total(), r, self.n1)
            mine = self.piece(self.block(), q, self.n2)

            def go():
                self.await_rows((n_seq - 1) * self.n2, 2)
                value = self.piece(total, q, self.n2)[...].astype(F32)
                for d in range(n_seq - 1):
                    value = value + seq_buf[self.l, d, pl.ds(self.at2, self.n2), :].astype(F32)
                mine[...] = value.astype(BF16)

                def one(d, acc):
                    to = lax.rem(q + d, n_seq)
                    self.send(mine, mine, 3, (s, to, r)).start()
                    return acc

                lax.fori_loop(1, n_seq, one, 0)

            self.when(q < self.owners, go)

        def back_rows(self):
            self.when(q < self.owners, lambda: self.await_rows((self.owners - 1) * self.n2, 3))
            if self.owners < n_seq:
                self.when(q >= self.owners, lambda: self.await_rows(self.owners * self.n2, 3))
            mine = self.block()

            def one(d, acc):
                self.send(mine, mine, 4, (s, q, lax.rem(r + d, n_rows))).start()
                return acc

            lax.fori_loop(1, n_rows, one, 0)

        def out_copies(self):
            source = gfin.at[self.l, pl.ds(self.at, self.mine)]
            target = grad_out.at[pl.ds(pl.multiple_of(self.base + s * self.mine, 16), self.mine)]
            which = self.sem // 5
            local = pltpu.make_async_copy(source, target, gout_sem.at[0, which])
            remote = pltpu.make_async_remote_copy(
                src_ref=source,
                dst_ref=target,
                send_sem=gout_sem.at[1, which],
                recv_sem=gout_sem.at[2, which],
                device_id=partner,
                device_id_type=MESH,
            )
            return local, remote

        def out(self):
            self.await_rows((n_rows - 1) * self.n1, 4)
            local, remote = self.out_copies()
            pl.when(s == self.l)(local.start)
            pl.when(s != self.l)(remote.start)

        def done(self):
            local, remote = self.out_copies()

            def settle():
                local.wait()
                remote.wait_recv()

            pl.when(s == self.l)(settle)
            pl.when(s != self.l)(remote.wait_send)
            self.await_rows(self.mine, 0, rs_sem)
            self.await_rows((n_rows - 1) * self.n1, 1, rs_sem)
            self.when(q < self.owners, lambda: self.await_rows((self.owners - 1) * self.n2, 2, rs_sem))
            if self.owners < n_seq:
                self.when(q >= self.owners, lambda: self.await_rows(self.owners * self.n2, 2, rs_sem))
            self.when(q < self.owners, lambda: self.await_rows((n_seq - 1) * self.n2, 3, rs_sem))
            self.await_rows((n_rows - 1) * self.n1, 4, rs_sem)

    reduce = [[Reduce(l, g) for g in range(2)] for l in range(2)]

    def send_small(l):
        buf = gsmall.at[l]
        both = sm[2 * l]
        for m in range(1, micro):
            both = both + sm[2 * l + m]
        buf[me] = jnp.concatenate(
            [to_tile(both[i : i + 1]) for i in range(5)] + [jnp.zeros((4, LANES), F32)], axis=0
        )
        gather_start(buf, me, n_all, peer_all, SEM_SMALL + l)

    for item in loads:
        item.wait()
    for m in range(micro):
        send_stats(0, m, enter(m))
    for item in own_w:
        item.wait()
    for item in shares:
        item.wait()
    for l in range(2):
        decay = jnp.exp(-jnp.exp(pv[l, 5:6, :ns]))
        phase = jnp.exp(pv[l, 5:6, ns:])
        re, im = decay * jnp.cos(phase), decay * jnp.sin(phase)
        dv[l, 0:1, :] = jnp.concatenate([re, im], axis=1)
        dv[l, 1:2, :] = jnp.concatenate(cpow(re, im, seg), axis=1)
        dv[l, 2:3, :] = jnp.concatenate(cpow(re, im, half), axis=1)
        dv[l, 3:4, :] = jnp.exp(pv[l, 6:7, :])
    gather_wait(meta, n_all, SEM_META)

    shifted = {}
    for m in range(micro):
        take_stats(0, m)
        shifted[m] = project(0, m)
    for m in range(micro):
        fill_states(0, m, shifted[m])
        send_stats(1, m, finish_lower(m))
        to_natural(low_s.at[m], nat.at[0, m])
    for m in range(micro):
        take_stats(1, m)
        shifted[m] = project(1, m)
    for item in cot_loads:
        item.wait()
    outgoing = []
    for m in range(micro):
        fill_states(1, m, shifted[m])
        shifted[m] = turn_upper(m)
        to_natural(low_s.at[m], nat.at[1, m])
        outgoing += ship(act_out, m, 0)
    weight_grads(1, slow, dread, per * width)
    weight_grads(1, alow, dgate, 2 * per * width)
    reduce[1][0].pair()
    fill_grads(1, 0, shifted[0])
    unproject(1, 0)
    reduce[1][0].rows()
    for m in range(1, micro):
        fill_grads(1, m, shifted[m])
        unproject(1, m)
    weight_grads(1, ulow, dproj, 0)
    reduce[1][1].pair()
    send_small(1)
    for item in outgoing:
        item.wait()
    outgoing = []
    take_norm(1, 0)
    shifted[0] = turn_lower(0)
    to_natural(low_s.at[0], nat.at[1, 0])
    reduce[1][0].seq()
    reduce[1][1].rows()
    for m in range(1, micro):
        take_norm(1, m)
        shifted[m] = turn_lower(m)
        to_natural(low_s.at[m], nat.at[1, m])
    reduce[1][0].back_seq()
    reduce[1][1].seq()
    weight_grads(0, slow, dread, per * width)
    weight_grads(0, alow, dgate, 2 * per * width)
    reduce[0][0].pair()
    reduce[1][0].back_rows()
    fill_grads(0, 0, shifted[0])
    unproject(0, 0)
    reduce[0][0].rows()
    reduce[1][1].back_seq()
    for m in range(1, micro):
        fill_grads(0, m, shifted[m])
        unproject(0, m)
    weight_grads(0, ulow, dproj, 0)
    reduce[0][1].pair()
    send_small(0)
    reduce[1][0].out()
    reduce[1][1].back_rows()
    reduce[0][0].seq()
    reduce[0][1].rows()
    for m in range(micro):
        take_norm(0, m)
        finish_grads(m)
        to_natural(low_s.at[m], nat.at[0, m])
        outgoing += ship(ig_out, m, 1)
    reduce[1][1].out()
    reduce[0][0].back_seq()
    reduce[0][1].seq()
    reduce[0][0].back_rows()
    reduce[0][1].back_seq()
    reduce[0][0].out()
    reduce[0][1].back_rows()
    reduce[0][1].out()

    def pick(values):
        return jnp.where(on_upper, values[1], values[0])

    totals = []
    for l in range(2):
        gather_wait(gsmall.at[l], n_all, SEM_SMALL + l)
        zero_tile = jnp.zeros(gsmall.shape[2:], F32)
        totals.append(
            lax.fori_loop(0, n_all, lambda g, acc, l=l: acc + gsmall[l, g], zero_tile)
        )
    tile_sum = pick(totals)
    wt = width // LANES
    rows_of = [to_row(tile_sum[i * wt : (i + 1) * wt]) for i in range(5)]
    dr, di, dg = rows_of[3][:, :ns], rows_of[3][:, ns:], rows_of[4]
    lam = pick([dv[l, 0:1, :] for l in range(2)])
    lr, li = lam[:, :ns], lam[:, ns:]
    by_nu = -jnp.exp(nu_ref[...]) * (lr * dr + li * di)
    by_theta = jnp.exp(theta_ref[...]) * (lr * di - li * dr)
    mean, var = rmean_ref[...], rvar_ref[...]
    for m in range(micro):
        mean = (1.0 - MOMENTUM) * mean + MOMENTUM * pick([sv[2 * l + m, 0:1, :] for l in range(2)])
        var = (1.0 - MOMENTUM) * var + MOMENTUM * pick([sv[2 * l + m, 3:4, :] for l in range(2)])
    by_bias = pick([sum(sv[2 * l + m, 5:6, :] for m in range(micro)) for l in range(2)])
    by_gain = pick([sum(sv[2 * l + m, 6:7, :] for m in range(micro)) for l in range(2)])
    blank = jnp.zeros((1, width), F32)
    small_out[...] = jnp.concatenate(
        [by_gain, by_bias]
        + rows_of[:3]
        + [jnp.concatenate([by_nu, by_theta], axis=1), dg, mean, var]
        + [blank] * 7,
        axis=0,
    )

    gather_sent(meta, n_all, SEM_META)
    for i in range(4):
        gather_sent(gst_all.at[i], n_all, SEM_STAT + i)
        gather_sent(gst_all.at[4 + i], n_all, SEM_NORM + i)
    for i in range(8):
        gather_sent(gline.at[i], n_line, SEM_LINE + i)
    for l in range(2):
        gather_sent(gsmall.at[l], n_all, SEM_SMALL + l)
    for group in reduce[1] + reduce[0]:
        group.done()
    for item in outgoing:
        item.wait()


def finish_kernel(
    act_in,
    ig_in,
    grad_in,
    small_in,
    act_out,
    ig_out,
    ggain_out,
    gbias_out,
    gb_out,
    gnu_out,
    gtheta_out,
    ggamma_out,
    gc_out,
    gskip_out,
    gglu_out,
    gglub_out,
    nmean_out,
    nvar_out,
    low,
    flat,
    small,
    flow,
    flow_sem,
    load_sem,
    store_sem,
    small_sem,
):
    small_load = pltpu.make_async_copy(small_in, small, small_sem.at[0])
    small_load.start()
    flows_in, flows_out = [], []
    for i, (source, target) in enumerate(((act_in, act_out), (ig_in, ig_out))):
        for m in range(source.shape[1]):
            k = 2 * i + m
            flows_in.append(
                pltpu.make_async_copy(source.at[0, m, 0], flow.at[k], flow_sem.at[0, k])
            )
            flows_out.append(
                pltpu.make_async_copy(flow.at[k], target.at[0, m, 0], flow_sem.at[1, k])
            )
    width, columns = gb_out.shape[1], low.shape[1]
    blocks = low.shape[0] // width
    loads, stores = [], []
    targets = [(gb_out, 0), (gb_out, 1), (gc_out, 0), (gc_out, 1)] + [(gglu_out, k) for k in range(4)]
    for k in range(blocks):
        rows = pl.ds(k * width, width)
        loads.append(pltpu.make_async_copy(grad_in.at[rows], low.at[rows], load_sem.at[k]))
        out, column = targets[k]
        stores.append(
            pltpu.make_async_copy(
                flat.at[k], out.at[0, :, pl.ds(column * columns, columns)], store_sem.at[k]
            )
        )
    for item in loads + flows_in:
        item.start()
    small_load.wait()
    ns = gnu_out.shape[1]
    ggain_out[...] = small[0:1, :]
    gbias_out[...] = small[1:2, :]
    gskip_out[...] = small[2:3, :]
    gglub_out[:, :width] = small[3:4, :]
    gglub_out[:, width:] = small[4:5, :]
    gnu_out[...] = small[5:6, :ns]
    gtheta_out[...] = small[5:6, ns:]
    ggamma_out[...] = small[6:7, :ns]
    nmean_out[...] = small[7:8, :]
    nvar_out[...] = small[8:9, :]
    for k in range(blocks):
        loads[k].wait()
        flat[k] = low[k * width : (k + 1) * width, :].astype(F32)
        stores[k].start()
    for arrived, leave in zip(flows_in, flows_out):
        arrived.wait()
        leave.start()
    for item in stores + flows_out:
        item.wait()


def on_device(n_seq, n_rows, *args):
    inputs, starts = args[0], args[2]
    micro, _, tokens, width = inputs.shape
    ns = args[9].shape[1]
    half = tokens // 2
    n_line = 2 * n_seq
    n_all = n_line * n_rows
    any_space = pl.BlockSpec(memory_space=pl.ANY)
    hbm = pl.BlockSpec(memory_space=pltpu.HBM)
    vmem = pl.BlockSpec(memory_space=pltpu.VMEM)
    in_specs = [vmem] * 16
    for i in (0, 1, 8, 12, 14):
        in_specs[i] = any_space
    flow = jax.ShapeDtypeStruct((1, micro, 1, tokens, width), BF16)
    row = lambda size: jax.ShapeDtypeStruct((1, size), F32)
    mat = lambda size: jax.ShapeDtypeStruct((1, width, size), F32)
    vf = lambda *shape: pltpu.VMEM(shape, F32)
    vb = lambda *shape: pltpu.VMEM(shape, BF16)
    dma = lambda *count: pltpu.SemaphoreType.DMA(count)
    grad_rows = 4 * width * (width // GRAD_COLS)
    own_rows = grad_rows // 2
    scratch = [
        vb(micro, half, width),
        vb(micro, half, width),
        vb(2, width, 2 * ns),
        vb(2, 2 * ns, width),
        vb(2, width, 2 * width),
        vf(2, SUB, width),
        vf(2, SUB, width),
        vb(half, half),
        vb(half, half),
        vf(micro, half, LANES),
        vf(micro, half, LANES),
        vf(micro, half, LANES),
        vf(2 * micro, half, width),
        vb(2, micro * half, width),
        vf(2 * micro, half, width),
        vf(2 * micro, half + SUB, width),
        vb(2, micro * half, width),
        vb(2, micro * half, width),
        vb(micro * half, 2 * width),
        vb(micro * half, width),
        vf(micro, half, width),
        vb(micro * half, width),
        vf(micro, half, width),
        vf(micro, half, width),
        vf(micro, half, width),
        vb(micro, half, width),
        vb(micro, half, width),
        vb(micro, half, width),
        vb(micro, half, width),
        vb(2, micro, half, width),
        vf(2 * micro, SUB, width),
        vf(2 * micro, SUB, width),
        vf(n_all, SUB, LANES),
        vf(8, n_all, SUB, LANES),
        vf(8, n_line, SUB, LANES),
        vf(2, n_all, 24, LANES),
        vb(2, grad_rows, GRAD_COLS),
        vb(2, own_rows, GRAD_COLS),
        vb(2, n_rows - 1, own_rows // n_rows, GRAD_COLS),
        vb(2, n_seq - 1, max(32, own_rows // n_rows // n_seq), GRAD_COLS),
        vb(2, own_rows, GRAD_COLS),
        dma(7),
        dma(4),
        dma(4),
        dma(19),
        dma(19),
        dma(4),
        dma(4),
        dma(4),
        dma(20),
        dma(20),
        dma(3, 4),
    ]
    act, ig, grads, small = pl.pallas_call(
        functools.partial(step_kernel, n_seq, n_rows),
        out_shape=(
            flow,
            flow,
            jax.ShapeDtypeStruct((grad_rows, GRAD_COLS), BF16),
            jax.ShapeDtypeStruct((16, width), F32),
        ),
        in_specs=in_specs,
        out_specs=[any_space, any_space, any_space, vmem],
        scratch_shapes=scratch,
        compiler_params=pltpu.CompilerParams(
            collective_id=0, has_side_effects=True, vmem_limit_bytes=63 * 2**20
        ),
        name="lru_blocks",
    )(*args)
    return pl.pallas_call(
        finish_kernel,
        out_shape=(
            flow,
            flow,
            row(width),
            row(width),
            mat(2 * ns),
            row(ns),
            row(ns),
            row(ns),
            mat(width),
            row(width),
            mat(2 * width),
            row(2 * width),
            row(width),
            row(width),
        ),
        in_specs=[hbm, hbm, hbm, hbm],
        out_specs=[any_space if i in (0, 1, 4, 8, 10) else vmem for i in range(14)],
        scratch_shapes=[
            vb(grad_rows, GRAD_COLS),
            vf(grad_rows // width, width, GRAD_COLS),
            vf(16, width),
            vb(2 * micro, tokens, width),
            dma(2, 4),
            dma(grad_rows // width),
            dma(grad_rows // width),
            dma(1),
        ],
        compiler_params=pltpu.CompilerParams(vmem_limit_bytes=62 * 2**20),
        name="write_results",
    )(act, ig, grads, small)


def solution(mesh):
    placed = (
        P(None, "rows", "seq", None),
        P(None, "rows", "seq", None),
        P(None, "rows", "seq"),
        P(None, "rows", "seq"),
        P("section", None),
        P("section", None),
        P("section", None),
        P("section", None),
        P("section", None, None),
        P("section", None),
        P("section", None),
        P("section", None),
        P("section", None, None),
        P("section", None),
        P("section", None, None),
        P("section", None),
    )
    return jax.shard_map(
        functools.partial(on_device, mesh.shape["seq"], mesh.shape["rows"]),
        mesh=mesh,
        in_specs=placed,
        out_specs=(
            P("section", None, "rows", "seq", None),
            P("section", None, "rows", "seq", None),
            P("section", None),
            P("section", None),
            P("section", None, None),
            P("section", None),
            P("section", None),
            P("section", None),
            P("section", None, None),
            P("section", None),
            P("section", None, None),
            P("section", None),
            P("section", None),
            P("section", None),
        ),
        check_vma=False,
    )
```

```python
import functools
import math

import jax
import jax.numpy as jnp
from jax import lax
from jax.experimental import pallas as pl
from jax.experimental.pallas import tpu as pltpu
from jax.sharding import PartitionSpec as P

NORM_EPS = 1e-05
MOMENTUM = 0.1
GELU_C = math.sqrt(2.0 / math.pi)
GELU_K = 0.044715
MESH = pl.DeviceIdType.MESH
F32 = jnp.float32
BF16 = jnp.bfloat16
SUB = 8
LANES = 128
GRAD_COLS = 256


def dot_nn(a, b):
    return lax.dot_general(a, b, (((1,), (0,)), ((), ())), preferred_element_type=F32)


def dot_nt(a, b):
    return lax.dot_general(a, b, (((1,), (1,)), ((), ())), preferred_element_type=F32)


def dot_tn(a, b):
    return lax.dot_general(a, b, (((0,), (0,)), ((), ())), preferred_element_type=F32)


def wide(mask, times):
    return jnp.concatenate([mask] * times, axis=1)


def to_tile(row):
    return jnp.concatenate(
        [row[:, i * LANES : (i + 1) * LANES] for i in range(row.shape[1] // LANES)], axis=0
    )


def to_row(tile):
    return jnp.concatenate([tile[i : i + 1, :] for i in range(tile.shape[0])], axis=1)


def cmul(ar, ai, br, bi):
    return ar * br - ai * bi, ar * bi + ai * br


def cpow(re, im, count):
    out = None
    while count:
        if count % 2:
            out = (re, im) if out is None else cmul(out[0], out[1], re, im)
        count //= 2
        if count:
            re, im = cmul(re, im, re, im)
    return out


def fold_rows(value):
    return jnp.sum(value.reshape(value.shape[0] // SUB, SUB, value.shape[1]), axis=0)


def step_kernel(
    n_seq,
    n_rows,
    x_hbm,
    cot_hbm,
    starts_ref,
    valid_ref,
    gain_ref,
    bias_ref,
    rmean_ref,
    rvar_ref,
    b_hbm,
    nu_ref,
    theta_ref,
    gamma_ref,
    c_hbm,
    skip_ref,
    glu_hbm,
    glub_ref,
    act_out,
    ig_out,
    grad_out,
    small_out,
    nat,
    wb,
    wc,
    wg,
    pv,
    dv,
    perm,
    perm_t,
    keep_a,
    keep_d,
    live,
    hid,
    ulow,
    drive,
    state,
    slow,
    alow,
    dgate,
    dread,
    gst,
    dproj,
    dmix,
    dunit,
    dout,
    sig_s,
    gat_s,
    dgelu_s,
    low_s,
    sv,
    sm,
    meta,
    gst_all,
    gline,
    small_own,
    small_other,
    small_by_row,
    small_by_seq,
    gbuf,
    pair_buf,
    rows_buf,
    seq_buf,
    gfin,
    in_sem,
    wsend_sem,
    wrecv_sem,
    gs_sem,
    gr_sem,
    out_sem,
    osend_sem,
    orecv_sem,
    rs_sem,
    rr_sem,
    gout_sem,
    ss_sem,
    sr_sem,
):
    micro = x_hbm.shape[0]
    tokens = x_hbm.shape[2]
    half = tokens // 2
    seg = half // SUB
    width = x_hbm.shape[3]
    ns = nu_ref.shape[1]
    n_line = 2 * n_seq
    n_all = n_line * n_rows
    chunk = min(512, half)
    n_chunk = half // chunk

    s = lax.axis_index("section")
    q = lax.axis_index("seq")
    r = lax.axis_index("rows")
    rank = q * 2 + s
    me = rank * n_rows + r
    partner = (1 - s, q, r)

    def peer_all(d):
        g = me ^ d
        k = g // n_rows
        return (k % 2, k // 2, g % n_rows)

    def peer_line(d):
        k = rank ^ d
        return (k % 2, k // 2, r)

    def gather_start(buf, mine, count, peer, sem):
        def one(d, carry):
            pltpu.make_async_remote_copy(
                src_ref=buf.at[mine],
                dst_ref=buf.at[mine],
                send_sem=gs_sem.at[sem],
                recv_sem=gr_sem.at[sem],
                device_id=peer(d),
                device_id_type=MESH,
            ).start()
            return carry

        lax.fori_loop(1, count, one, 0, unroll=count <= 32)

    def gather_wait(buf, count, sem):
        part = buf.at[pl.ds(0, count - 1)]
        pltpu.make_async_copy(part, part, gr_sem.at[sem]).wait()

    def gather_sent(buf, count, sem):
        part = buf.at[pl.ds(0, count - 1)]
        pltpu.make_async_copy(part, part, gs_sem.at[sem]).wait()

    barrier = pltpu.get_barrier_semaphore()

    def greet(d, carry):
        pl.semaphore_signal(barrier, inc=1, device_id=peer_all(d), device_id_type=MESH)
        return carry

    lax.fori_loop(1, n_all, greet, 0)

    start_at = pl.multiple_of(s * half, half)
    my_tokens = pl.ds(start_at, half)
    loads = []
    for m in range(micro):
        loads.append(
            pltpu.make_async_copy(x_hbm.at[m, 0, my_tokens], nat.at[0, m], in_sem.at[m])
        )
    own_w = [
        pltpu.make_async_copy(b_hbm.at[0], wb.at[s], in_sem.at[4]),
        pltpu.make_async_copy(c_hbm.at[0], wc.at[s], in_sem.at[5]),
        pltpu.make_async_copy(glu_hbm.at[0], wg.at[s], in_sem.at[6]),
    ]
    cot_loads = [
        pltpu.make_async_copy(cot_hbm.at[m, 0, my_tokens], nat.at[1, m], in_sem.at[2 + m])
        for m in range(micro)
    ]
    for item in loads + own_w + cot_loads:
        item.start()

    pv[s, 0:1, :] = gain_ref[...]
    pv[s, 1:2, :] = bias_ref[...]
    pv[s, 2:3, :] = skip_ref[...]
    pv[s, 3:4, :] = glub_ref[:, :width]
    pv[s, 4:5, :] = glub_ref[:, width:]
    pv[s, 5:6, :] = jnp.concatenate([nu_ref[...], theta_ref[...]], axis=1)
    pv[s, 6:7, :] = jnp.concatenate([gamma_ref[...], gamma_ref[...]], axis=1)
    pv[s, 7:8, :] = jnp.zeros((1, width), F32)

    here = lax.broadcasted_iota(jnp.int32, (half, half), 0)
    there = lax.broadcasted_iota(jnp.int32, (half, half), 1)
    perm[...] = jnp.where((here % SUB) * seg + here // SUB == there, 1.0, 0.0).astype(BF16)
    perm_t[...] = jnp.where((there % SUB) * seg + there // SUB == here, 1.0, 0.0).astype(BF16)

    st_all = starts_ref[:, 0, :].astype(F32)
    va_all = valid_ref[:, 0, :].astype(F32)
    nx_all = pltpu.roll(st_all, tokens - 1, 1)
    on_upper = s == 1
    st_half = jnp.where(on_upper, st_all[:, half:], st_all[:, :half])
    va_half = jnp.where(on_upper, va_all[:, half:], va_all[:, :half])
    nx_half = jnp.where(on_upper, nx_all[:, half:], nx_all[:, :half])
    place = lax.broadcasted_iota(jnp.int32, (micro, half), 1)
    nx_half = jnp.where(place == half - 1, 0.0, nx_half)
    counts = []
    for m in range(micro):
        stacked = jnp.concatenate(
            [
                jnp.broadcast_to(1.0 - st_half[m : m + 1], (LANES, half)),
                jnp.broadcast_to(1.0 - nx_half[m : m + 1], (LANES, half)),
                jnp.broadcast_to(va_half[m : m + 1], (LANES, half)),
            ],
            axis=0,
        ).astype(BF16)
        spread = dot_nt(perm[...], stacked)
        keep_a[m] = spread[:, :LANES]
        keep_d[m] = spread[:, LANES : 2 * LANES]
        live[m] = spread[:, 2 * LANES :]
        counts.append(jnp.sum(va_half[m : m + 1], axis=1, keepdims=True))
    rows_low = lax.broadcasted_iota(jnp.int32, (SUB, LANES), 0) < 4
    meta[me] = jnp.where(
        rows_low,
        jnp.broadcast_to(counts[0], (SUB, LANES)),
        jnp.broadcast_to(counts[micro - 1], (SUB, LANES)),
    )

    def share(source, target, index):
        return pltpu.make_async_remote_copy(
            src_ref=source,
            dst_ref=target,
            send_sem=wsend_sem.at[index],
            recv_sem=wrecv_sem.at[index],
            device_id=partner,
            device_id_type=MESH,
        )

    shares = [
        share(pv.at[s], pv.at[s], 0),
        share(b_hbm.at[0], wb.at[s], 1),
        share(c_hbm.at[0], wc.at[s], 2),
        share(glu_hbm.at[0], wg.at[s], 3),
    ]
    SEM_META, SEM_STAT, SEM_NORM, SEM_LINE = 0, 1, 5, 9

    def chunks(body, init):
        return lax.fori_loop(0, n_chunk, lambda c, acc: body(pl.multiple_of(c * chunk, chunk), acc), init)

    zero_sum = jnp.zeros((SUB, width), F32)

    def enter(m):
        def body(at, acc):
            rows = pl.ds(at, chunk)
            value = dot_nn(perm[rows, :], nat[0, m])
            hid[m, rows, :] = value
            return acc + fold_rows(value * wide(live[m, rows, :], width // LANES))

        return chunks(body, zero_sum)

    def stats_of(l, m, total):
        mean = jnp.sum(total, axis=0, keepdims=True) / jnp.maximum(counts[m], 1.0)

        def body(at, acc):
            rows = pl.ds(at, chunk)
            off = hid[2 * l + m, rows, :] - mean
            return acc + fold_rows(off * off * wide(live[m, rows, :], width // LANES))

        spread = jnp.sum(chunks(body, zero_sum), axis=0, keepdims=True)
        gst_all[2 * l + m, me] = jnp.concatenate([to_tile(mean), to_tile(spread)], axis=0)

    def send_stats(l, m):
        gather_start(gst_all.at[2 * l + m], me, n_all, peer_all, SEM_STAT + 2 * l + m)

    def take_stats(l, m):
        buf = gst_all.at[2 * l + m]
        gather_wait(buf, n_all, SEM_STAT + 2 * l + m)
        data = buf[...]
        count = meta[:, 4 * m : 4 * m + 1, :] if micro == 2 else meta[:, 0:1, :]
        total = jnp.sum(count, axis=0)
        low4 = lax.broadcasted_iota(jnp.int32, (1, SUB, LANES), 1) < 4
        weighted = jnp.sum(data * jnp.where(low4, count, 1.0), axis=0)
        mean = weighted[0:4] / total
        apart = data[:, 0:4, :] - mean[None]
        var = (weighted[4:8] + jnp.sum(count * apart * apart, axis=0)) / total
        mean_row, var_row = to_row(mean), to_row(var)
        scale = lax.rsqrt(var_row + NORM_EPS)
        box = sv.at[2 * l + m]
        box[0:1, :] = mean_row
        box[1:2, :] = scale
        box[2:3, :] = scale * pv[l, 0:1, :]
        box[3:4, :] = var_row
        box[4:5, :] = jnp.broadcast_to(total[:, 0:1], (1, width))

    def unit_of(l, m, rows):
        box = sv.at[2 * l + m]
        return (hid[2 * l + m, rows, :] - box[0:1, :]) * box[2:3, :] + pv[l, 1:2, :]

    def lam_rows(l, which, conj):
        re = dv[l, which : which + 1, :ns]
        im = dv[l, which : which + 1, ns:]
        return re, (-im if conj else im)

    unroll = min(8, seg)

    def scan_local(u_ref, keep_ref, l, desc, conj):
        lr, li = lam_rows(l, 0, conj)
        lr = jnp.broadcast_to(lr, (SUB, ns))
        li = jnp.broadcast_to(li, (SUB, ns))

        def body(jj, carry):
            re, im = carry
            for t in range(unroll):
                j = jj * unroll + t
                if desc:
                    j = seg - 1 - j
                rows = pl.ds(pl.multiple_of(j * SUB, SUB), SUB)
                keep = wide(keep_ref[rows, :], ns // LANES)
                u = u_ref[rows, :]
                kr, ki = keep * re, keep * im
                re = lr * kr - li * ki + u[:, :ns]
                im = lr * ki + li * kr + u[:, ns:]
            return re, im

        zero = jnp.zeros((SUB, ns), F32)
        return lax.fori_loop(0, seg // unroll, body, (zero, zero))

    spot = lambda: lax.broadcasted_iota(jnp.int32, (SUB, ns), 0)

    def before(value, step, desc, blank):
        if desc:
            return jnp.where(spot() < SUB - step, pltpu.roll(value, SUB - step, 0), blank)
        return jnp.where(spot() >= step, pltpu.roll(value, step, 0), blank)

    def join_segments(er, ei, keep_ref, l, desc, conj):
        shut = jnp.min(keep_ref[...].reshape(seg, SUB, LANES), axis=0)
        lr, li = lam_rows(l, 1, conj)
        ar, ai = lr * wide(shut, ns // LANES), li * wide(shut, ns // LANES)
        for step in (1, 2, 4):
            pr, pi = cmul(ar, ai, before(er, step, desc, 0.0), before(ei, step, desc, 0.0))
            er, ei = er + pr, ei + pi
            ar, ai = cmul(ar, ai, before(ar, step, desc, 1.0), before(ai, step, desc, 0.0))
        last = 0 if desc else SUB - 1
        out = (er[last : last + 1], ei[last : last + 1], jnp.min(shut, axis=0, keepdims=True))
        shifted = (
            before(er, 1, desc, 0.0),
            before(ei, 1, desc, 0.0),
            before(ar, 1, desc, 1.0),
            before(ai, 1, desc, 0.0),
        )
        return out, shifted

    def send_carry(phase, l, m, u_ref, desc, conj):
        keep_ref = keep_d.at[m] if desc else keep_a.at[m]
        er, ei = scan_local(u_ref, keep_ref, l, desc, conj)
        (tr, ti, shut), shifted = join_segments(er, ei, keep_ref, l, desc, conj)
        if desc:
            first = keep_a[m, 0:1, :]
            tr, ti, shut = tr * wide(first, ns // LANES), ti * wide(first, ns // LANES), shut * first
        index = phase * 4 + 2 * l + m
        buf = gline.at[index]
        buf[rank] = jnp.concatenate(
            [
                to_tile(tr),
                to_tile(ti),
                shut,
                jnp.zeros((SUB - 2 * ns // LANES - 1, LANES), F32),
            ],
            axis=0,
        )
        gather_start(buf, rank, n_line, peer_line, SEM_LINE + index)
        return shifted

    def take_carry(phase, l, m, shifted, desc, conj):
        index = phase * 4 + 2 * l + m
        buf = gline.at[index]
        gather_wait(buf, n_line, SEM_LINE + index)
        lr, li = lam_rows(l, 2, conj)
        tiles = ns // LANES

        def body(step, carry):
            cr, ci = carry
            k = n_line - 1 - step if desc else step
            box = buf[k]
            shut = wide(box[2 * tiles : 2 * tiles + 1], tiles)
            pr, pi = cmul(lr * shut, li * shut, cr, ci)
            pr = pr + to_row(box[:tiles])
            pi = pi + to_row(box[tiles : 2 * tiles])
            use = k > rank if desc else k < rank
            return jnp.where(use, pr, cr), jnp.where(use, pi, ci)

        zero = jnp.zeros((1, ns), F32)
        cr, ci = lax.fori_loop(0, n_line, body, (zero, zero))
        er, ei, ar, ai = shifted
        pr, pi = cmul(ar, ai, cr, ci)
        return er + pr, ei + pi

    def fill_states(l, m, shifted):
        desc = l == 1
        re, im = take_carry(0, l, m, shifted, desc, False)
        keep_ref = keep_d.at[m] if desc else keep_a.at[m]
        u_ref, s_ref = drive.at[2 * l + m], state.at[2 * l + m]
        lr, li = lam_rows(l, 0, False)
        lr = jnp.broadcast_to(lr, (SUB, ns))
        li = jnp.broadcast_to(li, (SUB, ns))
        s_ref[pl.ds(half if desc else 0, SUB), :] = jnp.concatenate([re, im], axis=1)

        def body(jj, carry):
            re, im = carry
            for t in range(unroll):
                j = jj * unroll + t
                if desc:
                    j = seg - 1 - j
                at = pl.multiple_of(j * SUB, SUB)
                rows = pl.ds(at, SUB)
                keep = wide(keep_ref[rows, :], ns // LANES)
                u = u_ref[rows, :]
                kr, ki = keep * re, keep * im
                re = lr * kr - li * ki + u[:, :ns]
                im = lr * ki + li * kr + u[:, ns:]
                to = rows if desc else pl.ds(at + SUB, SUB)
                s_ref[to, :] = jnp.concatenate([re, im], axis=1)
            return re, im

        lax.fori_loop(0, seg // unroll, body, (re, im))

    def fill_grads(l, m, shifted):
        desc = l == 0
        re, im = take_carry(1, l, m, shifted, desc, True)
        keep_ref = keep_d.at[m] if desc else keep_a.at[m]
        pkeep_ref = keep_a.at[m] if desc else keep_d.at[m]
        u_ref, s_ref, g_ref = drive.at[2 * l + m], state.at[2 * l + m], gst.at[m]
        lr, li = lam_rows(l, 0, True)
        lr = jnp.broadcast_to(lr, (SUB, ns))
        li = jnp.broadcast_to(li, (SUB, ns))
        zero = jnp.zeros((SUB, ns), F32)

        def body(jj, carry):
            re, im, dr, di, dg = carry
            for t in range(unroll):
                j = jj * unroll + t
                if desc:
                    j = seg - 1 - j
                at = pl.multiple_of(j * SUB, SUB)
                rows = pl.ds(at, SUB)
                keep = wide(keep_ref[rows, :], ns // LANES)
                g = g_ref[rows, :]
                kr, ki = keep * re, keep * im
                re = lr * kr - li * ki + g[:, :ns]
                im = lr * ki + li * kr + g[:, ns:]
                g_ref[rows, :] = jnp.concatenate([re, im], axis=1)
                u = u_ref[rows, :]
                dg = dg + (re * u[:, :ns] + im * u[:, ns:])
                old = s_ref[rows if desc else pl.ds(at + SUB, SUB), :]
                pkeep = wide(pkeep_ref[rows, :], ns // LANES)
                pr, pi = pkeep * old[:, :ns], pkeep * old[:, ns:]
                dr = dr + (pr * re + pi * im)
                di = di + (pr * im - pi * re)
            return re, im, dr, di, dg

        _, _, dr, di, dg = lax.fori_loop(0, seg // unroll, body, (re, im, zero, zero, zero))
        box = sm.at[2 * l + m]
        box[3:4, :] = jnp.sum(jnp.concatenate([dr, di], axis=1), axis=0, keepdims=True)
        box[4:5, :] = jnp.sum(jnp.concatenate([dg, dg], axis=1), axis=0, keepdims=True)

    def project(l, m):
        gamma2 = dv[l, 3:4, :]

        def body(at, acc):
            rows = pl.ds(at, chunk)
            low = unit_of(l, m, rows).astype(BF16)
            ulow[l, pl.ds(m * half + at, chunk), :] = low
            drive[2 * l + m, rows, :] = dot_nn(low, wb[l]) * gamma2
            return acc

        chunks(body, 0)
        return send_carry(0, l, m, drive.at[2 * l + m], l == 1, False)

    def mix(l, m, at):
        rows = pl.ds(at, chunk)
        big = pl.ds(m * half + at, chunk)
        low = state[2 * l + m, pl.ds(at + (0 if l == 1 else SUB), chunk), :].astype(BF16)
        slow[l, big, :] = low
        unit = unit_of(l, m, rows)
        mixed = dot_nn(low, wc[l]) + pv[l, 2:3, :] * unit
        square = mixed * mixed
        t = jnp.tanh((GELU_C * mixed) * (1.0 + GELU_K * square))
        half_up = 0.5 * (1.0 + t)
        act = (mixed * half_up).astype(BF16)
        alow[l, big, :] = act
        slope = half_up + (0.5 * GELU_C) * mixed * (1.0 - t * t) * (1.0 + (3.0 * GELU_K) * square)
        gates = dot_nn(act, wg[l])
        value = gates[:, :width] + pv[l, 3:4, :]
        gate = 0.5 * jnp.tanh(0.5 * (gates[:, width:] + pv[l, 4:5, :])) + 0.5
        branch = value * gate
        return unit, slope, gate, branch, (hid[2 * l + m, rows, :] + branch).astype(BF16)

    def finish_lower(m):
        def body(at, acc):
            rows = pl.ds(at, chunk)
            unit, slope, gate, branch, low = mix(0, m, at)
            sig_s[m, rows, :] = gate.astype(BF16)
            gat_s[m, rows, :] = (branch * (1.0 - gate)).astype(BF16)
            dgelu_s[m, rows, :] = slope.astype(BF16)
            low_s[m, rows, :] = low
            value = low.astype(F32)
            hid[2 + m, rows, :] = value
            return acc + fold_rows(value * wide(live[m, rows, :], width // LANES))

        return chunks(body, zero_sum)

    def to_natural(low_ref, nat_ref):
        def body(at, acc):
            rows = pl.ds(at, chunk)
            nat_ref[rows, :] = dot_nn(perm_t[rows, :], low_ref[...]).astype(BF16)
            return acc

        chunks(body, 0)

    def ship(out, m, tag):
        base = tag * 2 + m
        local = pltpu.make_async_copy(
            nat.at[s, m], out.at[0, m, 0, my_tokens], out_sem.at[base]
        )
        remote = pltpu.make_async_remote_copy(
            src_ref=nat.at[1 - s, m],
            dst_ref=out.at[0, m, 0, my_tokens],
            send_sem=osend_sem.at[base],
            recv_sem=orecv_sem.at[base],
            device_id=partner,
            device_id_type=MESH,
        )
        local.start()
        remote.start()
        return local, remote

    def gate_grads(l, m, at, unit, slope, gate, other, grad, acc):
        rows = pl.ds(at, chunk)
        big = pl.ds(m * half + at, chunk)
        d_gates = jnp.concatenate([grad * gate, grad * other], axis=1).astype(BF16)
        dgate[big, :] = d_gates
        d_mixed = dot_nt(d_gates, wg[l]) * slope
        dmix[m, rows, :] = d_mixed
        d_read = d_mixed.astype(BF16)
        dread[big, :] = d_read
        gst[m, rows, :] = dot_nt(d_read, wc[l])
        return acc[0] + fold_rows(d_gates.astype(F32)), acc[1] + fold_rows(d_mixed * unit)

    gate_zero = (jnp.zeros((SUB, 2 * width), F32), zero_sum)

    def keep_gate_sums(l, m, acc):
        box = sm.at[2 * l + m]
        box[0:1, :] = jnp.sum(acc[1], axis=0, keepdims=True)
        both = jnp.sum(acc[0], axis=0, keepdims=True)
        box[1:2, :] = both[:, :width]
        box[2:3, :] = both[:, width:]

    def turn_upper(m):
        def body(at, acc):
            rows = pl.ds(at, chunk)
            unit, slope, gate, branch, low = mix(1, m, at)
            low_s[m, rows, :] = low
            grad = dot_nn(perm[rows, :], nat[1, m])
            dout[m, rows, :] = grad.astype(BF16)
            return gate_grads(1, m, at, unit, slope, gate, branch * (1.0 - gate), grad, acc)

        keep_gate_sums(1, m, chunks(body, gate_zero))
        return send_carry(1, 1, m, gst.at[m], False, True)

    def unproject(l, m):
        gamma2 = dv[l, 3:4, :]

        def body(at, acc):
            rows = pl.ds(at, chunk)
            low = (gst[m, rows, :] * gamma2).astype(BF16)
            dproj[pl.ds(m * half + at, chunk), :] = low
            value = dmix[m, rows, :] * pv[l, 2:3, :] + dot_nt(low, wb[l])
            dunit[m, rows, :] = value
            normed = (hid[2 * l + m, rows, :] - sv[2 * l + m, 0:1, :]) * sv[2 * l + m, 1:2, :]
            return acc[0] + fold_rows(value), acc[1] + fold_rows(value * normed)

        by_bias, by_gain = chunks(body, (zero_sum, zero_sum))
        buf = gst_all.at[4 + 2 * l + m]
        buf[me] = jnp.concatenate(
            [
                to_tile(jnp.sum(by_bias, axis=0, keepdims=True)),
                to_tile(jnp.sum(by_gain, axis=0, keepdims=True)),
            ],
            axis=0,
        )
        gather_start(buf, me, n_all, peer_all, SEM_NORM + 2 * l + m)

    def take_norm(l, m):
        buf = gst_all.at[4 + 2 * l + m]
        gather_wait(buf, n_all, SEM_NORM + 2 * l + m)
        both = jnp.sum(buf[...], axis=0)
        box = sv.at[2 * l + m]
        box[5:6, :] = to_row(both[0:4])
        box[6:7, :] = to_row(both[4:8])

    def input_grads(l, m, rows):
        box = sv.at[2 * l + m]
        share_of = 1.0 / box[4:5, :]
        by_bias = box[2:3, :] * box[5:6, :] * share_of
        by_gain = box[2:3, :] * box[6:7, :] * share_of
        normed = (hid[2 * l + m, rows, :] - box[0:1, :]) * box[1:2, :]
        mask = wide(live[m, rows, :], width // LANES)
        return (
            dout[m, rows, :].astype(F32)
            + dunit[m, rows, :] * box[2:3, :]
            - mask * (by_bias + normed * by_gain)
        ).astype(BF16)

    def turn_lower(m):
        def body(at, acc):
            rows = pl.ds(at, chunk)
            low = input_grads(1, m, rows)
            low_s[m, rows, :] = low
            grad = low.astype(F32)
            dout[m, rows, :] = low
            return gate_grads(
                0,
                m,
                at,
                unit_of(0, m, rows),
                dgelu_s[m, rows, :].astype(F32),
                sig_s[m, rows, :].astype(F32),
                gat_s[m, rows, :].astype(F32),
                grad,
                acc,
            )

        keep_gate_sums(0, m, chunks(body, gate_zero))
        return send_carry(1, 0, m, gst.at[m], True, True)

    def finish_grads(m):
        def body(at, acc):
            rows = pl.ds(at, chunk)
            low_s[m, rows, :] = input_grads(0, m, rows)
            return acc

        chunks(body, 0)

    part = 256

    def weight_grads(l, left, right, row_at):
        blocks = right.shape[1] // GRAD_COLS

        def body(c, acc):
            at = pl.multiple_of(c * part, part)
            for k in range(blocks):
                columns = pl.ds(k * GRAD_COLS, GRAD_COLS)
                value = dot_tn(left[l, :, pl.ds(at, part)], right[:, columns])
                to = pl.multiple_of(row_at + k * width + at, part)
                gbuf[l, pl.ds(to, part), :] = value.astype(BF16)
            return acc

        lax.fori_loop(0, width // part, body, 0)

    per = width // GRAD_COLS
    n_group = 4

    class Reduce:
        def __init__(self, l, g):
            count = per * width
            self.l, self.base = l, g * count
            self.mine = count // 2
            self.at = g * self.mine
            self.n1 = self.mine // n_rows
            self.n2 = max(16, self.n1 // n_seq)
            self.owners = self.n1 // self.n2
            self.at1 = g * self.n1
            self.at2 = g * self.n2
            self.sem = (n_group * l + g) * 5

        def send(self, source, target, sem, where):
            return pltpu.make_async_remote_copy(
                src_ref=source,
                dst_ref=target,
                send_sem=rs_sem.at[self.sem + sem],
                recv_sem=rr_sem.at[self.sem + sem],
                device_id=where,
                device_id_type=MESH,
            )

        def await_rows(self, count, sem, sems=None):
            ref = gbuf.at[0, pl.ds(0, count)]
            pltpu.make_async_copy(ref, ref, (rr_sem if sems is None else sems).at[self.sem + sem]).wait()

        def half_of(self, core):
            return gbuf.at[self.l, pl.ds(pl.multiple_of(self.base + core * self.mine, 16), self.mine)]

        def total(self):
            return pair_buf.at[self.l, pl.ds(self.at, self.mine)]

        def piece(self, ref, index, size):
            return ref.at[pl.ds(pl.multiple_of(index * size, 16), size)]

        def pair(self):
            self.send(self.half_of(1 - s), self.total(), 0, partner).start()

        def rows(self):
            self.await_rows(self.mine, 0)
            own, total = self.half_of(s), self.total()
            total[...] = (own[...].astype(F32) + total[...].astype(F32)).astype(BF16)
            into = rows_buf.at[self.l, :, pl.ds(self.at1, self.n1)]
            for d in range(1, n_rows):
                to = r ^ d
                self.send(self.piece(total, to, self.n1), into.at[d - 1], 1, (s, q, to)).start()

        def seq(self):
            self.await_rows((n_rows - 1) * self.n1, 1)
            total = self.piece(self.total(), r, self.n1)
            value = total[...].astype(F32)
            for d in range(n_rows - 1):
                value = value + rows_buf[self.l, d, pl.ds(self.at1, self.n1), :].astype(F32)
            total[...] = value.astype(BF16)
            into = seq_buf.at[self.l, :, pl.ds(self.at2, self.n2)]

            def one(d, acc):
                to = q ^ d

                def go():
                    self.send(self.piece(total, to, self.n2), into.at[d - 1], 2, (s, to, r)).start()

                self.when(to < self.owners, go)
                return acc

            lax.fori_loop(1, n_seq, one, 0, unroll=n_seq <= 4)

        def when(self, condition, go):
            if self.owners == n_seq:
                go()
            else:
                pl.when(condition)(go)

        def block(self):
            return gfin.at[self.l, pl.ds(self.at1, self.n1)]

        def back_seq(self):
            total = self.piece(self.total(), r, self.n1)
            mine = self.piece(self.block(), q, self.n2)

            def go():
                self.await_rows((n_seq - 1) * self.n2, 2)
                value = self.piece(total, q, self.n2)[...].astype(F32)
                for d in range(n_seq - 1):
                    value = value + seq_buf[self.l, d, pl.ds(self.at2, self.n2), :].astype(F32)
                mine[...] = value.astype(BF16)

                def one(d, acc):
                    self.send(mine, mine, 3, (s, q ^ d, r)).start()
                    return acc

                lax.fori_loop(1, n_seq, one, 0, unroll=n_seq <= 4)

            self.when(q < self.owners, go)

        def result(self):
            at = self.base + s * self.mine + r * self.n1
            return grad_out.at[pl.ds(pl.multiple_of(at, 16), self.n1)]

        def keep_own(self):
            return pltpu.make_async_copy(self.block(), self.result(), gout_sem.at[self.sem // 5])

        def back_rows(self):
            self.when(q < self.owners, lambda: self.await_rows((self.owners - 1) * self.n2, 3))
            if self.owners < n_seq:
                self.when(q >= self.owners, lambda: self.await_rows(self.owners * self.n2, 3))
            pl.when(s == self.l)(lambda: self.keep_own().start())
            pl.when(s != self.l)(lambda: self.send(self.block(), self.result(), 4, partner).start())
            for d in range(1, n_rows):
                self.send(self.block(), self.result(), 4, (self.l, q, r ^ d)).start()

        def done(self):
            def settle():
                self.keep_own().wait()
                self.await_rows((2 * n_rows - 1) * self.n1, 4)
                self.await_rows((n_rows - 1) * self.n1, 4, rs_sem)

            pl.when(s == self.l)(settle)
            pl.when(s != self.l)(lambda: self.await_rows(n_rows * self.n1, 4, rs_sem))
            self.await_rows(self.mine, 0, rs_sem)
            self.await_rows((n_rows - 1) * self.n1, 1, rs_sem)
            self.when(q < self.owners, lambda: self.await_rows((self.owners - 1) * self.n2, 2, rs_sem))
            if self.owners < n_seq:
                self.when(q >= self.owners, lambda: self.await_rows(self.owners * self.n2, 2, rs_sem))
            self.when(q < self.owners, lambda: self.await_rows((n_seq - 1) * self.n2, 3, rs_sem))

    reduce = [[Reduce(l, g) for g in range(n_group)] for l in range(2)]
    B, C, GA, GB = range(n_group)

    def run(*plan):
        for l, g, step in plan:
            getattr(reduce[l][g], step)()

    def small_copy(source, target, sem, where):
        return pltpu.make_async_remote_copy(
            src_ref=source,
            dst_ref=target,
            send_sem=ss_sem.at[sem],
            recv_sem=sr_sem.at[sem],
            device_id=where,
            device_id_type=MESH,
        )

    def small_await(ref, sems, sem):
        pltpu.make_async_copy(ref, ref, sems.at[sem]).wait()

    def small_pair():
        for l in range(2):
            both = sm[2 * l]
            for m in range(1, micro):
                both = both + sm[2 * l + m]
            small_own[l] = jnp.concatenate(
                [to_tile(both[i : i + 1]) for i in range(5)] + [jnp.zeros((4, LANES), F32)], axis=0
            )
        small_copy(small_own.at[1 - s], small_other, 0, partner).start()

    def small_rows():
        small_await(small_other, sr_sem, 0)
        first, second = small_own[s], small_other[...]
        small_by_row[r] = first + second
        for d in range(1, n_rows):
            small_copy(small_by_row.at[r], small_by_row.at[r], 1, (s, q, r ^ d)).start()

    def small_seq():
        small_await(small_by_row.at[pl.ds(0, n_rows - 1)], sr_sem, 1)
        total = small_by_row[0]
        for k in range(1, n_rows):
            total = total + small_by_row[k]
        small_by_seq[q] = total

        def one(d, acc):
            small_copy(small_by_seq.at[q], small_by_seq.at[q], 2, (s, q ^ d, r)).start()
            return acc

        lax.fori_loop(1, n_seq, one, 0)

    def small_total():
        small_await(small_by_seq.at[pl.ds(0, n_seq - 1)], sr_sem, 2)
        return jnp.sum(small_by_seq[...], axis=0)

    def small_done():
        small_await(small_other, ss_sem, 0)
        small_await(small_by_row.at[pl.ds(0, n_rows - 1)], ss_sem, 1)
        small_await(small_by_seq.at[pl.ds(0, n_seq - 1)], ss_sem, 2)

    for m in range(micro):
        loads[m].wait()
        stats_of(0, m, enter(m))
    pl.semaphore_wait(barrier, n_all - 1)
    gather_start(meta, me, n_all, peer_all, SEM_META)
    for m in range(micro):
        send_stats(0, m)
    for item in shares:
        item.start()
    for item in own_w:
        item.wait()
    for item in shares:
        item.wait()
    for l in range(2):
        decay = jnp.exp(-jnp.exp(pv[l, 5:6, :ns]))
        phase = jnp.exp(pv[l, 5:6, ns:])
        re, im = decay * jnp.cos(phase), decay * jnp.sin(phase)
        dv[l, 0:1, :] = jnp.concatenate([re, im], axis=1)
        dv[l, 1:2, :] = jnp.concatenate(cpow(re, im, seg), axis=1)
        dv[l, 2:3, :] = jnp.concatenate(cpow(re, im, half), axis=1)
        dv[l, 3:4, :] = jnp.exp(pv[l, 6:7, :])
    gather_wait(meta, n_all, SEM_META)

    shifted = {}
    for m in range(micro):
        take_stats(0, m)
        shifted[m] = project(0, m)
    for m in range(micro):
        fill_states(0, m, shifted[m])
        stats_of(1, m, finish_lower(m))
        send_stats(1, m)
        to_natural(low_s.at[m], nat.at[0, m])
    for m in range(micro):
        take_stats(1, m)
        shifted[m] = project(1, m)
    for item in cot_loads:
        item.wait()
    outgoing = []
    for m in range(micro):
        fill_states(1, m, shifted[m])
        shifted[m] = turn_upper(m)
        to_natural(low_s.at[m], nat.at[1, m])
        outgoing += ship(act_out, m, 0)
    weight_grads(1, slow, dread, per * width)
    run((1, C, "pair"))
    weight_grads(1, alow, dgate, 2 * per * width)
    run((1, GA, "pair"), (1, GB, "pair"))
    fill_grads(1, 0, shifted[0])
    unproject(1, 0)
    run((1, C, "rows"))
    for m in range(1, micro):
        fill_grads(1, m, shifted[m])
        unproject(1, m)
    run((1, GA, "rows"), (1, GB, "rows"))
    weight_grads(1, ulow, dproj, 0)
    run((1, B, "pair"))
    for item in outgoing:
        item.wait()
    outgoing = []
    take_norm(1, 0)
    shifted[0] = turn_lower(0)
    run((1, B, "rows"), (1, C, "seq"))
    to_natural(low_s.at[0], nat.at[1, 0])
    for m in range(1, micro):
        take_norm(1, m)
        shifted[m] = turn_lower(m)
        to_natural(low_s.at[m], nat.at[1, m])
    run((1, GA, "seq"))
    weight_grads(0, slow, dread, per * width)
    run((0, C, "pair"))
    weight_grads(0, alow, dgate, 2 * per * width)
    run((0, GA, "pair"), (0, GB, "pair"))
    run((1, GB, "seq"))
    fill_grads(0, 0, shifted[0])
    unproject(0, 0)
    run((0, C, "rows"), (1, C, "back_seq"))
    for m in range(1, micro):
        fill_grads(0, m, shifted[m])
        unproject(0, m)
    run((0, GA, "rows"), (0, GB, "rows"))
    weight_grads(0, ulow, dproj, 0)
    run((0, B, "pair"))
    small_pair()
    run((1, B, "seq"), (1, GA, "back_seq"))
    take_norm(0, 0)
    finish_grads(0)
    to_natural(low_s.at[0], nat.at[0, 0])
    outgoing += ship(ig_out, 0, 1)
    run((0, B, "rows"), (1, GB, "back_seq"))
    for m in range(1, micro):
        take_norm(0, m)
        finish_grads(m)
        to_natural(low_s.at[m], nat.at[0, m])
        outgoing += ship(ig_out, m, 1)
    small_rows()
    run((0, C, "seq"), (1, C, "back_rows"), (1, B, "back_seq"), (0, GA, "seq"), (1, GA, "back_rows"))
    small_seq()
    run((0, GB, "seq"), (0, C, "back_seq"), (1, GB, "back_rows"), (0, B, "seq"), (0, GA, "back_seq"))
    run((0, C, "back_rows"), (1, B, "back_rows"), (0, GB, "back_seq"), (0, GA, "back_rows"))
    run((0, B, "back_seq"), (0, GB, "back_rows"), (0, B, "back_rows"))

    def pick(values):
        return jnp.where(on_upper, values[1], values[0])

    tile_sum = small_total()
    wt = width // LANES
    rows_of = [to_row(tile_sum[i * wt : (i + 1) * wt]) for i in range(5)]
    dr, di, dg = rows_of[3][:, :ns], rows_of[3][:, ns:], rows_of[4]
    lam = pick([dv[l, 0:1, :] for l in range(2)])
    lr, li = lam[:, :ns], lam[:, ns:]
    by_nu = -jnp.exp(nu_ref[...]) * (lr * dr + li * di)
    by_theta = jnp.exp(theta_ref[...]) * (lr * di - li * dr)
    mean, var = rmean_ref[...], rvar_ref[...]
    for m in range(micro):
        mean = (1.0 - MOMENTUM) * mean + MOMENTUM * pick([sv[2 * l + m, 0:1, :] for l in range(2)])
        var = (1.0 - MOMENTUM) * var + MOMENTUM * pick([sv[2 * l + m, 3:4, :] for l in range(2)])
    by_bias = pick([sum(sv[2 * l + m, 5:6, :] for m in range(micro)) for l in range(2)])
    by_gain = pick([sum(sv[2 * l + m, 6:7, :] for m in range(micro)) for l in range(2)])
    blank = jnp.zeros((1, width), F32)
    small_out[...] = jnp.concatenate(
        [by_gain, by_bias]
        + rows_of[:3]
        + [jnp.concatenate([by_nu, by_theta], axis=1), dg, mean, var]
        + [blank] * 7,
        axis=0,
    )

    gather_sent(meta, n_all, SEM_META)
    for i in range(4):
        gather_sent(gst_all.at[i], n_all, SEM_STAT + i)
        gather_sent(gst_all.at[4 + i], n_all, SEM_NORM + i)
    for i in range(8):
        gather_sent(gline.at[i], n_line, SEM_LINE + i)
    small_done()
    for group in reduce[1] + reduce[0]:
        group.done()
    for item in outgoing:
        item.wait()


def finish_kernel(
    act_in,
    ig_in,
    grad_in,
    small_in,
    act_out,
    ig_out,
    ggain_out,
    gbias_out,
    gb_out,
    gnu_out,
    gtheta_out,
    ggamma_out,
    gc_out,
    gskip_out,
    gglu_out,
    gglub_out,
    nmean_out,
    nvar_out,
    low,
    flat,
    small,
    flow,
    flow_sem,
    load_sem,
    store_sem,
    small_sem,
):
    small_load = pltpu.make_async_copy(small_in, small, small_sem.at[0])
    small_load.start()
    flows_in, flows_out = [], []
    for i, (source, target) in enumerate(((act_in, act_out), (ig_in, ig_out))):
        for m in range(source.shape[1]):
            k = 2 * i + m
            flows_in.append(
                pltpu.make_async_copy(source.at[0, m, 0], flow.at[k], flow_sem.at[0, k])
            )
            flows_out.append(
                pltpu.make_async_copy(flow.at[k], target.at[0, m, 0], flow_sem.at[1, k])
            )
    width, columns = gb_out.shape[1], low.shape[1]
    blocks = low.shape[0] // width
    loads, stores = [], []
    targets = [(gb_out, 0), (gb_out, 1), (gc_out, 0), (gc_out, 1)] + [(gglu_out, k) for k in range(4)]
    for k in range(blocks):
        rows = pl.ds(k * width, width)
        loads.append(pltpu.make_async_copy(grad_in.at[rows], low.at[rows], load_sem.at[k]))
        out, column = targets[k]
        stores.append(
            pltpu.make_async_copy(
                flat.at[k], out.at[0, :, pl.ds(column * columns, columns)], store_sem.at[k]
            )
        )
    for item in loads + flows_in:
        item.start()
    small_load.wait()
    ns = gnu_out.shape[1]
    ggain_out[...] = small[0:1, :]
    gbias_out[...] = small[1:2, :]
    gskip_out[...] = small[2:3, :]
    gglub_out[:, :width] = small[3:4, :]
    gglub_out[:, width:] = small[4:5, :]
    gnu_out[...] = small[5:6, :ns]
    gtheta_out[...] = small[5:6, ns:]
    ggamma_out[...] = small[6:7, :ns]
    nmean_out[...] = small[7:8, :]
    nvar_out[...] = small[8:9, :]
    for k in range(blocks):
        loads[k].wait()
        flat[k] = low[k * width : (k + 1) * width, :].astype(F32)
        stores[k].start()
    for arrived, leave in zip(flows_in, flows_out):
        arrived.wait()
        leave.start()
    for item in stores + flows_out:
        item.wait()


def on_device(n_seq, n_rows, *args):
    inputs, starts = args[0], args[2]
    micro, _, tokens, width = inputs.shape
    ns = args[9].shape[1]
    half = tokens // 2
    n_line = 2 * n_seq
    n_all = n_line * n_rows
    any_space = pl.BlockSpec(memory_space=pl.ANY)
    hbm = pl.BlockSpec(memory_space=pltpu.HBM)
    vmem = pl.BlockSpec(memory_space=pltpu.VMEM)
    in_specs = [vmem] * 16
    for i in (0, 1, 8, 12, 14):
        in_specs[i] = any_space
    flow = jax.ShapeDtypeStruct((1, micro, 1, tokens, width), BF16)
    row = lambda size: jax.ShapeDtypeStruct((1, size), F32)
    mat = lambda size: jax.ShapeDtypeStruct((1, width, size), F32)
    vf = lambda *shape: pltpu.VMEM(shape, F32)
    vb = lambda *shape: pltpu.VMEM(shape, BF16)
    dma = lambda *count: pltpu.SemaphoreType.DMA(count)
    grad_rows = 4 * width * (width // GRAD_COLS)
    own_rows = grad_rows // 2
    scratch = [
        vb(2, micro, half, width),
        vb(2, width, 2 * ns),
        vb(2, 2 * ns, width),
        vb(2, width, 2 * width),
        vf(2, SUB, width),
        vf(2, SUB, width),
        vb(half, half),
        vb(half, half),
        vf(micro, half, LANES),
        vf(micro, half, LANES),
        vf(micro, half, LANES),
        vf(2 * micro, half, width),
        vb(2, micro * half, width),
        vf(2 * micro, half, width),
        vf(2 * micro, half + SUB, width),
        vb(2, micro * half, width),
        vb(2, micro * half, width),
        vb(micro * half, 2 * width),
        vb(micro * half, width),
        vf(micro, half, width),
        vb(micro * half, width),
        vf(micro, half, width),
        vf(micro, half, width),
        vb(micro, half, width),
        vb(micro, half, width),
        vb(micro, half, width),
        vb(micro, half, width),
        vb(micro, half, width),
        vf(2 * micro, SUB, width),
        vf(2 * micro, SUB, width),
        vf(n_all, SUB, LANES),
        vf(8, n_all, SUB, LANES),
        vf(8, n_line, SUB, LANES),
        vf(2, 24, LANES),
        vf(24, LANES),
        vf(n_rows, 24, LANES),
        vf(n_seq, 24, LANES),
        vb(2, grad_rows, GRAD_COLS),
        vb(2, own_rows, GRAD_COLS),
        vb(2, n_rows - 1, own_rows // n_rows, GRAD_COLS),
        vb(2, n_seq - 1, max(64, own_rows // n_rows // n_seq), GRAD_COLS),
        vb(2, own_rows // n_rows, GRAD_COLS),
        dma(7),
        dma(4),
        dma(4),
        dma(17),
        dma(17),
        dma(4),
        dma(4),
        dma(4),
        dma(40),
        dma(40),
        dma(8),
        dma(3),
        dma(3),
    ]
    act, ig, grads, small = pl.pallas_call(
        functools.partial(step_kernel, n_seq, n_rows),
        out_shape=(
            flow,
            flow,
            jax.ShapeDtypeStruct((grad_rows, GRAD_COLS), BF16),
            jax.ShapeDtypeStruct((16, width), F32),
        ),
        in_specs=in_specs,
        out_specs=[any_space, any_space, any_space, vmem],
        scratch_shapes=scratch,
        compiler_params=pltpu.CompilerParams(
            collective_id=0, has_side_effects=True, vmem_limit_bytes=63 * 2**20
        ),
        name="lru_blocks",
    )(*args)
    return pl.pallas_call(
        finish_kernel,
        out_shape=(
            flow,
            flow,
            row(width),
            row(width),
            mat(2 * ns),
            row(ns),
            row(ns),
            row(ns),
            mat(width),
            row(width),
            mat(2 * width),
            row(2 * width),
            row(width),
            row(width),
        ),
        in_specs=[hbm, hbm, hbm, hbm],
        out_specs=[any_space if i in (0, 1, 4, 8, 10) else vmem for i in range(14)],
        scratch_shapes=[
            vb(grad_rows, GRAD_COLS),
            vf(grad_rows // width, width, GRAD_COLS),
            vf(16, width),
            vb(2 * micro, tokens, width),
            dma(2, 4),
            dma(grad_rows // width),
            dma(grad_rows // width),
            dma(1),
        ],
        compiler_params=pltpu.CompilerParams(vmem_limit_bytes=62 * 2**20),
        name="write_results",
    )(act, ig, grads, small)


def solution(mesh):
    placed = (
        P(None, "rows", "seq", None),
        P(None, "rows", "seq", None),
        P(None, "rows", "seq"),
        P(None, "rows", "seq"),
        P("section", None),
        P("section", None),
        P("section", None),
        P("section", None),
        P("section", None, None),
        P("section", None),
        P("section", None),
        P("section", None),
        P("section", None, None),
        P("section", None),
        P("section", None, None),
        P("section", None),
    )
    return jax.shard_map(
        functools.partial(on_device, mesh.shape["seq"], mesh.shape["rows"]),
        mesh=mesh,
        in_specs=placed,
        out_specs=(
            P("section", None, "rows", "seq", None),
            P("section", None, "rows", "seq", None),
            P("section", None),
            P("section", None),
            P("section", None, None),
            P("section", None),
            P("section", None),
            P("section", None),
            P("section", None, None),
            P("section", None),
            P("section", None, None),
            P("section", None),
            P("section", None),
            P("section", None),
        ),
        check_vma=False,
    )
```

```python
import functools
import math

import jax
import jax.numpy as jnp
from jax import lax
from jax.experimental import pallas as pl
from jax.experimental.pallas import tpu as pltpu
from jax.sharding import PartitionSpec as P

NORM_EPS = 1e-05
MOMENTUM = 0.1
GELU_C = math.sqrt(2.0 / math.pi)
GELU_K = 0.044715
MESH = pl.DeviceIdType.MESH
F32 = jnp.float32
BF16 = jnp.bfloat16
SUB = 8
NSEG = 16
LANES = 128
GRAD_COLS = 256
SEQ_FIRST = ()
SPLIT = (2, 1)


def dot_nn(a, b):
    return lax.dot_general(a, b, (((1,), (0,)), ((), ())), preferred_element_type=F32)


def dot_nt(a, b):
    return lax.dot_general(a, b, (((1,), (1,)), ((), ())), preferred_element_type=F32)


def dot_tn(a, b):
    return lax.dot_general(a, b, (((0,), (0,)), ((), ())), preferred_element_type=F32)


def wide(mask, times):
    return jnp.concatenate([mask] * times, axis=1)


def to_tile(row):
    return jnp.concatenate(
        [row[:, i * LANES : (i + 1) * LANES] for i in range(row.shape[1] // LANES)], axis=0
    )


def to_row(tile):
    return jnp.concatenate([tile[i : i + 1, :] for i in range(tile.shape[0])], axis=1)


def cmul(ar, ai, br, bi):
    return ar * br - ai * bi, ar * bi + ai * br


def cpow(re, im, count):
    out = None
    while count:
        if count % 2:
            out = (re, im) if out is None else cmul(out[0], out[1], re, im)
        count //= 2
        if count:
            re, im = cmul(re, im, re, im)
    return out


def fold_rows(value):
    return jnp.sum(value.reshape(value.shape[0] // SUB, SUB, value.shape[1]), axis=0)


def step_kernel(
    n_seq,
    n_rows,
    x_hbm,
    cot_hbm,
    starts_ref,
    valid_ref,
    gain_ref,
    bias_ref,
    rmean_ref,
    rvar_ref,
    b_hbm,
    nu_ref,
    theta_ref,
    gamma_ref,
    c_hbm,
    skip_ref,
    glu_hbm,
    glub_ref,
    act_out,
    ig_out,
    grad_out,
    small_out,
    nat,
    wb,
    wc,
    wg,
    pv,
    dv,
    perm,
    perm_t,
    keep_a,
    keep_d,
    live,
    hid,
    ulow,
    drive,
    state,
    slow,
    alow,
    dgate,
    dread,
    gst,
    dproj,
    dmix,
    dunit,
    dout,
    sig_s,
    gat_s,
    dgelu_s,
    low_s,
    sv,
    sm,
    meta,
    gst_all,
    gline,
    small_own,
    small_other,
    small_by_row,
    small_by_seq,
    gbuf,
    pair_buf,
    first_buf,
    second_buf,
    gfin,
    in_sem,
    wsend_sem,
    wrecv_sem,
    gs_sem,
    gr_sem,
    out_sem,
    osend_sem,
    orecv_sem,
    rs_sem,
    rr_sem,
    gout_sem,
    ss_sem,
    sr_sem,
):
    micro = x_hbm.shape[0]
    tokens = x_hbm.shape[2]
    half = tokens // 2
    seg = half // NSEG
    width = x_hbm.shape[3]
    ns = nu_ref.shape[1]
    n_line = 2 * n_seq
    n_all = n_line * n_rows
    chunk = min(512, half)
    n_chunk = half // chunk

    s = lax.axis_index("section")
    q = lax.axis_index("seq")
    r = lax.axis_index("rows")
    rank = q * 2 + s
    me = rank * n_rows + r
    partner = (1 - s, q, r)

    def peer_all(d):
        g = me ^ d
        k = g // n_rows
        return (k % 2, k // 2, g % n_rows)

    def peer_line(d):
        k = rank ^ d
        return (k % 2, k // 2, r)

    def gather_start(buf, mine, count, peer, sem):
        def one(d, carry):
            pltpu.make_async_remote_copy(
                src_ref=buf.at[mine],
                dst_ref=buf.at[mine],
                send_sem=gs_sem.at[sem],
                recv_sem=gr_sem.at[sem],
                device_id=peer(d),
                device_id_type=MESH,
            ).start()
            return carry

        lax.fori_loop(1, count, one, 0, unroll=count <= 32)

    def gather_wait(buf, count, sem):
        part = buf.at[pl.ds(0, count - 1)]
        pltpu.make_async_copy(part, part, gr_sem.at[sem]).wait()

    def gather_sent(buf, count, sem):
        part = buf.at[pl.ds(0, count - 1)]
        pltpu.make_async_copy(part, part, gs_sem.at[sem]).wait()

    barrier = pltpu.get_barrier_semaphore()

    def greet(d, carry):
        pl.semaphore_signal(barrier, inc=1, device_id=peer_all(d), device_id_type=MESH)
        return carry

    lax.fori_loop(1, n_all, greet, 0)

    start_at = pl.multiple_of(s * half, half)
    my_tokens = pl.ds(start_at, half)
    loads = []
    for m in range(micro):
        loads.append(
            pltpu.make_async_copy(x_hbm.at[m, 0, my_tokens], nat.at[0, m], in_sem.at[m])
        )
    own_w = [
        pltpu.make_async_copy(b_hbm.at[0], wb.at[s], in_sem.at[4]),
        pltpu.make_async_copy(c_hbm.at[0], wc.at[s], in_sem.at[5]),
        pltpu.make_async_copy(glu_hbm.at[0], wg.at[s], in_sem.at[6]),
    ]
    cot_loads = [
        pltpu.make_async_copy(cot_hbm.at[m, 0, my_tokens], nat.at[1, m], in_sem.at[2 + m])
        for m in range(micro)
    ]
    for item in loads + own_w + cot_loads:
        item.start()

    pv[s, 0:1, :] = gain_ref[...]
    pv[s, 1:2, :] = bias_ref[...]
    pv[s, 2:3, :] = skip_ref[...]
    pv[s, 3:4, :] = glub_ref[:, :width]
    pv[s, 4:5, :] = glub_ref[:, width:]
    pv[s, 5:6, :] = jnp.concatenate([nu_ref[...], theta_ref[...]], axis=1)
    pv[s, 6:7, :] = jnp.concatenate([gamma_ref[...], gamma_ref[...]], axis=1)
    pv[s, 7:8, :] = jnp.zeros((1, width), F32)

    here = lax.broadcasted_iota(jnp.int32, (half, half), 0)
    there = lax.broadcasted_iota(jnp.int32, (half, half), 1)
    perm[...] = jnp.where((here % NSEG) * seg + here // NSEG == there, 1.0, 0.0).astype(BF16)
    perm_t[...] = jnp.where((there % NSEG) * seg + there // NSEG == here, 1.0, 0.0).astype(BF16)

    st_all = starts_ref[:, 0, :].astype(F32)
    va_all = valid_ref[:, 0, :].astype(F32)
    nx_all = pltpu.roll(st_all, tokens - 1, 1)
    on_upper = s == 1
    st_half = jnp.where(on_upper, st_all[:, half:], st_all[:, :half])
    va_half = jnp.where(on_upper, va_all[:, half:], va_all[:, :half])
    nx_half = jnp.where(on_upper, nx_all[:, half:], nx_all[:, :half])
    place = lax.broadcasted_iota(jnp.int32, (micro, half), 1)
    nx_half = jnp.where(place == half - 1, 0.0, nx_half)
    counts = []
    for m in range(micro):
        stacked = jnp.concatenate(
            [
                jnp.broadcast_to(1.0 - st_half[m : m + 1], (LANES, half)),
                jnp.broadcast_to(1.0 - nx_half[m : m + 1], (LANES, half)),
                jnp.broadcast_to(va_half[m : m + 1], (LANES, half)),
            ],
            axis=0,
        ).astype(BF16)
        spread = dot_nt(perm[...], stacked)
        keep_a[m] = spread[:, :LANES]
        keep_d[m] = spread[:, LANES : 2 * LANES]
        live[m] = spread[:, 2 * LANES :]
        counts.append(jnp.sum(va_half[m : m + 1], axis=1, keepdims=True))
    meta[me] = jnp.concatenate([jnp.broadcast_to(item, (1, LANES)) for item in counts], axis=0)

    def share(source, target, index):
        return pltpu.make_async_remote_copy(
            src_ref=source,
            dst_ref=target,
            send_sem=wsend_sem.at[index],
            recv_sem=wrecv_sem.at[index],
            device_id=partner,
            device_id_type=MESH,
        )

    shares = [
        share(pv.at[s], pv.at[s], 0),
        share(b_hbm.at[0], wb.at[s], 1),
        share(c_hbm.at[0], wc.at[s], 2),
        share(glu_hbm.at[0], wg.at[s], 3),
    ]
    SEM_META, SEM_STAT, SEM_NORM, SEM_LINE = 0, 1, 5, 9

    def chunks(body, init):
        return lax.fori_loop(0, n_chunk, lambda c, acc: body(pl.multiple_of(c * chunk, chunk), acc), init)

    zero_sum = jnp.zeros((SUB, width), F32)

    def enter(m):
        def body(at, acc):
            rows = pl.ds(at, chunk)
            value = dot_nn(perm[rows, :], nat[0, m])
            hid[m, rows, :] = value
            return acc + fold_rows(value * wide(live[m, rows, :], width // LANES))

        return chunks(body, zero_sum)

    def stats_of(l, m, total):
        mean = jnp.sum(total, axis=0, keepdims=True) / jnp.maximum(counts[m], 1.0)

        def body(at, acc):
            rows = pl.ds(at, chunk)
            off = hid[2 * l + m, rows, :] - mean
            return acc + fold_rows(off * off * wide(live[m, rows, :], width // LANES))

        spread = jnp.sum(chunks(body, zero_sum), axis=0, keepdims=True)
        gst_all[2 * l + m, me] = jnp.concatenate([to_tile(mean), to_tile(spread)], axis=0)

    def send_stats(l, m):
        gather_start(gst_all.at[2 * l + m], me, n_all, peer_all, SEM_STAT + 2 * l + m)

    def take_stats(l, m):
        buf = gst_all.at[2 * l + m]
        gather_wait(buf, n_all, SEM_STAT + 2 * l + m)
        data = buf[...]
        count = meta[:, m : m + 1, :]
        total = jnp.sum(count, axis=0)
        low4 = lax.broadcasted_iota(jnp.int32, (1, SUB, LANES), 1) < 4
        weighted = jnp.sum(data * jnp.where(low4, count, 1.0), axis=0)
        mean = weighted[0:4] / total
        apart = data[:, 0:4, :] - mean[None]
        var = (weighted[4:8] + jnp.sum(count * apart * apart, axis=0)) / total
        mean_row, var_row = to_row(mean), to_row(var)
        scale = lax.rsqrt(var_row + NORM_EPS)
        box = sv.at[2 * l + m]
        box[0:1, :] = mean_row
        box[1:2, :] = scale
        box[2:3, :] = scale * pv[l, 0:1, :]
        box[3:4, :] = var_row
        box[4:5, :] = jnp.broadcast_to(total[:, 0:1], (1, width))

    def unit_of(l, m, rows):
        box = sv.at[2 * l + m]
        return (hid[2 * l + m, rows, :] - box[0:1, :]) * box[2:3, :] + pv[l, 1:2, :]

    def lam_rows(l, which, conj):
        re = dv[l, which : which + 1, :ns]
        im = dv[l, which : which + 1, ns:]
        return re, (-im if conj else im)

    unroll = min(16, seg)

    def scan_local(u_ref, keep_ref, l, desc, conj):
        lr, li = lam_rows(l, 0, conj)
        lr = jnp.broadcast_to(lr, (NSEG, ns))
        li = jnp.broadcast_to(li, (NSEG, ns))

        def body(jj, carry):
            re, im = carry
            for t in range(unroll):
                j = jj * unroll + t
                if desc:
                    j = seg - 1 - j
                rows = pl.ds(pl.multiple_of(j * NSEG, NSEG), NSEG)
                keep = wide(keep_ref[rows, :], ns // LANES)
                u = u_ref[rows, :]
                kr, ki = keep * re, keep * im
                re = lr * kr - li * ki + u[:, :ns]
                im = lr * ki + li * kr + u[:, ns:]
            return re, im

        zero = jnp.zeros((NSEG, ns), F32)
        return lax.fori_loop(0, seg // unroll, body, (zero, zero))

    spot = lambda: lax.broadcasted_iota(jnp.int32, (NSEG, ns), 0)

    def before(value, step, desc, blank):
        if desc:
            return jnp.where(spot() < NSEG - step, pltpu.roll(value, NSEG - step, 0), blank)
        return jnp.where(spot() >= step, pltpu.roll(value, step, 0), blank)

    def join_segments(er, ei, keep_ref, l, desc, conj):
        shut = jnp.min(keep_ref[...].reshape(seg, NSEG, LANES), axis=0)
        lr, li = lam_rows(l, 1, conj)
        ar, ai = lr * wide(shut, ns // LANES), li * wide(shut, ns // LANES)
        for step in (1, 2, 4, 8):
            pr, pi = cmul(ar, ai, before(er, step, desc, 0.0), before(ei, step, desc, 0.0))
            er, ei = er + pr, ei + pi
            ar, ai = cmul(ar, ai, before(ar, step, desc, 1.0), before(ai, step, desc, 0.0))
        last = 0 if desc else NSEG - 1
        out = (er[last : last + 1], ei[last : last + 1], jnp.min(shut, axis=0, keepdims=True))
        shifted = (
            before(er, 1, desc, 0.0),
            before(ei, 1, desc, 0.0),
            before(ar, 1, desc, 1.0),
            before(ai, 1, desc, 0.0),
        )
        return out, shifted

    def send_carry(phase, l, m, u_ref, desc, conj):
        keep_ref = keep_d.at[m] if desc else keep_a.at[m]
        er, ei = scan_local(u_ref, keep_ref, l, desc, conj)
        (tr, ti, shut), shifted = join_segments(er, ei, keep_ref, l, desc, conj)
        if desc:
            first = keep_a[m, 0:1, :]
            tr, ti, shut = tr * wide(first, ns // LANES), ti * wide(first, ns // LANES), shut * first
        index = phase * 4 + 2 * l + m
        buf = gline.at[index]
        buf[rank] = jnp.concatenate(
            [
                to_tile(tr),
                to_tile(ti),
                shut,
                jnp.zeros((SUB - 2 * ns // LANES - 1, LANES), F32),
            ],
            axis=0,
        )
        gather_start(buf, rank, n_line, peer_line, SEM_LINE + index)
        return shifted

    def take_carry(phase, l, m, shifted, desc, conj):
        index = phase * 4 + 2 * l + m
        buf = gline.at[index]
        gather_wait(buf, n_line, SEM_LINE + index)
        lr, li = lam_rows(l, 2, conj)
        tiles = ns // LANES

        def body(step, carry):
            cr, ci = carry
            k = n_line - 1 - step if desc else step
            box = buf[k]
            shut = wide(box[2 * tiles : 2 * tiles + 1], tiles)
            pr, pi = cmul(lr * shut, li * shut, cr, ci)
            pr = pr + to_row(box[:tiles])
            pi = pi + to_row(box[tiles : 2 * tiles])
            use = k > rank if desc else k < rank
            return jnp.where(use, pr, cr), jnp.where(use, pi, ci)

        zero = jnp.zeros((1, ns), F32)
        cr, ci = lax.fori_loop(0, n_line, body, (zero, zero))
        er, ei, ar, ai = shifted
        pr, pi = cmul(ar, ai, cr, ci)
        return er + pr, ei + pi

    def fill_states(l, m, shifted):
        desc = l == 1
        re, im = take_carry(0, l, m, shifted, desc, False)
        keep_ref = keep_d.at[m] if desc else keep_a.at[m]
        u_ref, s_ref = drive.at[2 * l + m], state.at[2 * l + m]
        lr, li = lam_rows(l, 0, False)
        lr = jnp.broadcast_to(lr, (NSEG, ns))
        li = jnp.broadcast_to(li, (NSEG, ns))
        s_ref[pl.ds(half if desc else 0, NSEG), :] = jnp.concatenate([re, im], axis=1)

        def body(jj, carry):
            re, im = carry
            for t in range(unroll):
                j = jj * unroll + t
                if desc:
                    j = seg - 1 - j
                at = pl.multiple_of(j * NSEG, NSEG)
                rows = pl.ds(at, NSEG)
                keep = wide(keep_ref[rows, :], ns // LANES)
                u = u_ref[rows, :]
                kr, ki = keep * re, keep * im
                re = lr * kr - li * ki + u[:, :ns]
                im = lr * ki + li * kr + u[:, ns:]
                to = rows if desc else pl.ds(at + NSEG, NSEG)
                s_ref[to, :] = jnp.concatenate([re, im], axis=1)
            return re, im

        lax.fori_loop(0, seg // unroll, body, (re, im))

    def fill_grads(l, m, shifted):
        desc = l == 0
        re, im = take_carry(1, l, m, shifted, desc, True)
        keep_ref = keep_d.at[m] if desc else keep_a.at[m]
        pkeep_ref = keep_a.at[m] if desc else keep_d.at[m]
        u_ref, s_ref, g_ref = drive.at[2 * l + m], state.at[2 * l + m], gst.at[m]
        lr, li = lam_rows(l, 0, True)
        lr = jnp.broadcast_to(lr, (NSEG, ns))
        li = jnp.broadcast_to(li, (NSEG, ns))
        zero = jnp.zeros((NSEG, ns), F32)

        def body(jj, carry):
            re, im, dr, di, dg = carry
            for t in range(unroll):
                j = jj * unroll + t
                if desc:
                    j = seg - 1 - j
                at = pl.multiple_of(j * NSEG, NSEG)
                rows = pl.ds(at, NSEG)
                keep = wide(keep_ref[rows, :], ns // LANES)
                g = g_ref[rows, :]
                kr, ki = keep * re, keep * im
                re = lr * kr - li * ki + g[:, :ns]
                im = lr * ki + li * kr + g[:, ns:]
                g_ref[rows, :] = jnp.concatenate([re, im], axis=1)
                u = u_ref[rows, :]
                dg = dg + (re * u[:, :ns] + im * u[:, ns:])
                old = s_ref[rows if desc else pl.ds(at + NSEG, NSEG), :]
                pkeep = wide(pkeep_ref[rows, :], ns // LANES)
                pr, pi = pkeep * old[:, :ns], pkeep * old[:, ns:]
                dr = dr + (pr * re + pi * im)
                di = di + (pr * im - pi * re)
            return re, im, dr, di, dg

        _, _, dr, di, dg = lax.fori_loop(0, seg // unroll, body, (re, im, zero, zero, zero))
        box = sm.at[2 * l + m]
        box[3:4, :] = jnp.sum(jnp.concatenate([dr, di], axis=1), axis=0, keepdims=True)
        box[4:5, :] = jnp.sum(jnp.concatenate([dg, dg], axis=1), axis=0, keepdims=True)

    def project(l, m):
        gamma2 = dv[l, 3:4, :]

        def body(at, acc):
            rows = pl.ds(at, chunk)
            low = unit_of(l, m, rows).astype(BF16)
            ulow[l, pl.ds(m * half + at, chunk), :] = low
            drive[2 * l + m, rows, :] = dot_nn(low, wb[l]) * gamma2
            return acc

        chunks(body, 0)
        return send_carry(0, l, m, drive.at[2 * l + m], l == 1, False)

    def mix(l, m, at):
        rows = pl.ds(at, chunk)
        big = pl.ds(m * half + at, chunk)
        low = state[2 * l + m, pl.ds(at + (0 if l == 1 else NSEG), chunk), :].astype(BF16)
        slow[l, big, :] = low
        unit = unit_of(l, m, rows)
        mixed = dot_nn(low, wc[l]) + pv[l, 2:3, :] * unit
        square = mixed * mixed
        t = jnp.tanh((GELU_C * mixed) * (1.0 + GELU_K * square))
        half_up = 0.5 * (1.0 + t)
        act = (mixed * half_up).astype(BF16)
        alow[l, big, :] = act
        slope = half_up + (0.5 * GELU_C) * mixed * (1.0 - t * t) * (1.0 + (3.0 * GELU_K) * square)
        gates = dot_nn(act, wg[l])
        value = gates[:, :width] + pv[l, 3:4, :]
        gate = 0.5 * jnp.tanh(0.5 * (gates[:, width:] + pv[l, 4:5, :])) + 0.5
        branch = value * gate
        return unit, slope, gate, branch, (hid[2 * l + m, rows, :] + branch).astype(BF16)

    def finish_lower(m):
        def body(at, acc):
            rows = pl.ds(at, chunk)
            unit, slope, gate, branch, low = mix(0, m, at)
            sig_s[m, rows, :] = gate.astype(BF16)
            gat_s[m, rows, :] = (branch * (1.0 - gate)).astype(BF16)
            dgelu_s[m, rows, :] = slope.astype(BF16)
            low_s[m, rows, :] = low
            value = low.astype(F32)
            hid[2 + m, rows, :] = value
            return acc + fold_rows(value * wide(live[m, rows, :], width // LANES))

        return chunks(body, zero_sum)

    def to_natural(low_ref, nat_ref):
        def body(at, acc):
            rows = pl.ds(at, chunk)
            nat_ref[rows, :] = dot_nn(perm_t[rows, :], low_ref[...]).astype(BF16)
            return acc

        chunks(body, 0)

    def ship(out, m, tag):
        base = tag * 2 + m
        local = pltpu.make_async_copy(
            nat.at[s, m], out.at[0, m, 0, my_tokens], out_sem.at[base]
        )
        remote = pltpu.make_async_remote_copy(
            src_ref=nat.at[1 - s, m],
            dst_ref=out.at[0, m, 0, my_tokens],
            send_sem=osend_sem.at[base],
            recv_sem=orecv_sem.at[base],
            device_id=partner,
            device_id_type=MESH,
        )
        local.start()
        remote.start()
        return local, remote

    def gate_grads(l, m, at, unit, slope, gate, other, grad, acc):
        rows = pl.ds(at, chunk)
        big = pl.ds(m * half + at, chunk)
        d_gates = jnp.concatenate([grad * gate, grad * other], axis=1).astype(BF16)
        dgate[big, :] = d_gates
        d_mixed = dot_nt(d_gates, wg[l]) * slope
        dmix[m, rows, :] = d_mixed
        d_read = d_mixed.astype(BF16)
        dread[big, :] = d_read
        gst[m, rows, :] = dot_nt(d_read, wc[l])
        return acc[0] + fold_rows(d_gates.astype(F32)), acc[1] + fold_rows(d_mixed * unit)

    gate_zero = (jnp.zeros((SUB, 2 * width), F32), zero_sum)

    def keep_gate_sums(l, m, acc):
        box = sm.at[2 * l + m]
        box[0:1, :] = jnp.sum(acc[1], axis=0, keepdims=True)
        both = jnp.sum(acc[0], axis=0, keepdims=True)
        box[1:2, :] = both[:, :width]
        box[2:3, :] = both[:, width:]

    def turn_upper(m):
        def body(at, acc):
            rows = pl.ds(at, chunk)
            unit, slope, gate, branch, low = mix(1, m, at)
            low_s[m, rows, :] = low
            grad = dout[m, rows, :].astype(F32)
            return gate_grads(1, m, at, unit, slope, gate, branch * (1.0 - gate), grad, acc)

        keep_gate_sums(1, m, chunks(body, gate_zero))
        return send_carry(1, 1, m, gst.at[m], False, True)

    def scale_grads(l, m):
        gamma2 = dv[l, 3:4, :]

        def body(at, acc):
            dproj[pl.ds(m * half + at, chunk), :] = (gst[m, pl.ds(at, chunk), :] * gamma2).astype(BF16)
            return acc

        chunks(body, 0)

    def unproject(l, m):
        def body(at, acc):
            rows = pl.ds(at, chunk)
            low = (gst[m, rows, :] * dv[l, 3:4, :]).astype(BF16)
            dproj[pl.ds(m * half + at, chunk), :] = low
            value = dmix[m, rows, :] * pv[l, 2:3, :] + dot_nt(low, wb[l])
            dunit[m, rows, :] = value
            normed = (hid[2 * l + m, rows, :] - sv[2 * l + m, 0:1, :]) * sv[2 * l + m, 1:2, :]
            return acc[0] + fold_rows(value), acc[1] + fold_rows(value * normed)

        by_bias, by_gain = chunks(body, (zero_sum, zero_sum))
        buf = gst_all.at[4 + 2 * l + m]
        buf[me] = jnp.concatenate(
            [
                to_tile(jnp.sum(by_bias, axis=0, keepdims=True)),
                to_tile(jnp.sum(by_gain, axis=0, keepdims=True)),
            ],
            axis=0,
        )
        gather_start(buf, me, n_all, peer_all, SEM_NORM + 2 * l + m)

    def take_norm(l, m):
        buf = gst_all.at[4 + 2 * l + m]
        gather_wait(buf, n_all, SEM_NORM + 2 * l + m)
        both = jnp.sum(buf[...], axis=0)
        box = sv.at[2 * l + m]
        box[5:6, :] = to_row(both[0:4])
        box[6:7, :] = to_row(both[4:8])

    def input_grads(l, m, rows):
        box = sv.at[2 * l + m]
        share_of = 1.0 / box[4:5, :]
        by_bias = box[2:3, :] * box[5:6, :] * share_of
        by_gain = box[2:3, :] * box[6:7, :] * share_of
        normed = (hid[2 * l + m, rows, :] - box[0:1, :]) * box[1:2, :]
        mask = wide(live[m, rows, :], width // LANES)
        return (
            dout[m, rows, :].astype(F32)
            + dunit[m, rows, :] * box[2:3, :]
            - mask * (by_bias + normed * by_gain)
        ).astype(BF16)

    def turn_lower(m):
        def body(at, acc):
            rows = pl.ds(at, chunk)
            low = input_grads(1, m, rows)
            low_s[m, rows, :] = low
            grad = low.astype(F32)
            dout[m, rows, :] = low
            return gate_grads(
                0,
                m,
                at,
                unit_of(0, m, rows),
                dgelu_s[m, rows, :].astype(F32),
                sig_s[m, rows, :].astype(F32),
                gat_s[m, rows, :].astype(F32),
                grad,
                acc,
            )

        keep_gate_sums(0, m, chunks(body, gate_zero))
        return send_carry(1, 0, m, gst.at[m], True, True)

    def finish_grads(m):
        def body(at, acc):
            rows = pl.ds(at, chunk)
            low_s[m, rows, :] = input_grads(0, m, rows)
            return acc

        chunks(body, 0)

    part = 256

    def weight_grads(l, left, right, row_at):
        blocks = right.shape[1] // GRAD_COLS

        def body(c, acc):
            at = pl.multiple_of(c * part, part)
            for k in range(blocks):
                columns = pl.ds(k * GRAD_COLS, GRAD_COLS)
                value = dot_tn(left[l, :, pl.ds(at, part)], right[:, columns])
                to = pl.multiple_of(row_at + k * width + at, part)
                gbuf[l, pl.ds(to, part), :] = value.astype(BF16)
            return acc

        lax.fori_loop(0, width // part, body, 0)

    per = width // GRAD_COLS
    n_group = 4
    row_axis = (n_rows, r, lambda core, d: (core, q, r ^ d))
    seq_axis = (n_seq, q, lambda core, d: (core, q ^ d, r))
    seq_first_fits = (per * width // 2) % (16 * n_seq * n_rows) == 0

    class Reduce:
        def __init__(self, number, l, base, count, seq_first):
            self.l, self.base = l, base
            self.mine = count // 2
            self.at = base // 2
            axes = (seq_axis, row_axis) if seq_first and seq_first_fits else (row_axis, seq_axis)
            (self.k1, self.i1, self.peer1), (self.k2, self.i2, self.peer2) = axes
            self.n1 = self.mine // self.k1
            self.n2 = max(16, self.n1 // self.k2)
            self.owners = self.n1 // self.n2
            self.at1 = base // 8
            self.at2 = base // 32
            self.sem = number * 5

        def send(self, source, target, sem, where):
            return pltpu.make_async_remote_copy(
                src_ref=source,
                dst_ref=target,
                send_sem=rs_sem.at[self.sem + sem],
                recv_sem=rr_sem.at[self.sem + sem],
                device_id=where,
                device_id_type=MESH,
            )

        def await_rows(self, count, sem, sems=None):
            ref = gbuf.at[0, pl.ds(0, count)]
            pltpu.make_async_copy(ref, ref, (rr_sem if sems is None else sems).at[self.sem + sem]).wait()

        def half_of(self, core):
            return gbuf.at[self.l, pl.ds(pl.multiple_of(self.base + core * self.mine, 16), self.mine)]

        def total(self):
            return pair_buf.at[self.l, pl.ds(self.at, self.mine)]

        def piece(self, ref, index, size):
            return ref.at[pl.ds(pl.multiple_of(index * size, 16), size)]

        def pair(self):
            self.send(self.half_of(1 - s), self.total(), 0, partner).start()

        def first(self):
            self.await_rows(self.mine, 0)
            own, total = self.half_of(s), self.total()
            total[...] = (own[...].astype(F32) + total[...].astype(F32)).astype(BF16)
            into = first_buf.at[self.l, :, pl.ds(self.at1, self.n1)]
            for d in range(1, self.k1):
                self.send(
                    self.piece(total, self.i1 ^ d, self.n1), into.at[d - 1], 1, self.peer1(s, d)
                ).start()

        def second(self):
            self.await_rows((self.k1 - 1) * self.n1, 1)
            total = self.piece(self.total(), self.i1, self.n1)
            value = total[...].astype(F32)
            for d in range(self.k1 - 1):
                value = value + first_buf[self.l, d, pl.ds(self.at1, self.n1), :].astype(F32)
            total[...] = value.astype(BF16)
            into = second_buf.at[self.l, :, pl.ds(self.at2, self.n2)]

            def one(d, acc):
                to = self.i2 ^ d

                def go():
                    self.send(self.piece(total, to, self.n2), into.at[d - 1], 2, self.peer2(s, d)).start()

                self.when(to < self.owners, go)
                return acc

            lax.fori_loop(1, self.k2, one, 0, unroll=self.k2 <= 4)

        def when(self, condition, go):
            if self.owners == self.k2:
                go()
            else:
                pl.when(condition)(go)

        def block(self):
            return gfin.at[self.l, pl.ds(self.at1, self.n1)]

        def back_second(self):
            total = self.piece(self.total(), self.i1, self.n1)
            mine = self.piece(self.block(), self.i2, self.n2)

            def go():
                self.await_rows((self.k2 - 1) * self.n2, 2)
                value = self.piece(total, self.i2, self.n2)[...].astype(F32)
                for d in range(self.k2 - 1):
                    value = value + second_buf[self.l, d, pl.ds(self.at2, self.n2), :].astype(F32)
                mine[...] = value.astype(BF16)

                def one(d, acc):
                    self.send(mine, mine, 3, self.peer2(s, d)).start()
                    return acc

                lax.fori_loop(1, self.k2, one, 0, unroll=self.k2 <= 4)

            self.when(self.i2 < self.owners, go)

        def result(self):
            at = self.base + s * self.mine + self.i1 * self.n1
            return grad_out.at[pl.ds(pl.multiple_of(at, 16), self.n1)]

        def keep_own(self):
            return pltpu.make_async_copy(self.block(), self.result(), gout_sem.at[self.sem // 5])

        def some_owners(self, sem, sems=None):
            self.when(
                self.i2 < self.owners, lambda: self.await_rows((self.owners - 1) * self.n2, sem, sems)
            )
            if self.owners < self.k2:
                self.when(
                    self.i2 >= self.owners, lambda: self.await_rows(self.owners * self.n2, sem, sems)
                )

        def back_first(self):
            self.some_owners(3)
            pl.when(s == self.l)(lambda: self.keep_own().start())
            pl.when(s != self.l)(lambda: self.send(self.block(), self.result(), 4, partner).start())
            for d in range(1, self.k1):
                self.send(self.block(), self.result(), 4, self.peer1(self.l, d)).start()

        def done(self):
            def settle():
                self.keep_own().wait()
                self.await_rows((2 * self.k1 - 1) * self.n1, 4)
                self.await_rows((self.k1 - 1) * self.n1, 4, rs_sem)

            pl.when(s == self.l)(settle)
            pl.when(s != self.l)(lambda: self.await_rows(self.k1 * self.n1, 4, rs_sem))
            self.await_rows(self.mine, 0, rs_sem)
            self.await_rows((self.k1 - 1) * self.n1, 1, rs_sem)
            self.some_owners(2, rs_sem)
            self.when(
                self.i2 < self.owners, lambda: self.await_rows((self.k2 - 1) * self.n2, 3, rs_sem)
            )

    reduce = [[], []]
    for l in range(2):
        for g in range(n_group):
            count = per * width // SPLIT[l]
            for k in range(SPLIT[l]):
                number = len(reduce[0]) + len(reduce[1])
                reduce[l].append(
                    Reduce(number, l, g * per * width + k * count, count, (l, g) in SEQ_FIRST)
                )
    B, C, GA, GB = range(n_group)

    def run(*plan):
        for l, g, step in plan:
            for k in range(SPLIT[l]):
                getattr(reduce[l][g * SPLIT[l] + k], step)()

    def run_part(l, g, k, step):
        getattr(reduce[l][g * SPLIT[l] + k], step)()

    def small_copy(source, target, sem, where):
        return pltpu.make_async_remote_copy(
            src_ref=source,
            dst_ref=target,
            send_sem=ss_sem.at[sem],
            recv_sem=sr_sem.at[sem],
            device_id=where,
            device_id_type=MESH,
        )

    def small_await(ref, sems, sem):
        pltpu.make_async_copy(ref, ref, sems.at[sem]).wait()

    def small_pair():
        for l in range(2):
            both = sm[2 * l]
            for m in range(1, micro):
                both = both + sm[2 * l + m]
            small_own[l] = jnp.concatenate(
                [to_tile(both[i : i + 1]) for i in range(5)] + [jnp.zeros((4, LANES), F32)], axis=0
            )
        small_copy(small_own.at[1 - s], small_other, 0, partner).start()

    def small_rows():
        small_await(small_other, sr_sem, 0)
        first, second = small_own[s], small_other[...]
        small_by_row[r] = first + second
        for d in range(1, n_rows):
            small_copy(small_by_row.at[r], small_by_row.at[r], 1, (s, q, r ^ d)).start()

    def small_seq():
        small_await(small_by_row.at[pl.ds(0, n_rows - 1)], sr_sem, 1)
        total = small_by_row[0]
        for k in range(1, n_rows):
            total = total + small_by_row[k]
        small_by_seq[q] = total

        def one(d, acc):
            small_copy(small_by_seq.at[q], small_by_seq.at[q], 2, (s, q ^ d, r)).start()
            return acc

        lax.fori_loop(1, n_seq, one, 0)

    def small_total():
        small_await(small_by_seq.at[pl.ds(0, n_seq - 1)], sr_sem, 2)
        return jnp.sum(small_by_seq[...], axis=0)

    def small_done():
        small_await(small_other, ss_sem, 0)
        small_await(small_by_row.at[pl.ds(0, n_rows - 1)], ss_sem, 1)
        small_await(small_by_seq.at[pl.ds(0, n_seq - 1)], ss_sem, 2)

    for m in range(micro):
        loads[m].wait()
        stats_of(0, m, enter(m))
    pl.semaphore_wait(barrier, n_all - 1)
    gather_start(meta, me, n_all, peer_all, SEM_META)
    for m in range(micro):
        send_stats(0, m)
    for item in shares[:2]:
        item.start()
    for item in own_w:
        item.wait()
    for item in shares[:2]:
        item.wait()
    for item in shares[2:]:
        item.start()
    for l in range(2):
        decay = jnp.exp(-jnp.exp(pv[l, 5:6, :ns]))
        phase = jnp.exp(pv[l, 5:6, ns:])
        re, im = decay * jnp.cos(phase), decay * jnp.sin(phase)
        dv[l, 0:1, :] = jnp.concatenate([re, im], axis=1)
        dv[l, 1:2, :] = jnp.concatenate(cpow(re, im, seg), axis=1)
        dv[l, 2:3, :] = jnp.concatenate(cpow(re, im, half), axis=1)
        dv[l, 3:4, :] = jnp.exp(pv[l, 6:7, :])
    gather_wait(meta, n_all, SEM_META)

    shifted = {}
    for m in range(micro):
        take_stats(0, m)
        shifted[m] = project(0, m)
    for item in shares[2:]:
        item.wait()
    for m in range(micro):
        fill_states(0, m, shifted[m])
        stats_of(1, m, finish_lower(m))
        send_stats(1, m)
    for m in range(micro):
        to_natural(low_s.at[m], nat.at[0, m])
    for m in range(micro):
        take_stats(1, m)
        shifted[m] = project(1, m)
    for item in cot_loads:
        item.wait()
    for m in range(micro):
        dout[m] = dot_nn(perm[...], nat[1, m]).astype(BF16)
    outgoing = []
    for m in range(micro):
        fill_states(1, m, shifted[m])
        shifted[m] = turn_upper(m)
    fill_grads(1, 0, shifted[0])
    unproject(1, 0)
    weight_grads(1, slow, dread, per * width)
    run((1, C, "pair"))
    weight_grads(1, alow, dgate, 2 * per * width)
    run((1, GA, "pair"), (1, GB, "pair"), (1, C, "first"))
    for m in range(1, micro):
        fill_grads(1, m, shifted[m])
        unproject(1, m)
    run((1, GA, "first"), (1, GB, "first"))
    weight_grads(1, ulow, dproj, 0)
    run((1, B, "pair"))
    for m in range(micro):
        to_natural(low_s.at[m], nat.at[1, m])
        outgoing += ship(act_out, m, 0)
    take_norm(1, 0)
    shifted[0] = turn_lower(0)
    for item in outgoing:
        item.wait()
    outgoing = []
    run((1, B, "first"), (1, C, "second"))
    to_natural(low_s.at[0], nat.at[1, 0])
    for m in range(1, micro):
        take_norm(1, m)
        shifted[m] = turn_lower(m)
        to_natural(low_s.at[m], nat.at[1, m])
    run((1, GA, "second"))
    weight_grads(0, slow, dread, per * width)
    run((0, C, "pair"))
    weight_grads(0, alow, dgate, 2 * per * width)
    run((0, GA, "pair"), (0, GB, "pair"))
    run((1, GB, "second"))
    fill_grads(0, 0, shifted[0])
    unproject(0, 0)
    run((0, C, "first"), (1, C, "back_second"))
    for m in range(1, micro):
        fill_grads(0, m, shifted[m])
        unproject(0, m)
    run((0, GA, "first"), (0, GB, "first"))
    weight_grads(0, ulow, dproj, 0)
    run((0, B, "pair"))
    small_pair()
    run((1, B, "second"), (1, GA, "back_second"))
    take_norm(0, 0)
    finish_grads(0)
    to_natural(low_s.at[0], nat.at[0, 0])
    outgoing += ship(ig_out, 0, 1)
    run((0, B, "first"), (1, GB, "back_second"))
    for m in range(1, micro):
        take_norm(0, m)
        finish_grads(m)
        to_natural(low_s.at[m], nat.at[0, m])
        outgoing += ship(ig_out, m, 1)
    small_rows()
    run((1, B, "back_second"))
    order = [(g, k) for g in (C, GA, GB, B) for k in range(SPLIT[0])]
    late = [(1, C), (1, GA), (1, GB), (1, B)]
    lag = 3
    for i in range(len(order) + 2 * lag):
        if i < len(order):
            run_part(0, *order[i], "second")
        if 0 <= i - lag < len(order):
            run_part(0, *order[i - lag], "back_second")
        if i % 2 == 0 and late:
            run((*late.pop(0), "back_first"))
        if 0 <= i - 2 * lag < len(order):
            run_part(0, *order[i - 2 * lag], "back_first")
        if i == 2:
            small_seq()

    def pick(values):
        return jnp.where(on_upper, values[1], values[0])

    tile_sum = small_total()
    wt = width // LANES
    rows_of = [to_row(tile_sum[i * wt : (i + 1) * wt]) for i in range(5)]
    dr, di, dg = rows_of[3][:, :ns], rows_of[3][:, ns:], rows_of[4]
    lam = pick([dv[l, 0:1, :] for l in range(2)])
    lr, li = lam[:, :ns], lam[:, ns:]
    by_nu = -jnp.exp(nu_ref[...]) * (lr * dr + li * di)
    by_theta = jnp.exp(theta_ref[...]) * (lr * di - li * dr)
    mean, var = rmean_ref[...], rvar_ref[...]
    for m in range(micro):
        mean = (1.0 - MOMENTUM) * mean + MOMENTUM * pick([sv[2 * l + m, 0:1, :] for l in range(2)])
        var = (1.0 - MOMENTUM) * var + MOMENTUM * pick([sv[2 * l + m, 3:4, :] for l in range(2)])
    by_bias = pick([sum(sv[2 * l + m, 5:6, :] for m in range(micro)) for l in range(2)])
    by_gain = pick([sum(sv[2 * l + m, 6:7, :] for m in range(micro)) for l in range(2)])
    blank = jnp.zeros((1, width), F32)
    small_out[...] = jnp.concatenate(
        [by_gain, by_bias]
        + rows_of[:3]
        + [jnp.concatenate([by_nu, by_theta], axis=1), dg, mean, var]
        + [blank] * 7,
        axis=0,
    )

    gather_sent(meta, n_all, SEM_META)
    for i in range(4):
        gather_sent(gst_all.at[i], n_all, SEM_STAT + i)
        gather_sent(gst_all.at[4 + i], n_all, SEM_NORM + i)
    for i in range(8):
        gather_sent(gline.at[i], n_line, SEM_LINE + i)
    small_done()
    for group in reduce[1] + reduce[0]:
        group.done()
    for item in outgoing:
        item.wait()


def finish_kernel(
    act_in,
    ig_in,
    grad_in,
    small_in,
    act_out,
    ig_out,
    ggain_out,
    gbias_out,
    gb_out,
    gnu_out,
    gtheta_out,
    ggamma_out,
    gc_out,
    gskip_out,
    gglu_out,
    gglub_out,
    nmean_out,
    nvar_out,
    low,
    flat,
    small,
    flow,
    flow_sem,
    load_sem,
    store_sem,
    small_sem,
):
    small_load = pltpu.make_async_copy(small_in, small, small_sem.at[0])
    small_load.start()
    flows_in, flows_out = [], []
    for i, (source, target) in enumerate(((act_in, act_out), (ig_in, ig_out))):
        for m in range(source.shape[1]):
            k = 2 * i + m
            flows_in.append(
                pltpu.make_async_copy(source.at[0, m, 0], flow.at[k], flow_sem.at[0, k])
            )
            flows_out.append(
                pltpu.make_async_copy(flow.at[k], target.at[0, m, 0], flow_sem.at[1, k])
            )
    width, columns = gb_out.shape[1], low.shape[1]
    blocks = low.shape[0] // width
    loads, stores = [], []
    targets = [(gb_out, 0), (gb_out, 1), (gc_out, 0), (gc_out, 1)] + [(gglu_out, k) for k in range(4)]
    for k in range(blocks):
        rows = pl.ds(k * width, width)
        loads.append(pltpu.make_async_copy(grad_in.at[rows], low.at[rows], load_sem.at[k]))
        out, column = targets[k]
        stores.append(
            pltpu.make_async_copy(
                flat.at[k], out.at[0, :, pl.ds(column * columns, columns)], store_sem.at[k]
            )
        )
    for item in loads + flows_in:
        item.start()
    small_load.wait()
    ns = gnu_out.shape[1]
    ggain_out[...] = small[0:1, :]
    gbias_out[...] = small[1:2, :]
    gskip_out[...] = small[2:3, :]
    gglub_out[:, :width] = small[3:4, :]
    gglub_out[:, width:] = small[4:5, :]
    gnu_out[...] = small[5:6, :ns]
    gtheta_out[...] = small[5:6, ns:]
    ggamma_out[...] = small[6:7, :ns]
    nmean_out[...] = small[7:8, :]
    nvar_out[...] = small[8:9, :]
    for k in range(blocks):
        loads[k].wait()
        flat[k] = low[k * width : (k + 1) * width, :].astype(F32)
        stores[k].start()
    for arrived, leave in zip(flows_in, flows_out):
        arrived.wait()
        leave.start()
    for item in stores + flows_out:
        item.wait()


def on_device(n_seq, n_rows, *args):
    inputs, starts = args[0], args[2]
    micro, _, tokens, width = inputs.shape
    ns = args[9].shape[1]
    half = tokens // 2
    n_line = 2 * n_seq
    n_all = n_line * n_rows
    any_space = pl.BlockSpec(memory_space=pl.ANY)
    hbm = pl.BlockSpec(memory_space=pltpu.HBM)
    vmem = pl.BlockSpec(memory_space=pltpu.VMEM)
    in_specs = [vmem] * 16
    for i in (0, 1, 8, 12, 14):
        in_specs[i] = any_space
    flow = jax.ShapeDtypeStruct((1, micro, 1, tokens, width), BF16)
    row = lambda size: jax.ShapeDtypeStruct((1, size), F32)
    mat = lambda size: jax.ShapeDtypeStruct((1, width, size), F32)
    vf = lambda *shape: pltpu.VMEM(shape, F32)
    vb = lambda *shape: pltpu.VMEM(shape, BF16)
    dma = lambda *count: pltpu.SemaphoreType.DMA(count)
    grad_rows = 4 * width * (width // GRAD_COLS)
    own_rows = grad_rows // 2
    scratch = [
        vb(2, micro, half, width),
        vb(2, width, 2 * ns),
        vb(2, 2 * ns, width),
        vb(2, width, 2 * width),
        vf(2, SUB, width),
        vf(2, SUB, width),
        vb(half, half),
        vb(half, half),
        vf(micro, half, LANES),
        vf(micro, half, LANES),
        vf(micro, half, LANES),
        vf(2 * micro, half, width),
        vb(2, micro * half, width),
        vf(2 * micro, half, width),
        vf(2 * micro, half + NSEG, width),
        vb(2, micro * half, width),
        vb(2, micro * half, width),
        vb(micro * half, 2 * width),
        vb(micro * half, width),
        vf(micro, half, width),
        vb(micro * half, width),
        vf(micro, half, width),
        vf(micro, half, width),
        vb(micro, half, width),
        vb(micro, half, width),
        vb(micro, half, width),
        vb(micro, half, width),
        vb(micro, half, width),
        vf(2 * micro, SUB, width),
        vf(2 * micro, SUB, width),
        vf(n_all, micro, LANES),
        vf(8, n_all, SUB, LANES),
        vf(8, n_line, SUB, LANES),
        vf(2, 24, LANES),
        vf(24, LANES),
        vf(n_rows, 24, LANES),
        vf(n_seq, 24, LANES),
        vb(2, grad_rows, GRAD_COLS),
        vb(2, own_rows, GRAD_COLS),
        vb(2, n_rows - 1, own_rows // n_rows, GRAD_COLS),
        vb(2, n_seq - 1, own_rows // 16, GRAD_COLS),
        vb(2, own_rows // n_rows, GRAD_COLS),
        dma(7),
        dma(4),
        dma(4),
        dma(17),
        dma(17),
        dma(4),
        dma(4),
        dma(4),
        dma(60),
        dma(60),
        dma(12),
        dma(3),
        dma(3),
    ]
    act, ig, grads, small = pl.pallas_call(
        functools.partial(step_kernel, n_seq, n_rows),
        out_shape=(
            flow,
            flow,
            jax.ShapeDtypeStruct((grad_rows, GRAD_COLS), BF16),
            jax.ShapeDtypeStruct((16, width), F32),
        ),
        in_specs=in_specs,
        out_specs=[any_space, any_space, any_space, vmem],
        scratch_shapes=scratch,
        compiler_params=pltpu.CompilerParams(
            collective_id=0, has_side_effects=True, vmem_limit_bytes=63 * 2**20
        ),
        name="lru_blocks",
    )(*args)
    return pl.pallas_call(
        finish_kernel,
        out_shape=(
            flow,
            flow,
            row(width),
            row(width),
            mat(2 * ns),
            row(ns),
            row(ns),
            row(ns),
            mat(width),
            row(width),
            mat(2 * width),
            row(2 * width),
            row(width),
            row(width),
        ),
        in_specs=[hbm, hbm, hbm, hbm],
        out_specs=[any_space if i in (0, 1, 4, 8, 10) else vmem for i in range(14)],
        scratch_shapes=[
            vb(grad_rows, GRAD_COLS),
            vf(grad_rows // width, width, GRAD_COLS),
            vf(16, width),
            vb(2 * micro, tokens, width),
            dma(2, 4),
            dma(grad_rows // width),
            dma(grad_rows // width),
            dma(1),
        ],
        compiler_params=pltpu.CompilerParams(vmem_limit_bytes=62 * 2**20),
        name="write_results",
    )(act, ig, grads, small)


def solution(mesh):
    placed = (
        P(None, "rows", "seq", None),
        P(None, "rows", "seq", None),
        P(None, "rows", "seq"),
        P(None, "rows", "seq"),
        P("section", None),
        P("section", None),
        P("section", None),
        P("section", None),
        P("section", None, None),
        P("section", None),
        P("section", None),
        P("section", None),
        P("section", None, None),
        P("section", None),
        P("section", None, None),
        P("section", None),
    )
    return jax.shard_map(
        functools.partial(on_device, mesh.shape["seq"], mesh.shape["rows"]),
        mesh=mesh,
        in_specs=placed,
        out_specs=(
            P("section", None, "rows", "seq", None),
            P("section", None, "rows", "seq", None),
            P("section", None),
            P("section", None),
            P("section", None, None),
            P("section", None),
            P("section", None),
            P("section", None),
            P("section", None, None),
            P("section", None),
            P("section", None, None),
            P("section", None),
            P("section", None),
            P("section", None),
        ),
        check_vma=False,
    )
```

```python
import functools
import math

import jax
import jax.numpy as jnp
from jax import lax
from jax.experimental import pallas as pl
from jax.experimental.pallas import tpu as pltpu
from jax.sharding import PartitionSpec as P

NORM_EPS = 1e-05
MOMENTUM = 0.1
GELU_C = math.sqrt(2.0 / math.pi)
GELU_K = 0.044715
MESH = pl.DeviceIdType.MESH
F32 = jnp.float32
BF16 = jnp.bfloat16
SUB = 8
NSEG = 16
LANES = 128
GRAD_COLS = 256
SEQ_FIRST = ()
SPLIT = (2, 1)


def dot_nn(a, b):
    return lax.dot_general(a, b, (((1,), (0,)), ((), ())), preferred_element_type=F32)


def dot_nt(a, b):
    return lax.dot_general(a, b, (((1,), (1,)), ((), ())), preferred_element_type=F32)


def dot_tn(a, b):
    return lax.dot_general(a, b, (((0,), (0,)), ((), ())), preferred_element_type=F32)


def wide(mask, times):
    return jnp.concatenate([mask] * times, axis=1)


def to_tile(row):
    return jnp.concatenate(
        [row[:, i * LANES : (i + 1) * LANES] for i in range(row.shape[1] // LANES)], axis=0
    )


def to_row(tile):
    return jnp.concatenate([tile[i : i + 1, :] for i in range(tile.shape[0])], axis=1)


def cmul(ar, ai, br, bi):
    return ar * br - ai * bi, ar * bi + ai * br


def cpow(re, im, count):
    out = None
    while count:
        if count % 2:
            out = (re, im) if out is None else cmul(out[0], out[1], re, im)
        count //= 2
        if count:
            re, im = cmul(re, im, re, im)
    return out


def fold_rows(value):
    return jnp.sum(value.reshape(value.shape[0] // SUB, SUB, value.shape[1]), axis=0)


def step_kernel(
    n_seq,
    n_rows,
    x_hbm,
    cot_hbm,
    starts_ref,
    valid_ref,
    gain_ref,
    bias_ref,
    rmean_ref,
    rvar_ref,
    b_hbm,
    nu_ref,
    theta_ref,
    gamma_ref,
    c_hbm,
    skip_ref,
    glu_hbm,
    glub_ref,
    act_out,
    ig_out,
    grad_out,
    small_out,
    nat,
    wb,
    wc,
    wg,
    pv,
    dv,
    perm,
    perm_t,
    keep_a,
    keep_d,
    live,
    hid,
    ulow,
    drive,
    state,
    slow,
    alow,
    dgate,
    dread,
    gst,
    dproj,
    dmix,
    dunit,
    dout,
    sig_s,
    gat_s,
    dgelu_s,
    low_s,
    sv,
    sm,
    meta,
    gst_all,
    gline,
    small_own,
    small_other,
    small_by_row,
    small_by_seq,
    gbuf,
    pair_buf,
    first_buf,
    second_buf,
    gfin,
    in_sem,
    wsend_sem,
    wrecv_sem,
    gs_sem,
    gr_sem,
    out_sem,
    osend_sem,
    orecv_sem,
    rs_sem,
    rr_sem,
    gout_sem,
    ss_sem,
    sr_sem,
):
    micro = x_hbm.shape[0]
    tokens = x_hbm.shape[2]
    half = tokens // 2
    seg = half // NSEG
    width = x_hbm.shape[3]
    ns = nu_ref.shape[1]
    n_line = 2 * n_seq
    n_all = n_line * n_rows
    chunk = min(512, half)
    n_chunk = half // chunk

    s = lax.axis_index("section")
    q = lax.axis_index("seq")
    r = lax.axis_index("rows")
    rank = q * 2 + s
    me = rank * n_rows + r
    partner = (1 - s, q, r)

    def peer_all(d):
        g = me ^ d
        k = g // n_rows
        return (k % 2, k // 2, g % n_rows)

    def peer_line(d):
        k = rank ^ d
        return (k % 2, k // 2, r)

    def gather_start(buf, mine, count, peer, sem):
        def one(d, carry):
            pltpu.make_async_remote_copy(
                src_ref=buf.at[mine],
                dst_ref=buf.at[mine],
                send_sem=gs_sem.at[sem],
                recv_sem=gr_sem.at[sem],
                device_id=peer(d),
                device_id_type=MESH,
            ).start()
            return carry

        lax.fori_loop(1, count, one, 0, unroll=count <= 32)

    def gather_wait(buf, count, sem):
        part = buf.at[pl.ds(0, count - 1)]
        pltpu.make_async_copy(part, part, gr_sem.at[sem]).wait()

    def gather_sent(buf, count, sem):
        part = buf.at[pl.ds(0, count - 1)]
        pltpu.make_async_copy(part, part, gs_sem.at[sem]).wait()

    barrier = pltpu.get_barrier_semaphore()

    def greet(d, carry):
        pl.semaphore_signal(barrier, inc=1, device_id=peer_all(d), device_id_type=MESH)
        return carry

    lax.fori_loop(1, n_all, greet, 0)

    start_at = pl.multiple_of(s * half, half)
    my_tokens = pl.ds(start_at, half)
    loads = []
    for m in range(micro):
        loads.append(
            pltpu.make_async_copy(x_hbm.at[m, 0, my_tokens], nat.at[0, m], in_sem.at[m])
        )
    own_w = [
        pltpu.make_async_copy(b_hbm.at[0], wb.at[s], in_sem.at[4]),
        pltpu.make_async_copy(c_hbm.at[0], wc.at[s], in_sem.at[5]),
        pltpu.make_async_copy(glu_hbm.at[0], wg.at[s], in_sem.at[6]),
    ]
    cot_loads = [
        pltpu.make_async_copy(cot_hbm.at[m, 0, my_tokens], nat.at[1, m], in_sem.at[2 + m])
        for m in range(micro)
    ]
    for item in loads + own_w + cot_loads:
        item.start()

    pv[s, 0:1, :] = gain_ref[...]
    pv[s, 1:2, :] = bias_ref[...]
    pv[s, 2:3, :] = skip_ref[...]
    pv[s, 3:4, :] = glub_ref[:, :width]
    pv[s, 4:5, :] = glub_ref[:, width:]
    pv[s, 5:6, :] = jnp.concatenate([nu_ref[...], theta_ref[...]], axis=1)
    pv[s, 6:7, :] = jnp.concatenate([gamma_ref[...], gamma_ref[...]], axis=1)
    pv[s, 7:8, :] = jnp.zeros((1, width), F32)

    here = lax.broadcasted_iota(jnp.int32, (half, half), 0)
    there = lax.broadcasted_iota(jnp.int32, (half, half), 1)
    perm[...] = jnp.where((here % NSEG) * seg + here // NSEG == there, 1.0, 0.0).astype(BF16)
    perm_t[...] = jnp.where((there % NSEG) * seg + there // NSEG == here, 1.0, 0.0).astype(BF16)

    st_all = starts_ref[:, 0, :].astype(F32)
    va_all = valid_ref[:, 0, :].astype(F32)
    nx_all = pltpu.roll(st_all, tokens - 1, 1)
    on_upper = s == 1
    st_half = jnp.where(on_upper, st_all[:, half:], st_all[:, :half])
    va_half = jnp.where(on_upper, va_all[:, half:], va_all[:, :half])
    nx_half = jnp.where(on_upper, nx_all[:, half:], nx_all[:, :half])
    place = lax.broadcasted_iota(jnp.int32, (micro, half), 1)
    nx_half = jnp.where(place == half - 1, 0.0, nx_half)
    counts = []
    for m in range(micro):
        stacked = jnp.concatenate(
            [
                jnp.broadcast_to(1.0 - st_half[m : m + 1], (LANES, half)),
                jnp.broadcast_to(1.0 - nx_half[m : m + 1], (LANES, half)),
                jnp.broadcast_to(va_half[m : m + 1], (LANES, half)),
            ],
            axis=0,
        ).astype(BF16)
        spread = dot_nt(perm[...], stacked)
        keep_a[m] = spread[:, :LANES]
        keep_d[m] = spread[:, LANES : 2 * LANES]
        live[m] = spread[:, 2 * LANES :]
        counts.append(jnp.sum(va_half[m : m + 1], axis=1, keepdims=True))
    meta[me] = jnp.concatenate([jnp.broadcast_to(item, (1, LANES)) for item in counts], axis=0)

    def share(source, target, index):
        return pltpu.make_async_remote_copy(
            src_ref=source,
            dst_ref=target,
            send_sem=wsend_sem.at[index],
            recv_sem=wrecv_sem.at[index],
            device_id=partner,
            device_id_type=MESH,
        )

    shares = [
        share(pv.at[s], pv.at[s], 0),
        share(b_hbm.at[0], wb.at[s], 1),
        share(c_hbm.at[0], wc.at[s], 2),
        share(glu_hbm.at[0], wg.at[s], 3),
    ]
    SEM_META, SEM_STAT, SEM_NORM, SEM_LINE = 0, 1, 5, 9

    def chunks(body, init):
        return lax.fori_loop(0, n_chunk, lambda c, acc: body(pl.multiple_of(c * chunk, chunk), acc), init)

    zero_sum = jnp.zeros((SUB, width), F32)

    def enter(m):
        def body(at, acc):
            rows = pl.ds(at, chunk)
            value = dot_nn(perm[rows, :], nat[0, m])
            hid[m, rows, :] = value
            return acc + fold_rows(value * wide(live[m, rows, :], width // LANES))

        return chunks(body, zero_sum)

    def stats_of(l, m, total):
        mean = jnp.sum(total, axis=0, keepdims=True) / jnp.maximum(counts[m], 1.0)

        def body(at, acc):
            rows = pl.ds(at, chunk)
            off = hid[2 * l + m, rows, :] - mean
            return acc + fold_rows(off * off * wide(live[m, rows, :], width // LANES))

        spread = jnp.sum(chunks(body, zero_sum), axis=0, keepdims=True)
        gst_all[2 * l + m, me] = jnp.concatenate([to_tile(mean), to_tile(spread)], axis=0)

    def send_stats(l, m):
        gather_start(gst_all.at[2 * l + m], me, n_all, peer_all, SEM_STAT + 2 * l + m)

    def take_stats(l, m):
        buf = gst_all.at[2 * l + m]
        gather_wait(buf, n_all, SEM_STAT + 2 * l + m)
        data = buf[...]
        count = meta[:, m : m + 1, :]
        total = jnp.sum(count, axis=0)
        low4 = lax.broadcasted_iota(jnp.int32, (1, SUB, LANES), 1) < 4
        weighted = jnp.sum(data * jnp.where(low4, count, 1.0), axis=0)
        mean = weighted[0:4] / total
        apart = data[:, 0:4, :] - mean[None]
        var = (weighted[4:8] + jnp.sum(count * apart * apart, axis=0)) / total
        mean_row, var_row = to_row(mean), to_row(var)
        scale = lax.rsqrt(var_row + NORM_EPS)
        box = sv.at[2 * l + m]
        box[0:1, :] = mean_row
        box[1:2, :] = scale
        box[2:3, :] = scale * pv[l, 0:1, :]
        box[3:4, :] = var_row
        box[4:5, :] = jnp.broadcast_to(total[:, 0:1], (1, width))

    def unit_of(l, m, rows):
        box = sv.at[2 * l + m]
        return (hid[2 * l + m, rows, :] - box[0:1, :]) * box[2:3, :] + pv[l, 1:2, :]

    def lam_rows(l, which, conj):
        re = dv[l, which : which + 1, :ns]
        im = dv[l, which : which + 1, ns:]
        return re, (-im if conj else im)

    unroll = min(16, seg)

    def scan_local(u_ref, keep_ref, l, desc, conj):
        lr, li = lam_rows(l, 0, conj)
        lr = jnp.broadcast_to(lr, (NSEG, ns))
        li = jnp.broadcast_to(li, (NSEG, ns))

        def body(jj, carry):
            re, im = carry
            for t in range(unroll):
                j = jj * unroll + t
                if desc:
                    j = seg - 1 - j
                rows = pl.ds(pl.multiple_of(j * NSEG, NSEG), NSEG)
                keep = wide(keep_ref[rows, :], ns // LANES)
                u = u_ref[rows, :]
                kr, ki = keep * re, keep * im
                re = lr * kr - li * ki + u[:, :ns]
                im = lr * ki + li * kr + u[:, ns:]
            return re, im

        zero = jnp.zeros((NSEG, ns), F32)
        return lax.fori_loop(0, seg // unroll, body, (zero, zero))

    spot = lambda: lax.broadcasted_iota(jnp.int32, (NSEG, ns), 0)

    def before(value, step, desc, blank):
        if desc:
            return jnp.where(spot() < NSEG - step, pltpu.roll(value, NSEG - step, 0), blank)
        return jnp.where(spot() >= step, pltpu.roll(value, step, 0), blank)

    def join_segments(er, ei, keep_ref, l, desc, conj):
        shut = jnp.min(keep_ref[...].reshape(seg, NSEG, LANES), axis=0)
        lr, li = lam_rows(l, 1, conj)
        ar, ai = lr * wide(shut, ns // LANES), li * wide(shut, ns // LANES)
        for step in (1, 2, 4, 8):
            pr, pi = cmul(ar, ai, before(er, step, desc, 0.0), before(ei, step, desc, 0.0))
            er, ei = er + pr, ei + pi
            ar, ai = cmul(ar, ai, before(ar, step, desc, 1.0), before(ai, step, desc, 0.0))
        last = 0 if desc else NSEG - 1
        out = (er[last : last + 1], ei[last : last + 1], jnp.min(shut, axis=0, keepdims=True))
        shifted = (
            before(er, 1, desc, 0.0),
            before(ei, 1, desc, 0.0),
            before(ar, 1, desc, 1.0),
            before(ai, 1, desc, 0.0),
        )
        return out, shifted

    def send_carry(phase, l, m, u_ref, desc, conj):
        keep_ref = keep_d.at[m] if desc else keep_a.at[m]
        er, ei = scan_local(u_ref, keep_ref, l, desc, conj)
        (tr, ti, shut), shifted = join_segments(er, ei, keep_ref, l, desc, conj)
        if desc:
            first = keep_a[m, 0:1, :]
            tr, ti, shut = tr * wide(first, ns // LANES), ti * wide(first, ns // LANES), shut * first
        index = phase * 4 + 2 * l + m
        buf = gline.at[index]
        buf[rank] = jnp.concatenate(
            [
                to_tile(tr),
                to_tile(ti),
                shut,
                jnp.zeros((SUB - 2 * ns // LANES - 1, LANES), F32),
            ],
            axis=0,
        )
        gather_start(buf, rank, n_line, peer_line, SEM_LINE + index)
        return shifted

    def take_carry(phase, l, m, shifted, desc, conj):
        index = phase * 4 + 2 * l + m
        buf = gline.at[index]
        gather_wait(buf, n_line, SEM_LINE + index)
        lr, li = lam_rows(l, 2, conj)
        tiles = ns // LANES

        def body(step, carry):
            cr, ci = carry
            k = n_line - 1 - step if desc else step
            box = buf[k]
            shut = wide(box[2 * tiles : 2 * tiles + 1], tiles)
            pr, pi = cmul(lr * shut, li * shut, cr, ci)
            pr = pr + to_row(box[:tiles])
            pi = pi + to_row(box[tiles : 2 * tiles])
            use = k > rank if desc else k < rank
            return jnp.where(use, pr, cr), jnp.where(use, pi, ci)

        zero = jnp.zeros((1, ns), F32)
        cr, ci = lax.fori_loop(0, n_line, body, (zero, zero))
        er, ei, ar, ai = shifted
        pr, pi = cmul(ar, ai, cr, ci)
        return er + pr, ei + pi

    def fill_states(l, m, shifted):
        desc = l == 1
        re, im = take_carry(0, l, m, shifted, desc, False)
        keep_ref = keep_d.at[m] if desc else keep_a.at[m]
        u_ref, s_ref = drive.at[2 * l + m], state.at[2 * l + m]
        lr, li = lam_rows(l, 0, False)
        lr = jnp.broadcast_to(lr, (NSEG, ns))
        li = jnp.broadcast_to(li, (NSEG, ns))
        s_ref[pl.ds(half if desc else 0, NSEG), :] = jnp.concatenate([re, im], axis=1)

        def body(jj, carry):
            re, im = carry
            for t in range(unroll):
                j = jj * unroll + t
                if desc:
                    j = seg - 1 - j
                at = pl.multiple_of(j * NSEG, NSEG)
                rows = pl.ds(at, NSEG)
                keep = wide(keep_ref[rows, :], ns // LANES)
                u = u_ref[rows, :]
                kr, ki = keep * re, keep * im
                re = lr * kr - li * ki + u[:, :ns]
                im = lr * ki + li * kr + u[:, ns:]
                to = rows if desc else pl.ds(at + NSEG, NSEG)
                s_ref[to, :] = jnp.concatenate([re, im], axis=1)
            return re, im

        lax.fori_loop(0, seg // unroll, body, (re, im))

    def fill_grads(l, m, shifted):
        desc = l == 0
        re, im = take_carry(1, l, m, shifted, desc, True)
        keep_ref = keep_d.at[m] if desc else keep_a.at[m]
        pkeep_ref = keep_a.at[m] if desc else keep_d.at[m]
        u_ref, s_ref, g_ref = drive.at[2 * l + m], state.at[2 * l + m], gst.at[m]
        lr, li = lam_rows(l, 0, True)
        lr = jnp.broadcast_to(lr, (NSEG, ns))
        li = jnp.broadcast_to(li, (NSEG, ns))
        zero = jnp.zeros((NSEG, ns), F32)

        def body(jj, carry):
            re, im, dr, di, dg = carry
            for t in range(unroll):
                j = jj * unroll + t
                if desc:
                    j = seg - 1 - j
                at = pl.multiple_of(j * NSEG, NSEG)
                rows = pl.ds(at, NSEG)
                keep = wide(keep_ref[rows, :], ns // LANES)
                g = g_ref[rows, :]
                kr, ki = keep * re, keep * im
                re = lr * kr - li * ki + g[:, :ns]
                im = lr * ki + li * kr + g[:, ns:]
                g_ref[rows, :] = jnp.concatenate([re, im], axis=1)
                u = u_ref[rows, :]
                dg = dg + (re * u[:, :ns] + im * u[:, ns:])
                old = s_ref[rows if desc else pl.ds(at + NSEG, NSEG), :]
                pkeep = wide(pkeep_ref[rows, :], ns // LANES)
                pr, pi = pkeep * old[:, :ns], pkeep * old[:, ns:]
                dr = dr + (pr * re + pi * im)
                di = di + (pr * im - pi * re)
            return re, im, dr, di, dg

        _, _, dr, di, dg = lax.fori_loop(0, seg // unroll, body, (re, im, zero, zero, zero))
        box = sm.at[2 * l + m]
        box[3:4, :] = jnp.sum(jnp.concatenate([dr, di], axis=1), axis=0, keepdims=True)
        box[4:5, :] = jnp.sum(jnp.concatenate([dg, dg], axis=1), axis=0, keepdims=True)

    def project(l, m):
        gamma2 = dv[l, 3:4, :]

        def body(at, acc):
            rows = pl.ds(at, chunk)
            low = unit_of(l, m, rows).astype(BF16)
            ulow[l, pl.ds(m * half + at, chunk), :] = low
            drive[2 * l + m, rows, :] = dot_nn(low, wb[l]) * gamma2
            return acc

        chunks(body, 0)
        return send_carry(0, l, m, drive.at[2 * l + m], l == 1, False)

    def mix(l, m, at):
        rows = pl.ds(at, chunk)
        big = pl.ds(m * half + at, chunk)
        low = state[2 * l + m, pl.ds(at + (0 if l == 1 else NSEG), chunk), :].astype(BF16)
        slow[l, big, :] = low
        unit = unit_of(l, m, rows)
        mixed = dot_nn(low, wc[l]) + pv[l, 2:3, :] * unit
        square = mixed * mixed
        t = jnp.tanh((GELU_C * mixed) * (1.0 + GELU_K * square))
        half_up = 0.5 * (1.0 + t)
        act = (mixed * half_up).astype(BF16)
        alow[l, big, :] = act
        slope = half_up + (0.5 * GELU_C) * mixed * (1.0 - t * t) * (1.0 + (3.0 * GELU_K) * square)
        gates = dot_nn(act, wg[l])
        value = gates[:, :width] + pv[l, 3:4, :]
        gate = 0.5 * jnp.tanh(0.5 * (gates[:, width:] + pv[l, 4:5, :])) + 0.5
        branch = value * gate
        return unit, slope, gate, branch, (hid[2 * l + m, rows, :] + branch).astype(BF16)

    def finish_lower(m):
        def body(at, acc):
            rows = pl.ds(at, chunk)
            unit, slope, gate, branch, low = mix(0, m, at)
            sig_s[m, rows, :] = gate.astype(BF16)
            gat_s[m, rows, :] = (branch * (1.0 - gate)).astype(BF16)
            dgelu_s[m, rows, :] = slope.astype(BF16)
            low_s[m, rows, :] = low
            value = low.astype(F32)
            hid[2 + m, rows, :] = value
            return acc + fold_rows(value * wide(live[m, rows, :], width // LANES))

        return chunks(body, zero_sum)

    def to_natural(low_ref, nat_ref):
        def body(at, acc):
            rows = pl.ds(at, chunk)
            nat_ref[rows, :] = dot_nn(perm_t[rows, :], low_ref[...]).astype(BF16)
            return acc

        chunks(body, 0)

    def ship(out, m, tag):
        base = tag * 2 + m
        local = pltpu.make_async_copy(
            nat.at[s, m], out.at[0, m, 0, my_tokens], out_sem.at[base]
        )
        remote = pltpu.make_async_remote_copy(
            src_ref=nat.at[1 - s, m],
            dst_ref=out.at[0, m, 0, my_tokens],
            send_sem=osend_sem.at[base],
            recv_sem=orecv_sem.at[base],
            device_id=partner,
            device_id_type=MESH,
        )
        local.start()
        remote.start()
        return local, remote

    def gate_grads(l, m, at, unit, slope, gate, other, grad, acc):
        rows = pl.ds(at, chunk)
        big = pl.ds(m * half + at, chunk)
        d_gates = jnp.concatenate([grad * gate, grad * other], axis=1).astype(BF16)
        dgate[big, :] = d_gates
        d_mixed = dot_nt(d_gates, wg[l]) * slope
        dmix[m, rows, :] = d_mixed
        d_read = d_mixed.astype(BF16)
        dread[big, :] = d_read
        gst[m, rows, :] = dot_nt(d_read, wc[l])
        return acc[0] + fold_rows(d_gates.astype(F32)), acc[1] + fold_rows(d_mixed * unit)

    gate_zero = (jnp.zeros((SUB, 2 * width), F32), zero_sum)

    def keep_gate_sums(l, m, acc):
        box = sm.at[2 * l + m]
        box[0:1, :] = jnp.sum(acc[1], axis=0, keepdims=True)
        both = jnp.sum(acc[0], axis=0, keepdims=True)
        box[1:2, :] = both[:, :width]
        box[2:3, :] = both[:, width:]

    def turn_upper(m):
        def body(at, acc):
            rows = pl.ds(at, chunk)
            unit, slope, gate, branch, low = mix(1, m, at)
            low_s[m, rows, :] = low
            grad = dout[m, rows, :].astype(F32)
            return gate_grads(1, m, at, unit, slope, gate, branch * (1.0 - gate), grad, acc)

        keep_gate_sums(1, m, chunks(body, gate_zero))
        return send_carry(1, 1, m, gst.at[m], False, True)

    def scale_grads(l, m):
        gamma2 = dv[l, 3:4, :]

        def body(at, acc):
            dproj[pl.ds(m * half + at, chunk), :] = (gst[m, pl.ds(at, chunk), :] * gamma2).astype(BF16)
            return acc

        chunks(body, 0)

    def unproject(l, m):
        def body(at, acc):
            rows = pl.ds(at, chunk)
            low = (gst[m, rows, :] * dv[l, 3:4, :]).astype(BF16)
            dproj[pl.ds(m * half + at, chunk), :] = low
            value = dmix[m, rows, :] * pv[l, 2:3, :] + dot_nt(low, wb[l])
            dunit[m, rows, :] = value
            normed = (hid[2 * l + m, rows, :] - sv[2 * l + m, 0:1, :]) * sv[2 * l + m, 1:2, :]
            return acc[0] + fold_rows(value), acc[1] + fold_rows(value * normed)

        by_bias, by_gain = chunks(body, (zero_sum, zero_sum))
        buf = gst_all.at[4 + 2 * l + m]
        buf[me] = jnp.concatenate(
            [
                to_tile(jnp.sum(by_bias, axis=0, keepdims=True)),
                to_tile(jnp.sum(by_gain, axis=0, keepdims=True)),
            ],
            axis=0,
        )
        gather_start(buf, me, n_all, peer_all, SEM_NORM + 2 * l + m)

    def take_norm(l, m):
        buf = gst_all.at[4 + 2 * l + m]
        gather_wait(buf, n_all, SEM_NORM + 2 * l + m)
        both = jnp.sum(buf[...], axis=0)
        box = sv.at[2 * l + m]
        box[5:6, :] = to_row(both[0:4])
        box[6:7, :] = to_row(both[4:8])

    def input_grads(l, m, rows):
        box = sv.at[2 * l + m]
        share_of = 1.0 / box[4:5, :]
        by_bias = box[2:3, :] * box[5:6, :] * share_of
        by_gain = box[2:3, :] * box[6:7, :] * share_of
        normed = (hid[2 * l + m, rows, :] - box[0:1, :]) * box[1:2, :]
        mask = wide(live[m, rows, :], width // LANES)
        return (
            dout[m, rows, :].astype(F32)
            + dunit[m, rows, :] * box[2:3, :]
            - mask * (by_bias + normed * by_gain)
        ).astype(BF16)

    def turn_lower(m):
        def body(at, acc):
            rows = pl.ds(at, chunk)
            low = input_grads(1, m, rows)
            low_s[m, rows, :] = low
            grad = low.astype(F32)
            dout[m, rows, :] = low
            return gate_grads(
                0,
                m,
                at,
                unit_of(0, m, rows),
                dgelu_s[m, rows, :].astype(F32),
                sig_s[m, rows, :].astype(F32),
                gat_s[m, rows, :].astype(F32),
                grad,
                acc,
            )

        keep_gate_sums(0, m, chunks(body, gate_zero))
        return send_carry(1, 0, m, gst.at[m], True, True)

    def finish_grads(m):
        def body(at, acc):
            rows = pl.ds(at, chunk)
            low_s[m, rows, :] = input_grads(0, m, rows)
            return acc

        chunks(body, 0)

    part = 256

    def weight_grads(l, left, right, row_at):
        blocks = right.shape[1] // GRAD_COLS

        def body(c, acc):
            at = pl.multiple_of(c * part, part)
            for k in range(blocks):
                columns = pl.ds(k * GRAD_COLS, GRAD_COLS)
                value = dot_tn(left[l, :, pl.ds(at, part)], right[:, columns])
                to = pl.multiple_of(row_at + k * width + at, part)
                gbuf[l, pl.ds(to, part), :] = value.astype(BF16)
            return acc

        lax.fori_loop(0, width // part, body, 0)

    per = width // GRAD_COLS
    n_group = 4
    row_axis = (n_rows, r, lambda core, d: (core, q, r ^ d))
    seq_axis = (n_seq, q, lambda core, d: (core, q ^ d, r))
    seq_first_fits = (per * width // 2) % (16 * n_seq * n_rows) == 0

    class Reduce:
        def __init__(self, number, l, base, count, seq_first):
            self.l, self.base = l, base
            self.mine = count // 2
            self.at = base // 2
            axes = (seq_axis, row_axis) if seq_first and seq_first_fits else (row_axis, seq_axis)
            (self.k1, self.i1, self.peer1), (self.k2, self.i2, self.peer2) = axes
            self.n1 = self.mine // self.k1
            self.n2 = max(16, self.n1 // self.k2)
            self.owners = self.n1 // self.n2
            self.at1 = base // 8
            self.at2 = base // 32
            self.sem = number * 5

        def send(self, source, target, sem, where):
            return pltpu.make_async_remote_copy(
                src_ref=source,
                dst_ref=target,
                send_sem=rs_sem.at[self.sem + sem],
                recv_sem=rr_sem.at[self.sem + sem],
                device_id=where,
                device_id_type=MESH,
            )

        def await_rows(self, count, sem, sems=None):
            ref = gbuf.at[0, pl.ds(0, count)]
            pltpu.make_async_copy(ref, ref, (rr_sem if sems is None else sems).at[self.sem + sem]).wait()

        def half_of(self, core):
            return gbuf.at[self.l, pl.ds(pl.multiple_of(self.base + core * self.mine, 16), self.mine)]

        def total(self):
            return pair_buf.at[self.l, pl.ds(self.at, self.mine)]

        def piece(self, ref, index, size):
            return ref.at[pl.ds(pl.multiple_of(index * size, 16), size)]

        def pair(self):
            self.send(self.half_of(1 - s), self.total(), 0, partner).start()

        def first(self):
            self.await_rows(self.mine, 0)
            own, total = self.half_of(s), self.total()
            total[...] = (own[...].astype(F32) + total[...].astype(F32)).astype(BF16)
            into = first_buf.at[self.l, :, pl.ds(self.at1, self.n1)]
            for d in range(1, self.k1):
                self.send(
                    self.piece(total, self.i1 ^ d, self.n1), into.at[d - 1], 1, self.peer1(s, d)
                ).start()

        def second(self):
            self.await_rows((self.k1 - 1) * self.n1, 1)
            total = self.piece(self.total(), self.i1, self.n1)
            value = total[...].astype(F32)
            for d in range(self.k1 - 1):
                value = value + first_buf[self.l, d, pl.ds(self.at1, self.n1), :].astype(F32)
            total[...] = value.astype(BF16)
            into = second_buf.at[self.l, :, pl.ds(self.at2, self.n2)]

            def one(d, acc):
                to = self.i2 ^ d

                def go():
                    self.send(self.piece(total, to, self.n2), into.at[d - 1], 2, self.peer2(s, d)).start()

                self.when(to < self.owners, go)
                return acc

            lax.fori_loop(1, self.k2, one, 0, unroll=self.k2 <= 4)

        def when(self, condition, go):
            if self.owners == self.k2:
                go()
            else:
                pl.when(condition)(go)

        def block(self):
            return gfin.at[self.l, pl.ds(self.at1, self.n1)]

        def back_second(self):
            total = self.piece(self.total(), self.i1, self.n1)
            mine = self.piece(self.block(), self.i2, self.n2)

            def go():
                self.await_rows((self.k2 - 1) * self.n2, 2)
                value = self.piece(total, self.i2, self.n2)[...].astype(F32)
                for d in range(self.k2 - 1):
                    value = value + second_buf[self.l, d, pl.ds(self.at2, self.n2), :].astype(F32)
                mine[...] = value.astype(BF16)

                def one(d, acc):
                    self.send(mine, mine, 3, self.peer2(s, d)).start()
                    return acc

                lax.fori_loop(1, self.k2, one, 0, unroll=self.k2 <= 4)

            self.when(self.i2 < self.owners, go)

        def result(self):
            at = self.base + s * self.mine + self.i1 * self.n1
            return grad_out.at[pl.ds(pl.multiple_of(at, 16), self.n1)]

        def keep_own(self):
            return pltpu.make_async_copy(self.block(), self.result(), gout_sem.at[self.sem // 5])

        def some_owners(self, sem, sems=None):
            self.when(
                self.i2 < self.owners, lambda: self.await_rows((self.owners - 1) * self.n2, sem, sems)
            )
            if self.owners < self.k2:
                self.when(
                    self.i2 >= self.owners, lambda: self.await_rows(self.owners * self.n2, sem, sems)
                )

        def back_first(self):
            self.some_owners(3)
            pl.when(s == self.l)(lambda: self.keep_own().start())
            pl.when(s != self.l)(lambda: self.send(self.block(), self.result(), 4, partner).start())
            for d in range(1, self.k1):
                self.send(self.block(), self.result(), 4, self.peer1(self.l, d)).start()

        def done(self):
            def settle():
                self.keep_own().wait()
                self.await_rows((2 * self.k1 - 1) * self.n1, 4)
                self.await_rows((self.k1 - 1) * self.n1, 4, rs_sem)

            pl.when(s == self.l)(settle)
            pl.when(s != self.l)(lambda: self.await_rows(self.k1 * self.n1, 4, rs_sem))
            self.await_rows(self.mine, 0, rs_sem)
            self.await_rows((self.k1 - 1) * self.n1, 1, rs_sem)
            self.some_owners(2, rs_sem)
            self.when(
                self.i2 < self.owners, lambda: self.await_rows((self.k2 - 1) * self.n2, 3, rs_sem)
            )

    reduce = [[], []]
    for l in range(2):
        for g in range(n_group):
            count = per * width // SPLIT[l]
            for k in range(SPLIT[l]):
                number = len(reduce[0]) + len(reduce[1])
                reduce[l].append(
                    Reduce(number, l, g * per * width + k * count, count, (l, g) in SEQ_FIRST)
                )
    B, C, GA, GB = range(n_group)

    def run(*plan):
        for l, g, step in plan:
            for k in range(SPLIT[l]):
                getattr(reduce[l][g * SPLIT[l] + k], step)()

    def run_part(l, g, k, step):
        getattr(reduce[l][g * SPLIT[l] + k], step)()

    def small_copy(source, target, sem, where):
        return pltpu.make_async_remote_copy(
            src_ref=source,
            dst_ref=target,
            send_sem=ss_sem.at[sem],
            recv_sem=sr_sem.at[sem],
            device_id=where,
            device_id_type=MESH,
        )

    def small_await(ref, sems, sem):
        pltpu.make_async_copy(ref, ref, sems.at[sem]).wait()

    def small_pair():
        for l in range(2):
            both = sm[2 * l]
            for m in range(1, micro):
                both = both + sm[2 * l + m]
            small_own[l] = jnp.concatenate(
                [to_tile(both[i : i + 1]) for i in range(5)] + [jnp.zeros((4, LANES), F32)], axis=0
            )
        small_copy(small_own.at[1 - s], small_other, 0, partner).start()

    def small_rows():
        small_await(small_other, sr_sem, 0)
        first, second = small_own[s], small_other[...]
        small_by_row[r] = first + second
        for d in range(1, n_rows):
            small_copy(small_by_row.at[r], small_by_row.at[r], 1, (s, q, r ^ d)).start()

    def small_seq():
        small_await(small_by_row.at[pl.ds(0, n_rows - 1)], sr_sem, 1)
        total = small_by_row[0]
        for k in range(1, n_rows):
            total = total + small_by_row[k]
        small_by_seq[q] = total

        def one(d, acc):
            small_copy(small_by_seq.at[q], small_by_seq.at[q], 2, (s, q ^ d, r)).start()
            return acc

        lax.fori_loop(1, n_seq, one, 0)

    def small_total():
        small_await(small_by_seq.at[pl.ds(0, n_seq - 1)], sr_sem, 2)
        return jnp.sum(small_by_seq[...], axis=0)

    def small_done():
        small_await(small_other, ss_sem, 0)
        small_await(small_by_row.at[pl.ds(0, n_rows - 1)], ss_sem, 1)
        small_await(small_by_seq.at[pl.ds(0, n_seq - 1)], ss_sem, 2)

    for m in range(micro):
        loads[m].wait()
        stats_of(0, m, enter(m))
    pl.semaphore_wait(barrier, n_all - 1)
    gather_start(meta, me, n_all, peer_all, SEM_META)
    for m in range(micro):
        send_stats(0, m)
    for item in shares[:2]:
        item.start()
    for item in own_w:
        item.wait()
    for item in shares[:2]:
        item.wait()
    for item in shares[2:]:
        item.start()
    for l in range(2):
        decay = jnp.exp(-jnp.exp(pv[l, 5:6, :ns]))
        phase = jnp.exp(pv[l, 5:6, ns:])
        re, im = decay * jnp.cos(phase), decay * jnp.sin(phase)
        dv[l, 0:1, :] = jnp.concatenate([re, im], axis=1)
        dv[l, 1:2, :] = jnp.concatenate(cpow(re, im, seg), axis=1)
        dv[l, 2:3, :] = jnp.concatenate(cpow(re, im, half), axis=1)
        dv[l, 3:4, :] = jnp.exp(pv[l, 6:7, :])
    gather_wait(meta, n_all, SEM_META)

    shifted = {}
    for m in range(micro):
        take_stats(0, m)
        shifted[m] = project(0, m)
    for item in shares[2:]:
        item.wait()
    for m in range(micro):
        fill_states(0, m, shifted[m])
        stats_of(1, m, finish_lower(m))
        send_stats(1, m)
    for m in range(micro):
        to_natural(low_s.at[m], nat.at[0, m])
    for m in range(micro):
        take_stats(1, m)
        shifted[m] = project(1, m)
    for item in cot_loads:
        item.wait()
    for m in range(micro):
        dout[m] = dot_nn(perm[...], nat[1, m]).astype(BF16)
    outgoing = []
    for m in range(micro):
        fill_states(1, m, shifted[m])
        shifted[m] = turn_upper(m)
    weight_grads(1, slow, dread, per * width)
    run((1, C, "pair"))
    fill_grads(1, 0, shifted[0])
    unproject(1, 0)
    run((1, C, "first"))
    weight_grads(1, alow, dgate, 2 * per * width)
    run((1, GA, "pair"), (1, GB, "pair"))
    for m in range(1, micro):
        fill_grads(1, m, shifted[m])
        unproject(1, m)
    run((1, GA, "first"), (1, GB, "first"))
    weight_grads(1, ulow, dproj, 0)
    run((1, B, "pair"))
    for m in range(micro):
        to_natural(low_s.at[m], nat.at[1, m])
        outgoing += ship(act_out, m, 0)
    take_norm(1, 0)
    shifted[0] = turn_lower(0)
    for item in outgoing:
        item.wait()
    outgoing = []
    run((1, B, "first"), (1, C, "second"))
    to_natural(low_s.at[0], nat.at[1, 0])
    for m in range(1, micro):
        take_norm(1, m)
        shifted[m] = turn_lower(m)
        to_natural(low_s.at[m], nat.at[1, m])
    weight_grads(0, slow, dread, per * width)
    run((0, C, "pair"), (1, GA, "second"), (1, C, "back_second"))
    weight_grads(0, alow, dgate, 2 * per * width)
    run((0, GA, "pair"), (0, GB, "pair"), (0, C, "first"), (1, GB, "second"), (1, C, "back_first"))
    fill_grads(0, 0, shifted[0])
    unproject(0, 0)
    for m in range(1, micro):
        fill_grads(0, m, shifted[m])
        unproject(0, m)
    run((0, GA, "first"), (0, GB, "first"))
    weight_grads(0, ulow, dproj, 0)
    run((0, B, "pair"))
    small_pair()
    run((1, B, "second"), (1, GA, "back_second"))
    take_norm(0, 0)
    finish_grads(0)
    to_natural(low_s.at[0], nat.at[0, 0])
    outgoing += ship(ig_out, 0, 1)
    run((0, B, "first"), (1, GB, "back_second"))
    for m in range(1, micro):
        take_norm(0, m)
        finish_grads(m)
        to_natural(low_s.at[m], nat.at[0, m])
        outgoing += ship(ig_out, m, 1)
    small_rows()
    run((1, B, "back_second"))
    order = [(g, k) for g in (C, GA, GB, B) for k in range(SPLIT[0])]
    late = [(1, GA), (1, GB), (1, B)]
    lag = 3
    for i in range(len(order) + 2 * lag):
        if i < len(order):
            run_part(0, *order[i], "second")
        if 0 <= i - lag < len(order):
            run_part(0, *order[i - lag], "back_second")
        if i % 2 == 0 and late:
            run((*late.pop(0), "back_first"))
        if 0 <= i - 2 * lag < len(order):
            run_part(0, *order[i - 2 * lag], "back_first")
        if i == 2:
            small_seq()

    def pick(values):
        return jnp.where(on_upper, values[1], values[0])

    tile_sum = small_total()
    wt = width // LANES
    rows_of = [to_row(tile_sum[i * wt : (i + 1) * wt]) for i in range(5)]
    dr, di, dg = rows_of[3][:, :ns], rows_of[3][:, ns:], rows_of[4]
    lam = pick([dv[l, 0:1, :] for l in range(2)])
    lr, li = lam[:, :ns], lam[:, ns:]
    by_nu = -jnp.exp(nu_ref[...]) * (lr * dr + li * di)
    by_theta = jnp.exp(theta_ref[...]) * (lr * di - li * dr)
    mean, var = rmean_ref[...], rvar_ref[...]
    for m in range(micro):
        mean = (1.0 - MOMENTUM) * mean + MOMENTUM * pick([sv[2 * l + m, 0:1, :] for l in range(2)])
        var = (1.0 - MOMENTUM) * var + MOMENTUM * pick([sv[2 * l + m, 3:4, :] for l in range(2)])
    by_bias = pick([sum(sv[2 * l + m, 5:6, :] for m in range(micro)) for l in range(2)])
    by_gain = pick([sum(sv[2 * l + m, 6:7, :] for m in range(micro)) for l in range(2)])
    blank = jnp.zeros((1, width), F32)
    small_out[...] = jnp.concatenate(
        [by_gain, by_bias]
        + rows_of[:3]
        + [jnp.concatenate([by_nu, by_theta], axis=1), dg, mean, var]
        + [blank] * 7,
        axis=0,
    )

    gather_sent(meta, n_all, SEM_META)
    for i in range(4):
        gather_sent(gst_all.at[i], n_all, SEM_STAT + i)
        gather_sent(gst_all.at[4 + i], n_all, SEM_NORM + i)
    for i in range(8):
        gather_sent(gline.at[i], n_line, SEM_LINE + i)
    small_done()
    for group in reduce[1] + reduce[0]:
        group.done()
    for item in outgoing:
        item.wait()


def finish_kernel(
    act_in,
    ig_in,
    grad_in,
    small_in,
    act_out,
    ig_out,
    ggain_out,
    gbias_out,
    gb_out,
    gnu_out,
    gtheta_out,
    ggamma_out,
    gc_out,
    gskip_out,
    gglu_out,
    gglub_out,
    nmean_out,
    nvar_out,
    low,
    flat,
    small,
    flow,
    flow_sem,
    load_sem,
    store_sem,
    small_sem,
):
    small_load = pltpu.make_async_copy(small_in, small, small_sem.at[0])
    small_load.start()
    flows_in, flows_out = [], []
    for i, (source, target) in enumerate(((act_in, act_out), (ig_in, ig_out))):
        for m in range(source.shape[1]):
            k = 2 * i + m
            flows_in.append(
                pltpu.make_async_copy(source.at[0, m, 0], flow.at[k], flow_sem.at[0, k])
            )
            flows_out.append(
                pltpu.make_async_copy(flow.at[k], target.at[0, m, 0], flow_sem.at[1, k])
            )
    width, columns = gb_out.shape[1], low.shape[1]
    blocks = low.shape[0] // width
    loads, stores = [], []
    targets = [(gb_out, 0), (gb_out, 1), (gc_out, 0), (gc_out, 1)] + [(gglu_out, k) for k in range(4)]
    for k in range(blocks):
        rows = pl.ds(k * width, width)
        loads.append(pltpu.make_async_copy(grad_in.at[rows], low.at[rows], load_sem.at[k]))
        out, column = targets[k]
        stores.append(
            pltpu.make_async_copy(
                flat.at[k], out.at[0, :, pl.ds(column * columns, columns)], store_sem.at[k]
            )
        )
    for item in flows_in + loads:
        item.start()
    small_load.wait()
    ns = gnu_out.shape[1]
    ggain_out[...] = small[0:1, :]
    gbias_out[...] = small[1:2, :]
    gskip_out[...] = small[2:3, :]
    gglub_out[:, :width] = small[3:4, :]
    gglub_out[:, width:] = small[4:5, :]
    gnu_out[...] = small[5:6, :ns]
    gtheta_out[...] = small[5:6, ns:]
    ggamma_out[...] = small[6:7, :ns]
    nmean_out[...] = small[7:8, :]
    nvar_out[...] = small[8:9, :]
    for arrived, leave in zip(flows_in, flows_out):
        arrived.wait()
        leave.start()
    for k in range(blocks):
        loads[k].wait()
        flat[k] = low[k * width : (k + 1) * width, :].astype(F32)
        stores[k].start()
    for item in stores + flows_out:
        item.wait()


def on_device(n_seq, n_rows, *args):
    inputs, starts = args[0], args[2]
    micro, _, tokens, width = inputs.shape
    ns = args[9].shape[1]
    half = tokens // 2
    n_line = 2 * n_seq
    n_all = n_line * n_rows
    any_space = pl.BlockSpec(memory_space=pl.ANY)
    hbm = pl.BlockSpec(memory_space=pltpu.HBM)
    vmem = pl.BlockSpec(memory_space=pltpu.VMEM)
    in_specs = [vmem] * 16
    for i in (0, 1, 8, 12, 14):
        in_specs[i] = any_space
    flow = jax.ShapeDtypeStruct((1, micro, 1, tokens, width), BF16)
    row = lambda size: jax.ShapeDtypeStruct((1, size), F32)
    mat = lambda size: jax.ShapeDtypeStruct((1, width, size), F32)
    vf = lambda *shape: pltpu.VMEM(shape, F32)
    vb = lambda *shape: pltpu.VMEM(shape, BF16)
    dma = lambda *count: pltpu.SemaphoreType.DMA(count)
    grad_rows = 4 * width * (width // GRAD_COLS)
    own_rows = grad_rows // 2
    scratch = [
        vb(2, micro, half, width),
        vb(2, width, 2 * ns),
        vb(2, 2 * ns, width),
        vb(2, width, 2 * width),
        vf(2, SUB, width),
        vf(2, SUB, width),
        vb(half, half),
        vb(half, half),
        vf(micro, half, LANES),
        vf(micro, half, LANES),
        vf(micro, half, LANES),
        vf(2 * micro, half, width),
        vb(2, micro * half, width),
        vf(2 * micro, half, width),
        vf(2 * micro, half + NSEG, width),
        vb(2, micro * half, width),
        vb(2, micro * half, width),
        vb(micro * half, 2 * width),
        vb(micro * half, width),
        vf(micro, half, width),
        vb(micro * half, width),
        vf(micro, half, width),
        vf(micro, half, width),
        vb(micro, half, width),
        vb(micro, half, width),
        vb(micro, half, width),
        vb(micro, half, width),
        vb(micro, half, width),
        vf(2 * micro, SUB, width),
        vf(2 * micro, SUB, width),
        vf(n_all, micro, LANES),
        vf(8, n_all, SUB, LANES),
        vf(8, n_line, SUB, LANES),
        vf(2, 24, LANES),
        vf(24, LANES),
        vf(n_rows, 24, LANES),
        vf(n_seq, 24, LANES),
        vb(2, grad_rows, GRAD_COLS),
        vb(2, own_rows, GRAD_COLS),
        vb(2, n_rows - 1, own_rows // n_rows, GRAD_COLS),
        vb(2, n_seq - 1, own_rows // 16, GRAD_COLS),
        vb(2, own_rows // n_rows, GRAD_COLS),
        dma(7),
        dma(4),
        dma(4),
        dma(17),
        dma(17),
        dma(4),
        dma(4),
        dma(4),
        dma(60),
        dma(60),
        dma(12),
        dma(3),
        dma(3),
    ]
    act, ig, grads, small = pl.pallas_call(
        functools.partial(step_kernel, n_seq, n_rows),
        out_shape=(
            flow,
            flow,
            jax.ShapeDtypeStruct((grad_rows, GRAD_COLS), BF16),
            jax.ShapeDtypeStruct((16, width), F32),
        ),
        in_specs=in_specs,
        out_specs=[any_space, any_space, any_space, vmem],
        scratch_shapes=scratch,
        compiler_params=pltpu.CompilerParams(
            collective_id=0, has_side_effects=True, vmem_limit_bytes=63 * 2**20
        ),
        name="lru_blocks",
    )(*args)
    return pl.pallas_call(
        finish_kernel,
        out_shape=(
            flow,
            flow,
            row(width),
            row(width),
            mat(2 * ns),
            row(ns),
            row(ns),
            row(ns),
            mat(width),
            row(width),
            mat(2 * width),
            row(2 * width),
            row(width),
            row(width),
        ),
        in_specs=[hbm, hbm, hbm, hbm],
        out_specs=[any_space if i in (0, 1, 4, 8, 10) else vmem for i in range(14)],
        scratch_shapes=[
            vb(grad_rows, GRAD_COLS),
            vf(grad_rows // width, width, GRAD_COLS),
            vf(16, width),
            vb(2 * micro, tokens, width),
            dma(2, 4),
            dma(grad_rows // width),
            dma(grad_rows // width),
            dma(1),
        ],
        compiler_params=pltpu.CompilerParams(vmem_limit_bytes=62 * 2**20),
        name="write_results",
    )(act, ig, grads, small)


def solution(mesh):
    placed = (
        P(None, "rows", "seq", None),
        P(None, "rows", "seq", None),
        P(None, "rows", "seq"),
        P(None, "rows", "seq"),
        P("section", None),
        P("section", None),
        P("section", None),
        P("section", None),
        P("section", None, None),
        P("section", None),
        P("section", None),
        P("section", None),
        P("section", None, None),
        P("section", None),
        P("section", None, None),
        P("section", None),
    )
    return jax.shard_map(
        functools.partial(on_device, mesh.shape["seq"], mesh.shape["rows"]),
        mesh=mesh,
        in_specs=placed,
        out_specs=(
            P("section", None, "rows", "seq", None),
            P("section", None, "rows", "seq", None),
            P("section", None),
            P("section", None),
            P("section", None, None),
            P("section", None),
            P("section", None),
            P("section", None),
            P("section", None, None),
            P("section", None),
            P("section", None, None),
            P("section", None),
            P("section", None),
            P("section", None),
        ),
        check_vma=False,
    )
```
